32 devices in a mesh: dp: 4 (over y, x), fsdp: 8 (over z, core).
Axes of the slice: x: 2, y: 2, z: 4, core: 2. Of those that a mesh axis runs over, the one named last changes fastest.
Arguments:
- tokens: bfloat16 [32, 1024, 768], P(('dp', 'fsdp')), may hold values from -6 to 6
- row_lengths: int32 [32], P(('dp', 'fsdp')), may hold values from 256 to 1024, as said below
- live_mask: int32 [2, 32, 1024], P(None, ('dp', 'fsdp')), may hold values 0 or 1
- pass_index: int32 [32], P(('dp', 'fsdp')), may hold values from 1 to 4
- w_qkv: bfloat16 [768, 2304], P(None, ('dp', 'fsdp')), may hold values from -0.21875 to 0.21875
- w_out: bfloat16 [768, 768], P(None, ('dp', 'fsdp')), may hold values from -2.5 to 2.5
- w_up: bfloat16 [768, 3072], P(None, ('dp', 'fsdp')), may hold values from -0.21875 to 0.21875
- w_down: bfloat16 [3072, 768], P(('dp', 'fsdp')), may hold values from -0.109375 to 0.109375
- norm_gains: bfloat16 [2, 768], P(None, ('dp', 'fsdp')), may hold values from 0.099609375 to 1.8984375
- norm_shifts: bfloat16 [2, 768], P(None, ('dp', 'fsdp')), may hold values from -4 to 4
- pass_table: bfloat16 [5, 768], P(None, ('dp', 'fsdp')), may hold values from -6 to 6
- cotangent: float32 [32, 1024, 768], P(('dp', 'fsdp')), may hold values from -6 to 6
Outputs:
- activations: bfloat16 [32, 1024, 768], P(('dp', 'fsdp'))
- input_grad: float32 [32, 1024, 768], P(('dp', 'fsdp'))
- grad_qkv: float32 [768, 2304], P(None, ('dp', 'fsdp'))
- grad_out: float32 [768, 768], P(None, ('dp', 'fsdp'))
- grad_up: float32 [768, 3072], P(None, ('dp', 'fsdp'))
- grad_down: float32 [3072, 768], P(('dp', 'fsdp'))
- grad_gains: float32 [2, 768], P(None, ('dp', 'fsdp'))
- grad_shifts: float32 [768], P(('dp', 'fsdp'))
- grad_second_shift: float32 [768], P(('dp', 'fsdp'))
- grad_table: float32 [5, 768], P(None, ('dp', 'fsdp'))
The draws below stay inside these ranges and needn't reach their ends.
Inputs may be any that keep to these rules, and one draw needn't show every extreme that they name: `row_lengths`: some row uses all 1024 positions and some row only 256.
All inputs are finite; a program needn't handle non-finite values. No bound on the sum of `live_mask` on one device may be relied on, other than what follows from the above.
Results may differ from the reference program's by a relative error of at most 0.015.
Values may be sent and summed in bfloat16 or wider, within the bound.
No kernel may reach another device: no remote copies, remote signals or barrier semaphores. Data moves between devices by JAX's collectives and lax.ppermute only.
A program may use at most 320 MiB of HBM per device.

```python
import math
import jax
import jax.numpy as jnp
from jax import lax

D = 768
HEADS = 12
HEAD = 64
FF = 3072
PASSES = 5
SEQ = 1024
ROWS = 32


def draw_row_lengths(key, part):
    key = jax.random.fold_in(key, 11)
    length_key, order_key = jax.random.split(key, 2)
    lengths = jax.random.randint(length_key, (ROWS,), SEQ // 4, SEQ + 1)
    ranking = jax.random.permutation(order_key, ROWS)
    lengths = jnp.where(ranking == 0, SEQ, lengths)
    lengths = jnp.where(ranking == 1, SEQ // 4, lengths)
    return lengths.astype(jnp.int32)


def set_ends(entries, stream_key, low, high):
    extent = entries.shape
    place = [jax.random.randint(jax.random.fold_in(stream_key, axis), (), 0, extent[axis]) for axis in range(len(extent))]
    entries = entries.at[tuple(place)].set(low)
    longest = extent.index(max(extent))
    place[longest] = (place[longest] + 1) % extent[longest]
    return entries.at[tuple(place)].set(high)


def block_levels(stream_key, extent, cuts, least, top_value):
    def one(dim, blocks):
        steps = jax.random.uniform(jax.random.fold_in(jax.random.fold_in(stream_key, 6), dim), (blocks,), jnp.float32, least / len(cuts), top_value / len(cuts))
        return jnp.repeat(jnp.exp(steps), extent[dim] // blocks).reshape((-1,) + (1,) * (len(extent) - dim - 1))

    factor_of = one(*cuts[0])
    for cut in cuts[1:]:
        factor_of = factor_of * one(*cut)
    return factor_of


def scatter_about(rng, dims, width, reach, cuts=(), kind=jnp.bfloat16):
    entries = jax.random.normal(rng, dims, jnp.float32) * width
    if len(cuts) > 0:
        entries = block_levels(rng, dims, cuts, -0.22, 0.18) * entries
    return jnp.clip(entries, min=-reach, max=reach).astype(kind)


def setup_inputs(seed: int = 0) -> dict:
    streams_of = jax.random.split(jax.random.key(seed), 13)
    tokens = scatter_about(streams_of[0], (ROWS, SEQ, D), 1.0, 6.0, ((0, 32),))
    row_lengths = draw_row_lengths(jax.random.fold_in(streams_of[12], 71), 0)
    live_mask = set_ends((jax.random.randint(streams_of[2], (2, ROWS, SEQ), 0, 8) < 7).astype(jnp.int32), jax.random.fold_in(streams_of[2], 1), 0, 1)
    pass_index = set_ends(jax.random.randint(streams_of[3], (ROWS,), 1, PASSES), jax.random.fold_in(streams_of[3], 1), 1, PASSES - 1).astype(jnp.int32)
    w_qkv = scatter_about(streams_of[4], (D, 3 * D), D ** -0.5, 0.21875, ((1, 32),))
    w_out = scatter_about(streams_of[5], (D, D), (max(D // 128, 1)) ** -0.5, 2.5, ((1, 32),))
    w_up = scatter_about(streams_of[6], (D, FF), D ** -0.5, 0.21875, ((1, 32),))
    w_down = scatter_about(streams_of[7], (FF, D), FF ** -0.5, 0.109375, ((0, 32),))
    norm_gains = jnp.clip(1.0 + 0.18 * jax.random.normal(streams_of[8], (2, D), jnp.float32), 0.099609375, 1.8984375).astype(jnp.bfloat16)
    norm_shifts = scatter_about(streams_of[9], (2, D), 0.3, 4.0, ((1, 32),))
    pass_table = scatter_about(streams_of[10], (PASSES, D), 0.5, 6.0, ((1, 32),))
    cotangent = scatter_about(streams_of[11], (ROWS, SEQ, D), 1.0, 6.0, ((0, 32),), jnp.float32)
    return dict(tokens=tokens, row_lengths=row_lengths, live_mask=live_mask, pass_index=pass_index, w_qkv=w_qkv, w_out=w_out, w_up=w_up, w_down=w_down, norm_gains=norm_gains, norm_shifts=norm_shifts, pass_table=pass_table, cotangent=cotangent)


@jax.custom_vjp
def low(v):
    return lax.optimization_barrier(v.astype(jnp.bfloat16)).astype(jnp.float32)

@jax.custom_vjp
def low_back(v):
    return v

def low_keep(v):
    return (low(v), None)

def low_pass(kept, grad):
    return (grad,)

def back_keep(v):
    return (v, None)

def back_low(kept, grad):
    return (low(grad),)
low.defvjp(low_keep, low_pass)
low_back.defvjp(back_keep, back_low)
norm_epsilon = 1e-05
masked_score = -1000000000.0

def product(left_side, right_side):
    return jnp.dot(left_side, right_side, precision=lax.Precision.HIGHEST, preferred_element_type=jnp.float32)

def norm_apply(values, gain, shift):
    center = lax.optimization_barrier(jnp.mean(values, axis=-1, keepdims=True))
    centered = values - center
    spread = lax.optimization_barrier(jnp.mean(centered * centered, axis=-1, keepdims=True))
    return centered * lax.rsqrt(spread + norm_epsilon) * gain + shift

def attend(query_heads, key_heads, value_heads, live_flags):
    block_rows = min(512, SEQ)
    positions = jnp.arange(SEQ, dtype=jnp.int32)

    def one_block(block_index):
        first_row = (block_index * block_rows).astype(jnp.int32)
        query_rows = lax.dynamic_slice_in_dim(query_heads, first_row, block_rows, 0)
        scores = jnp.einsum('qhe,khe->hqk', query_rows, key_heads, precision=lax.Precision.HIGHEST) * 0.125
        scores = low_back(scores)
        query_pos = first_row + jnp.arange(block_rows, dtype=jnp.int32)
        visible = (positions[None, :] <= query_pos[:, None]) & ((live_flags[None, :] > 0.5) | (positions[None, :] == query_pos[:, None]))
        scores = jnp.where(visible[None], scores, masked_score)
        row_top = lax.optimization_barrier(jnp.max(scores, axis=-1, keepdims=True))
        weights = jnp.exp(scores - row_top)
        soft_low = low(weights / lax.optimization_barrier(jnp.sum(weights, axis=-1, keepdims=True)))
        return jnp.einsum('hqk,khe->qhe', soft_low, value_heads, precision=lax.Precision.HIGHEST)
    block_outputs = lax.map(jax.checkpoint(one_block), jnp.arange(SEQ // block_rows, dtype=jnp.int32))
    return block_outputs.reshape(SEQ, HEADS * HEAD)

def block_layer(inputs, live_flags, params):
    w_qkv, w_out, w_up, w_down, gains, shifts = params
    group_size = inputs.shape[0]
    normed = low(norm_apply(inputs, gains[0], shifts[0]))
    mixed = low_back(low(product(normed, w_qkv)))
    split_heads = mixed.reshape(group_size, SEQ, 3, HEADS, HEAD)
    attended = jax.vmap(attend)(split_heads[:, :, 0], split_heads[:, :, 1], split_heads[:, :, 2], live_flags)
    attended = low_back(low(attended))
    branch = low_back(product(attended, w_out))
    hidden = inputs + live_flags[..., None] * branch
    second = low(norm_apply(hidden, gains[1], shifts[1]))
    lifted = low_back(product(second, w_up))
    activated = low(jax.nn.gelu(lifted, approximate=True))
    return hidden + live_flags[..., None] * low_back(product(activated, w_down))

def reference(tokens, row_lengths, live_mask, pass_index, w_qkv, w_out, w_up, w_down, norm_gains, norm_shifts, pass_table, cotangent):
    group_size = math.gcd(ROWS, max(1, 4096 // SEQ))
    groups = ROWS // group_size
    positions = jnp.arange(SEQ, dtype=jnp.int32)
    inside = positions[None, :] < row_lengths[:, None]
    live_flags = jnp.where(inside[None] & (live_mask > 0), 1.0, 0.0).astype(jnp.float32)
    params = tuple((weight.astype(jnp.float32) for weight in (w_qkv, w_out, w_up, w_down, norm_gains, norm_shifts)))
    pass_rows = pass_table.astype(jnp.float32)
    pass_onehot = jnp.where(jnp.arange(PASSES, dtype=jnp.int32)[None, :] == pass_index[:, None], 1.0, 0.0).astype(jnp.float32)

    def forward(layer_in, flags, onehot, param_in, table_in):
        middle = block_layer(layer_in, flags[:, 0], param_in)
        embedding = product(onehot, table_in)
        return block_layer(middle + embedding[:, None, :], flags[:, 1], param_in)

    def one_group(totals, pieces):
        layer_in, flags, onehot, grad_given = pieces
        outputs, pullback = jax.vjp(lambda first_arg, param_in, table_in: forward(first_arg, flags, onehot, param_in, table_in), layer_in, params, pass_rows)
        layer_grad, param_grads, table_grad = pullback(grad_given)
        totals = jax.tree.map(lambda left_side, right_side: left_side + right_side, totals, (param_grads, table_grad))
        return (totals, (outputs.astype(jnp.bfloat16), layer_grad))
    empty_sums = jax.tree.map(jnp.zeros_like, (params, pass_rows))
    pieces = (tokens.astype(jnp.float32).reshape(groups, group_size, SEQ, D), live_flags.reshape(2, groups, group_size, SEQ).transpose(1, 2, 0, 3), pass_onehot.reshape(groups, group_size, PASSES), cotangent.reshape(groups, group_size, SEQ, D))
    totals, (outputs, layer_grad) = lax.scan(one_group, empty_sums, pieces)
    param_grads, table_grad = totals
    return (outputs.reshape(ROWS, SEQ, D), layer_grad.reshape(ROWS, SEQ, D), param_grads[0], param_grads[1], param_grads[2], param_grads[3], param_grads[4], param_grads[5][0], param_grads[5][1], table_grad)
```

```python
import functools

import jax
import jax.numpy as jnp
from jax import lax
from jax.experimental import pallas as pl
from jax.experimental.pallas import tpu as pltpu
from jax.sharding import PartitionSpec as P

HEAD = 64
LANES = 128
AXES = ("dp", "fsdp")
bf16 = jnp.bfloat16
f32 = jnp.float32

norm_epsilon = 1e-05
masked_score = -1000000000.0
curve_one = 0.7978845608028654
curve_three = 0.7978845608028654 * 0.044715

VMEM_LIMIT = 60 * 1024 * 1024


def dot_nn(left, right):
    return lax.dot_general(left, right, (((1,), (0,)), ((), ())), preferred_element_type=f32)


def dot_nt(left, right):
    return lax.dot_general(left, right, (((1,), (1,)), ((), ())), preferred_element_type=f32)


def dot_tn(left, right):
    return lax.dot_general(left, right, (((0,), (0,)), ((), ())), preferred_element_type=f32)


def normalize(values):
    center = jnp.mean(values, axis=-1, keepdims=True)
    centered = values - center
    spread = jnp.mean(centered * centered, axis=-1, keepdims=True)
    scale = lax.rsqrt(spread + norm_epsilon)
    return centered * scale, scale


def norm_back(grad, gain, xhat, scale):
    gained = grad * gain
    first = jnp.mean(gained, axis=-1, keepdims=True)
    second = jnp.mean(gained * xhat, axis=-1, keepdims=True)
    return scale * (gained - first - xhat * second)


def gelu_pair(lifted):
    square = lifted * lifted
    cubic = curve_three * square
    half = 0.5 + 0.5 * jnp.tanh(lifted * (curve_one + cubic))
    value = lifted * half
    slope = half + value * ((1.0 - half) * (2.0 * curve_one + 6.0 * cubic))
    return value, slope


def call(kernel, grid, in_specs, out_specs, out_shape, flops, args, scratch=()):
    moved = sum(a.size * a.dtype.itemsize for a in args)
    moved += sum(o.size * o.dtype.itemsize for o in out_shape)
    return pl.pallas_call(
        kernel,
        grid=grid,
        in_specs=in_specs,
        out_specs=out_specs,
        out_shape=out_shape,
        scratch_shapes=list(scratch),
        compiler_params=pltpu.CompilerParams(
            dimension_semantics=("arbitrary",) * len(grid), vmem_limit_bytes=VMEM_LIMIT
        ),
        cost_estimate=pl.CostEstimate(flops=flops, bytes_accessed=moved, transcendentals=0),
    )(*args)


def rows_spec(block_rows, width):
    return pl.BlockSpec((block_rows, width), lambda i: (i, 0))


def whole_spec(array):
    zeros = (0,) * len(array.shape)
    return pl.BlockSpec(array.shape, lambda i: zeros, pipeline_mode=pl.Buffered(1))


def sds(shape, dtype):
    return jax.ShapeDtypeStruct(shape, dtype)


def head_part(x, gain, shift, w_qkv, mixed_ref, normed_ref):
    xhat, _ = normalize(x)
    normed = (xhat * gain + shift).astype(bf16)
    normed_ref[...] = normed
    mixed_ref[...] = dot_nt(normed, w_qkv[...]).astype(bf16)


def first_kernel(x_ref, norms_ref, wq_ref, mixed_ref, normed_ref):
    head_part(
        x_ref[...].astype(f32), norms_ref[0:1, :], norms_ref[2:3, :], wq_ref, mixed_ref, normed_ref
    )


def ff_chunks(ff):
    step = 768 if ff % 768 == 0 else ff
    return [pl.ds(at, step) for at in range(0, ff, step)]


def middle_kernel(
    att_ref, x_ref, live_ref, norms_ref, emb_ref, wo_ref, wu_ref, wd_ref, wq_ref,
    hidden_ref, second_ref, act_ref, slope_ref, later_ref, mixed_ref, normed_ref,
):
    live = live_ref[...]
    hidden = x_ref[...].astype(f32) + live * dot_nt(att_ref[...], wo_ref[...])
    hidden_ref[...] = hidden
    xhat, _ = normalize(hidden)
    second = (xhat * norms_ref[1:2, :] + norms_ref[3:4, :]).astype(bf16)
    second_ref[...] = second
    total = jnp.zeros_like(hidden)
    for part in ff_chunks(wu_ref.shape[0]):
        value, slope = gelu_pair(dot_nt(second, wu_ref[part, :]))
        value = value.astype(bf16)
        act_ref[:, part] = value
        slope_ref[:, part] = slope.astype(bf16)
        total = total + dot_nn(value, wd_ref[part, :])
    later = hidden + live * total + emb_ref[...]
    later_ref[...] = later
    head_part(later, norms_ref[0:1, :], norms_ref[2:3, :], wq_ref, mixed_ref, normed_ref)


def mlp_back_tail(
    grad, live, hidden, second_grad, norms_ref, wo_ref, branch_ref, hgrad_ref, agrad_ref
):
    xhat, scale = normalize(hidden)
    hgrad = grad + norm_back(second_grad, norms_ref[1:2, :], xhat, scale)
    hgrad_ref[...] = hgrad
    branch = (live * hgrad).astype(bf16)
    branch_ref[...] = branch
    agrad_ref[...] = dot_nn(branch, wo_ref[...]).astype(bf16)
    gain_sum = jnp.sum(second_grad * xhat, axis=0, keepdims=True)
    shift_sum = jnp.sum(second_grad, axis=0, keepdims=True)
    return gain_sum, shift_sum


def add_sums(sums_ref, sums):
    @pl.when(pl.program_id(0) == 0)
    def _():
        sums_ref[...] = jnp.zeros_like(sums_ref)

    for place, value in enumerate(sums):
        sums_ref[place : place + 1, :] += value


def turn_kernel(
    att_ref, x_ref, live_ref, norms_ref, grad_ref, wo_ref, wu_ref, wd_ref,
    out_ref, second_ref, act_ref, drop_ref, lift_ref, branch_ref, hgrad_ref, agrad_ref, sums_ref,
):
    live = live_ref[...]
    hidden = x_ref[...] + live * dot_nt(att_ref[...], wo_ref[...])
    xhat, _ = normalize(hidden)
    second = (xhat * norms_ref[1:2, :] + norms_ref[3:4, :]).astype(bf16)
    second_ref[...] = second
    grad = grad_ref[...]
    drop = (live * grad).astype(bf16)
    drop_ref[...] = drop
    total = jnp.zeros_like(hidden)
    second_grad = jnp.zeros_like(hidden)
    for part in ff_chunks(wu_ref.shape[0]):
        value, slope = gelu_pair(dot_nt(second, wu_ref[part, :]))
        value = value.astype(bf16)
        act_ref[:, part] = value
        total = total + dot_nn(value, wd_ref[part, :])
        lift = (dot_nt(drop, wd_ref[part, :]) * slope).astype(bf16)
        lift_ref[:, part] = lift
        second_grad = second_grad + dot_nn(lift, wu_ref[part, :])
    out_ref[...] = (hidden + live * total).astype(bf16)
    sums = mlp_back_tail(
        grad, live, hidden, second_grad, norms_ref, wo_ref, branch_ref, hgrad_ref, agrad_ref
    )
    add_sums(sums_ref, sums)


def head_back(mixed_grad_ref, wq_ref, x, hgrad, norms_ref):
    width = x.shape[1]
    normed_grad = dot_nn(mixed_grad_ref[0], wq_ref[0:width, :])
    normed_grad += dot_nn(mixed_grad_ref[1], wq_ref[width : 2 * width, :])
    normed_grad += dot_nn(mixed_grad_ref[2], wq_ref[2 * width : 3 * width, :])
    xhat, scale = normalize(x)
    grad = hgrad + norm_back(normed_grad, norms_ref[0:1, :], xhat, scale)
    gain_sum = jnp.sum(normed_grad * xhat, axis=0, keepdims=True)
    shift_sum = jnp.sum(normed_grad, axis=0, keepdims=True)
    return grad, gain_sum, shift_sum


def back_kernel(
    mgrad_ref, later_ref, hgrad1_ref, norms_ref, live_ref, hidden_ref, slope_ref,
    wq_ref, wo_ref, wu_ref, wd_ref,
    drop_ref, lift_ref, branch_ref, hgrad_ref, agrad_ref, sums_ref,
):
    grad, gain0, shift0 = head_back(mgrad_ref, wq_ref, later_ref[...], hgrad1_ref[...], norms_ref)
    table_sum = jnp.sum(grad, axis=0, keepdims=True)
    live = live_ref[...]
    drop = (live * grad).astype(bf16)
    drop_ref[...] = drop
    second_grad = jnp.zeros_like(grad)
    for part in ff_chunks(wu_ref.shape[0]):
        lift = (dot_nt(drop, wd_ref[part, :]) * slope_ref[:, part].astype(f32)).astype(bf16)
        lift_ref[:, part] = lift
        second_grad = second_grad + dot_nn(lift, wu_ref[part, :])
    sums = mlp_back_tail(
        grad, live, hidden_ref[...], second_grad, norms_ref, wo_ref, branch_ref, hgrad_ref, agrad_ref
    )
    add_sums(sums_ref, sums + (gain0, shift0, table_sum))


def last_kernel(mgrad_ref, x_ref, hgrad_ref, norms_ref, wq_ref, out_ref, sums_ref):
    grad, gain0, shift0 = head_back(
        mgrad_ref, wq_ref, x_ref[...].astype(f32), hgrad_ref[...], norms_ref
    )
    out_ref[...] = grad
    add_sums(sums_ref, (gain0, shift0))


def ff_grad_kernel(
    act0, act1, lift0, lift1, drop0, drop1, second0, second1, up_ref, down_ref
):
    down_ref[...] = (dot_tn(act0[...], drop0[...]) + dot_tn(act1[...], drop1[...])).astype(bf16)
    up_ref[...] = (dot_tn(lift0[...], second0[...]) + dot_tn(lift1[...], second1[...])).astype(bf16)


def pair_grad_kernel(left0, left1, right0, right1, out_ref):
    out_ref[...] = (dot_tn(left0[...], right0[...]) + dot_tn(left1[...], right1[...])).astype(bf16)


def ff_grads(kept0, kept1):
    tokens, ff = kept0["act"].shape
    width = kept0["drop"].shape[1]
    step = 384
    cols = pl.BlockSpec((tokens, step), lambda i: (0, i))
    full = [kept0["drop"], kept1["drop"], kept0["second"], kept1["second"]]
    args = [kept0["act"], kept1["act"], kept0["lift"], kept1["lift"]] + full
    return call(
        ff_grad_kernel,
        (ff // step,),
        [cols] * 4 + [whole_spec(a) for a in full],
        [rows_spec(step, width)] * 2,
        [sds((ff, width), bf16)] * 2,
        8 * tokens * ff * width,
        args,
    )


def pair_grads(left0, left1, right0, right1, step):
    tokens, high = left0.shape
    width = right0.shape[1]
    cols = pl.BlockSpec((tokens, step), lambda i: (0, i))
    return call(
        pair_grad_kernel,
        (high // step,),
        [cols] * 2 + [whole_spec(right0)] * 2,
        [rows_spec(step, width)],
        [sds((high, width), bf16)],
        4 * tokens * high * width,
        [left0, left1, right0, right1],
    )[0]


def qkv_grad_kernel(left0, left1, right0, right1, out_ref):
    out_ref[...] = (dot_tn(left0[0], right0[...]) + dot_tn(left1[0], right1[...])).astype(bf16)


def qkv_grads(left0, left1, right0, right1, step=384):
    parts, tokens, high = left0.shape
    width = right0.shape[1]
    per = high // step
    cols = pl.BlockSpec((1, tokens, step), lambda i: (i // per, 0, i % per))
    return call(
        qkv_grad_kernel,
        (parts * per,),
        [cols] * 2 + [whole_spec(right0)] * 2,
        [rows_spec(step, width)],
        [sds((parts * high, width), bf16)],
        4 * tokens * parts * high * width,
        [left0, left1, right0, right1],
    )[0]


def lane_index(shape):
    return lax.broadcasted_iota(jnp.int32, shape, len(shape) - 1)


def split_three(values):
    high = values.astype(bf16)
    rest = values - high.astype(f32)
    middle = rest.astype(bf16)
    low = (rest - middle.astype(f32)).astype(bf16)
    return high, middle, low


def own_lanes(lane, head):
    return (lane < HEAD) if head == 0 else (lane >= HEAD)


def attend_kernel(
    block, q_ref, k_ref, v_ref, live_col_ref, live_row_ref, out_ref, logs_ref, mask_ref
):
    seq = q_ref.shape[0]
    count = seq // block

    @pl.when(pl.program_id(0) == 0)
    def _():
        query = lax.broadcasted_iota(jnp.int32, (block, block), 0)
        key = lax.broadcasted_iota(jnp.int32, (block, block), 1)
        for i in range(count):
            alive = live_row_ref[:, i * block : (i + 1) * block] > 0.5
            visible = (key <= query) & (alive | (key == query))
            mask_ref[i] = jnp.where(visible, 0.0, masked_score)

    lane = lane_index((seq, LANES))
    q = q_ref[...] * 0.125
    k = k_ref[...]
    v = v_ref[...]
    bias = ((live_col_ref[...] - 1.0) * 1e9).astype(bf16)
    zero = jnp.zeros((seq, LANES), bf16)
    one = jnp.ones((seq, LANES), bf16)
    parts = []
    for head in range(2):
        mine = own_lanes(lane, head)
        spare = (1 - head) * HEAD
        parts.append(
            (
                jnp.where(mine, q, zero),
                jnp.where(mine, q, jnp.where(lane == spare, one, zero)),
                jnp.where(mine, k, jnp.where(lane == spare, bias, zero)),
                jnp.where(mine, v, one),
            )
        )
    low = lane_index((block, LANES)) < HEAD
    for i in range(count):
        at = slice(i * block, (i + 1) * block)
        before = slice(0, i * block)
        outs, logs = [], []
        for head in range(2):
            q_plain, q_bias, k_bias, v_ones = parts[head]
            diag = dot_nt(q_plain[at], k[at]) + mask_ref[i]
            top = jnp.max(diag, axis=-1, keepdims=True)
            if i > 0:
                off = dot_nt(q_bias[at], k_bias[before])
                top = jnp.maximum(top, jnp.max(off, axis=-1, keepdims=True))
            total = dot_nn(jnp.exp(diag - top).astype(bf16), v_ones[at])
            if i > 0:
                total += dot_nn(jnp.exp(off - top).astype(bf16), v_ones[before])
            spare = (1 - head) * HEAD
            weight = total[:, spare : spare + 1]
            outs.append(total * (1.0 / weight))
            logs.append(top + jnp.log(weight))
        out_ref[at, :] = jnp.where(low, outs[0], outs[1]).astype(bf16)
        logs_ref[at, :] = jnp.where(low, logs[0], logs[1])


def attend(mixed, live_col, live_row, block=256):
    seq, triple = mixed.shape
    width = triple // 3
    pairs = width // LANES
    block = min(block, seq)

    def cols(offset):
        return pl.BlockSpec((seq, LANES), lambda h: (0, offset + h))

    return call(
        functools.partial(attend_kernel, block),
        (pairs,),
        [cols(0), cols(pairs), cols(2 * pairs), whole_spec(live_col), whole_spec(live_row)],
        [cols(0), cols(0)],
        [sds((seq, width), bf16), sds((seq, width), f32)],
        4 * seq * seq * width,
        [mixed, mixed, mixed, live_col, live_row],
        scratch=[pltpu.VMEM((seq // block, block, block), f32)],
    )


def attend_back_kernel(
    block, q_ref, k_ref, v_ref, grad_ref, att_ref, logs_ref, live_col_ref, out_ref,
    mask_ref, dk_ref, dv_ref,
):
    seq = q_ref.shape[0]
    count = seq // block

    @pl.when(pl.program_id(0) == 0)
    def _():
        key = lax.broadcasted_iota(jnp.int32, (block, block), 0)
        query = lax.broadcasted_iota(jnp.int32, (block, block), 1)
        for i in range(count):
            alive = live_col_ref[i * block : (i + 1) * block, :] > 0.5
            visible = (key <= query) & (alive | (key == query))
            mask_ref[i] = jnp.where(visible, 0.0, masked_score)

    lane = lane_index((seq, LANES))
    q = q_ref[...] * 0.125
    k = k_ref[...]
    v = v_ref[...]
    grad = grad_ref[...]
    logs = logs_ref[...]
    dots = grad.astype(f32) * att_ref[...].astype(f32)
    bias = ((live_col_ref[...] - 1.0) * 1e9).astype(bf16)
    zero = jnp.zeros((seq, LANES), bf16)
    one = jnp.ones((seq, LANES), bf16)
    parts = []
    for head in range(2):
        mine = own_lanes(lane, head)
        spare = (1 - head) * HEAD
        log_terms = split_three(-logs[:, head * HEAD : head * HEAD + 1])
        dot_terms = split_three(-jnp.sum(jnp.where(mine, dots, 0.0), axis=-1, keepdims=True))
        q_more, k_more, k_diag, g_more, v_more = (
            jnp.where(lane == spare, one, zero),
            jnp.where(lane == spare, bias, zero),
            zero,
            zero,
            zero,
        )
        for place in range(3):
            here = lane == spare + 1 + place
            q_more = jnp.where(here, log_terms[place], q_more)
            k_more = jnp.where(here, one, k_more)
            k_diag = jnp.where(here, one, k_diag)
            g_more = jnp.where(here, dot_terms[place], g_more)
            v_more = jnp.where(here, one, v_more)
        parts.append(
            dict(
                q=jnp.where(mine, q, q_more),
                k=jnp.where(mine, k, k_more),
                kd=jnp.where(mine, k, k_diag),
                g=jnp.where(mine, grad, g_more),
                v=jnp.where(mine, v, v_more),
                q0=jnp.where(mine, q, zero),
                k0=jnp.where(mine, k, zero),
                g0=jnp.where(mine, grad, zero),
            )
        )
    for i in range(count):
        at = slice(i * block, (i + 1) * block)
        dq = jnp.zeros((block, LANES), f32)
        for j in range(i + 1):
            to = slice(j * block, (j + 1) * block)
            dk = jnp.zeros((block, LANES), f32)
            dv = jnp.zeros((block, LANES), f32)
            for head in range(2):
                part = parts[head]
                if j == i:
                    score = dot_nt(part["kd"][to], part["q"][at]) + mask_ref[i]
                else:
                    score = dot_nt(part["k"][to], part["q"][at])
                soft = jnp.exp(score)
                change = (soft * dot_nt(part["v"][to], part["g"][at])).astype(bf16)
                dv += dot_nn(soft.astype(bf16), part["g0"][at])
                dk += dot_nn(change, part["q0"][at])
                dq += dot_tn(change, part["k0"][to])
            if j == i:
                dk_ref[to, :] = dk
                dv_ref[to, :] = dv
            else:
                dk_ref[to, :] += dk
                dv_ref[to, :] += dv
        out_ref[0, at, :] = (dq * 0.125).astype(bf16)
    out_ref[1] = dk_ref[...].astype(bf16)
    out_ref[2] = dv_ref[...].astype(bf16)


def attend_back(mixed, att_grad, att, logs, live_col, block=256):
    seq, triple = mixed.shape
    width = triple // 3
    pairs = width // LANES
    block = min(block, seq)

    def cols(offset):
        return pl.BlockSpec((seq, LANES), lambda h: (0, offset + h))

    return call(
        functools.partial(attend_back_kernel, block),
        (pairs,),
        [cols(0), cols(pairs), cols(2 * pairs), cols(0), cols(0), cols(0), whole_spec(live_col)],
        [pl.BlockSpec((3, seq, LANES), lambda h: (0, 0, h))],
        [sds((3, seq, width), bf16)],
        10 * seq * seq * width,
        [mixed, mixed, mixed, att_grad, att, logs, live_col],
        scratch=[
            pltpu.VMEM((seq // block, block, block), f32),
            pltpu.VMEM((seq, LANES), f32),
            pltpu.VMEM((seq, LANES), f32),
        ],
    )[0]


def gather_all(w_qkv, w_out, w_up, w_down, norm_gains, norm_shifts, pass_table):
    width = w_out.shape[0]
    small = jnp.concatenate([norm_gains, norm_shifts, pass_table], axis=0)
    count, share = small.shape
    rows = [w_qkv.shape[1], w_out.shape[1], w_up.shape[1], w_down.shape[0]]
    flat = small.reshape(1, -1)
    slots = -(-flat.shape[1] // width)
    flat = jnp.pad(flat, ((0, 0), (0, slots * width - flat.shape[1]))).reshape(slots, width)
    packed = jnp.concatenate([w_qkv.T, w_out.T, w_up.T, w_down, flat], axis=0)
    fill = -packed.shape[0] % 16
    packed = jnp.pad(packed, ((0, fill), (0, 0)))
    whole = lax.all_gather(packed, AXES, axis=0, tiled=False)
    devices = whole.shape[0]
    found, at = [], 0
    for size in rows:
        found.append(whole[:, at : at + size].reshape(devices * size, width))
        at += size
    small = whole[:, at : at + slots].reshape(devices, slots * width)[:, : count * share]
    small = small.reshape(devices, count, share).transpose(1, 0, 2).reshape(count, devices * share)
    return tuple(found), small.astype(f32)


def body(
    tokens, row_lengths, live_mask, pass_index,
    w_qkv, w_out, w_up, w_down, norm_gains, norm_shifts, pass_table, cotangent,
):
    _, seq, width = tokens.shape
    ff = w_up.shape[1] * lax.axis_size(AXES)
    block = min(256, seq)
    grid = (seq // block,)
    passes = pass_table.shape[0]

    (wq, wo, wu, wd), small = gather_all(
        w_qkv, w_out, w_up, w_down, norm_gains, norm_shifts, pass_table
    )
    norms = jnp.concatenate([small[:4], jnp.zeros((4, width), f32)], axis=0)
    chosen = jnp.where(jnp.arange(passes, dtype=jnp.int32) == pass_index[0], 1.0, 0.0).astype(f32)
    emb = jnp.sum(chosen[:, None] * small[4:], axis=0, keepdims=True)

    positions = jnp.arange(seq, dtype=jnp.int32)
    inside = positions < row_lengths[0]
    live = jnp.where(inside[None, :] & (live_mask[:, 0] > 0), 1.0, 0.0).astype(f32)
    live_cols = [live[0][:, None], live[1][:, None]]
    live_rows = [live[0][None, :], live[1][None, :]]

    x = tokens[0]
    given = cotangent[0]
    rows_w = rows_spec(block, width)
    rows_f = rows_spec(block, ff)
    rows_q = rows_spec(block, 3 * width)
    rows_1 = rows_spec(block, 1)
    rows_3 = pl.BlockSpec((3, block, width), lambda i: (0, i, 0))
    sums_spec = pl.BlockSpec((8, width), lambda i: (0, 0))
    wide = sds((seq, width), f32)
    thin = sds((seq, width), bf16)
    tall = sds((seq, ff), bf16)
    triple = sds((seq, 3 * width), bf16)
    sums_shape = sds((8, width), f32)
    unit = 2 * seq * width

    mixed0, normed0 = call(
        first_kernel, grid,
        [rows_w, whole_spec(norms), whole_spec(wq)],
        [rows_q, rows_w], [triple, thin], unit * 3 * width, [x, norms, wq],
    )
    att0, logs0 = attend(mixed0, live_cols[0], live_rows[0])
    hidden0, second0, act0, slope0, later, mixed1, normed1 = call(
        middle_kernel, grid,
        [rows_w, rows_w, rows_1] + [whole_spec(a) for a in (norms, emb, wo, wu, wd, wq)],
        [rows_w, rows_w, rows_f, rows_f, rows_w, rows_q, rows_w],
        [wide, thin, tall, tall, wide, triple, thin],
        unit * (4 * width + 2 * ff),
        [att0, x, live_cols[0], norms, emb, wo, wu, wd, wq],
    )
    att1, logs1 = attend(mixed1, live_cols[1], live_rows[1])
    result, second1, act1, drop1, lift1, branch1, hgrad1, agrad1, sums1 = call(
        turn_kernel, grid,
        [rows_w, rows_w, rows_1, whole_spec(norms), rows_w] + [whole_spec(a) for a in (wo, wu, wd)],
        [rows_w, rows_w, rows_f, rows_w, rows_f, rows_w, rows_w, rows_w, sums_spec],
        [thin, thin, tall, thin, tall, thin, wide, thin, sums_shape],
        unit * (2 * width + 4 * ff),
        [att1, later, live_cols[1], norms, given, wo, wu, wd],
    )
    mgrad1 = attend_back(mixed1, agrad1, att1, logs1, live_cols[1])
    drop0, lift0, branch0, hgrad0, agrad0, sums0 = call(
        back_kernel, grid,
        [rows_3, rows_w, rows_w, whole_spec(norms), rows_1, rows_w, rows_f]
        + [whole_spec(a) for a in (wq, wo, wu, wd)],
        [rows_w, rows_f, rows_w, rows_w, rows_w, sums_spec],
        [thin, tall, thin, wide, thin, sums_shape],
        unit * (4 * width + 2 * ff),
        [mgrad1, later, hgrad1, norms, live_cols[0], hidden0, slope0, wq, wo, wu, wd],
    )
    up_grad, down_grad = ff_grads(
        dict(act=act0, lift=lift0, drop=drop0, second=second0),
        dict(act=act1, lift=lift1, drop=drop1, second=second1),
    )
    out_grad = pair_grads(branch0, branch1, att0, att1, 384)
    mgrad0 = attend_back(mixed0, agrad0, att0, logs0, live_cols[0])
    qkv_grad = qkv_grads(mgrad0, mgrad1, normed0, normed1)
    input_grad, sums_last = call(
        last_kernel, grid,
        [rows_3, rows_w, rows_w, whole_spec(norms), whole_spec(wq)],
        [rows_w, sums_spec], [wide, sums_shape], unit * 3 * width,
        [mgrad0, x, hgrad0, norms, wq],
    )

    gain0 = sums0[2] + sums_last[0]
    shift0 = sums0[3] + sums_last[1]
    gain1 = sums0[0] + sums1[0]
    shift1 = sums0[1] + sums1[1]
    table = chosen[:, None] * sums0[4][None, :]
    small_grad = jnp.concatenate([jnp.stack([gain0, gain1, shift0, shift1]), table], axis=0)

    def scatter(grads):
        return lax.psum_scatter(grads, AXES, scatter_dimension=0, tiled=True).astype(f32)

    up = scatter(up_grad).T
    down = scatter(down_grad)
    out = scatter(out_grad).T
    qkv = scatter(qkv_grad).T
    small = lax.psum_scatter(small_grad, AXES, scatter_dimension=1, tiled=True)
    return (
        result[None], input_grad[None], qkv, out, up, down,
        small[:2], small[2], small[3], small[4:],
    )


def solution(mesh):
    placed = (
        P(AXES, None, None),
        P(AXES),
        P(None, AXES, None),
        P(AXES),
        P(None, AXES),
        P(None, AXES),
        P(None, AXES),
        P(AXES, None),
        P(None, AXES),
        P(None, AXES),
        P(None, AXES),
        P(AXES, None, None),
    )
    return jax.shard_map(
        body,
        mesh=mesh,
        in_specs=placed,
        out_specs=(
            P(AXES, None, None),
            P(AXES, None, None),
            P(None, AXES),
            P(None, AXES),
            P(None, AXES),
            P(AXES, None),
            P(None, AXES),
            P(AXES),
            P(AXES),
            P(None, AXES),
        ),
        check_vma=False,
    )
```

```python
import functools

import jax
import jax.numpy as jnp
from jax import lax
from jax.experimental import pallas as pl
from jax.experimental.pallas import tpu as pltpu
from jax.sharding import PartitionSpec as P

HEAD = 64
LANES = 128
AXES = ("dp", "fsdp")
bf16 = jnp.bfloat16
f32 = jnp.float32

norm_epsilon = 1e-05
masked_score = -1000000000.0
curve_one = 0.7978845608028654
curve_three = 0.7978845608028654 * 0.044715

VMEM_LIMIT = 60 * 1024 * 1024


def dot_nn(left, right):
    return lax.dot_general(left, right, (((1,), (0,)), ((), ())), preferred_element_type=f32)


def dot_nt(left, right):
    return lax.dot_general(left, right, (((1,), (1,)), ((), ())), preferred_element_type=f32)


def dot_tn(left, right):
    return lax.dot_general(left, right, (((0,), (0,)), ((), ())), preferred_element_type=f32)


def normalize(values):
    center = jnp.mean(values, axis=-1, keepdims=True)
    centered = values - center
    spread = jnp.mean(centered * centered, axis=-1, keepdims=True)
    scale = lax.rsqrt(spread + norm_epsilon)
    return centered * scale, scale


def norm_back(grad, gain, xhat, scale):
    gained = grad * gain
    first = jnp.mean(gained, axis=-1, keepdims=True)
    second = jnp.mean(gained * xhat, axis=-1, keepdims=True)
    return scale * (gained - first - xhat * second)


def gelu_pair(lifted):
    square = lifted * lifted
    cubic = curve_three * square
    half = 0.5 + 0.5 * jnp.tanh(lifted * (curve_one + cubic))
    value = lifted * half
    slope = half + value * ((1.0 - half) * (2.0 * curve_one + 6.0 * cubic))
    return value, slope


def call(kernel, grid, in_specs, out_specs, out_shape, flops, args, scratch=(), hold=()):
    moved = sum(a.size * a.dtype.itemsize for a in args)
    moved += sum(o.size * o.dtype.itemsize for o in out_shape)
    given, held = len(args), len(hold)

    def run(*refs):
        kernel(*refs[:given], *refs[given + held :])

    return pl.pallas_call(
        run,
        grid=grid,
        in_specs=list(in_specs) + [pl.BlockSpec(memory_space=pl.ANY)] * held,
        out_specs=out_specs,
        out_shape=out_shape,
        scratch_shapes=list(scratch),
        compiler_params=pltpu.CompilerParams(
            dimension_semantics=("arbitrary",) * len(grid), vmem_limit_bytes=VMEM_LIMIT
        ),
        cost_estimate=pl.CostEstimate(
            flops=flops // 4096, bytes_accessed=moved // 4096, transcendentals=0
        ),
    )(*args, *hold)


def rows_spec(block_rows, width):
    return pl.BlockSpec((block_rows, width), lambda i: (i, 0))


def whole_spec(array):
    zeros = (0,) * len(array.shape)
    return pl.BlockSpec(array.shape, lambda i: zeros, pipeline_mode=pl.Buffered(1))


def sds(shape, dtype):
    return jax.ShapeDtypeStruct(shape, dtype)


def head_part(x, gain, shift, w_qkv, mixed_ref, normed_ref):
    xhat, _ = normalize(x)
    normed = (xhat * gain + shift).astype(bf16)
    normed_ref[...] = normed
    mixed_ref[...] = dot_nt(normed, w_qkv[...]).astype(bf16)


def first_kernel(x_ref, norms_ref, wq_ref, mixed_ref, normed_ref):
    head_part(
        x_ref[...].astype(f32), norms_ref[0:1, :], norms_ref[2:3, :], wq_ref, mixed_ref, normed_ref
    )


def ff_chunks(order, place_ref, packed_ref, share):
    found = []
    if share >= 768:
        for at in range(0, share, 768):
            up, down = pl.ds(at, 768), pl.ds(share + at, 768)
            found.append((lambda r=up: packed_ref[0, r, :], lambda r=down: packed_ref[0, r, :], pl.ds(at, 768)))
        return found
    per = 768 // share
    for first in range(0, len(order), per):

        def rows(at, first=first):
            return jnp.concatenate(
                [
                    packed_ref[place_ref[3] ^ mask, pl.ds(at, share), :]
                    for mask in order[first : first + per]
                ],
                axis=0,
            )

        found.append(
            (functools.partial(rows, 0), functools.partial(rows, share), pl.ds(first * share, 768))
        )
    return found


def middle_kernel(order, share, place_ref, packed_ref, *refs):
    chunks = ff_chunks(order, place_ref, packed_ref, share)
    atts, refs = refs[:-13], refs[-13:]
    (
        x_ref, live_ref, norms_ref, emb_ref, wo_ref, wq_ref,
        hidden_ref, second_ref, act_ref, slope_ref, later_ref, mixed_ref, normed_ref,
    ) = refs
    live = live_ref[...]
    branch, at = 0.0, 0
    for ref in atts:
        branch = branch + dot_nt(ref[...], wo_ref[:, at : at + ref.shape[1]])
        at += ref.shape[1]
    hidden = x_ref[...].astype(f32) + live * branch
    hidden_ref[...] = hidden
    xhat, _ = normalize(hidden)
    second = (xhat * norms_ref[1:2, :] + norms_ref[3:4, :]).astype(bf16)
    second_ref[...] = second
    total = jnp.zeros_like(hidden)
    for up, down, to in chunks:
        value, slope = gelu_pair(dot_nt(second, up()))
        value = value.astype(bf16)
        act_ref[:, to] = value
        slope_ref[:, to] = slope.astype(bf16)
        total = total + dot_nn(value, down())
    later = hidden + live * total + emb_ref[...]
    later_ref[...] = later
    head_part(later, norms_ref[0:1, :], norms_ref[2:3, :], wq_ref, mixed_ref, normed_ref)


def mlp_back_tail(
    grad, live, hidden, second_grad, norms_ref, wo_ref, branch_ref, hgrad_ref, agrad_ref
):
    xhat, scale = normalize(hidden)
    hgrad = grad + norm_back(second_grad, norms_ref[1:2, :], xhat, scale)
    hgrad_ref[...] = hgrad
    branch = (live * hgrad).astype(bf16)
    branch_ref[...] = branch
    agrad_ref[...] = dot_nn(branch, wo_ref[...]).astype(bf16)
    gain_sum = jnp.sum(second_grad * xhat, axis=0, keepdims=True)
    shift_sum = jnp.sum(second_grad, axis=0, keepdims=True)
    return gain_sum, shift_sum


def add_sums(sums_ref, sums):
    @pl.when(pl.program_id(0) == 0)
    def _():
        sums_ref[...] = jnp.zeros_like(sums_ref)

    for place, value in enumerate(sums):
        sums_ref[place : place + 1, :] += value


def turn_kernel(order, share, place_ref, packed_ref, *refs):
    chunks = ff_chunks(order, place_ref, packed_ref, share)
    (
        att_ref, x_ref, live_ref, norms_ref, grad_ref, wo_ref,
        out_ref, second_ref, act_ref, drop_ref, lift_ref, branch_ref, hgrad_ref, agrad_ref, sums_ref,
    ) = refs
    live = live_ref[...]
    hidden = x_ref[...] + live * dot_nt(att_ref[...], wo_ref[...])
    xhat, _ = normalize(hidden)
    second = (xhat * norms_ref[1:2, :] + norms_ref[3:4, :]).astype(bf16)
    second_ref[...] = second
    grad = grad_ref[...]
    drop = (live * grad).astype(bf16)
    drop_ref[...] = drop
    total = jnp.zeros_like(hidden)
    second_grad = jnp.zeros_like(hidden)
    for up, down, to in chunks:
        up, down = up(), down()
        value, slope = gelu_pair(dot_nt(second, up))
        value = value.astype(bf16)
        act_ref[:, to] = value
        total = total + dot_nn(value, down)
        lift = (dot_nt(drop, down) * slope).astype(bf16)
        lift_ref[:, to] = lift
        second_grad = second_grad + dot_nn(lift, up)
    out_ref[...] = (hidden + live * total).astype(bf16)
    sums = mlp_back_tail(
        grad, live, hidden, second_grad, norms_ref, wo_ref, branch_ref, hgrad_ref, agrad_ref
    )
    add_sums(sums_ref, sums)


def head_back(mixed_grad_refs, wq_ref, x, hgrad, norms_ref):
    width = x.shape[1]
    normed_grad = jnp.zeros_like(x)
    for part in range(3):
        at = part * width
        for ref in mixed_grad_refs:
            normed_grad += dot_nn(ref[part], wq_ref[at : at + ref.shape[2], :])
            at += ref.shape[2]
    xhat, scale = normalize(x)
    grad = hgrad + norm_back(normed_grad, norms_ref[0:1, :], xhat, scale)
    gain_sum = jnp.sum(normed_grad * xhat, axis=0, keepdims=True)
    shift_sum = jnp.sum(normed_grad, axis=0, keepdims=True)
    return grad, gain_sum, shift_sum


def back_kernel(order, share, place_ref, packed_ref, *refs):
    chunks = ff_chunks(order, place_ref, packed_ref, share)
    (
        mgrad_ref, later_ref, hgrad1_ref, norms_ref, live_ref, hidden_ref, slope_ref, wq_ref, wo_ref,
        drop_ref, lift_ref, branch_ref, hgrad_ref, agrad_ref, sums_ref,
    ) = refs
    grad, gain0, shift0 = head_back([mgrad_ref], wq_ref, later_ref[...], hgrad1_ref[...], norms_ref)
    table_sum = jnp.sum(grad, axis=0, keepdims=True)
    live = live_ref[...]
    drop = (live * grad).astype(bf16)
    drop_ref[...] = drop
    second_grad = jnp.zeros_like(grad)
    for up, down, to in chunks:
        lift = (dot_nt(drop, down()) * slope_ref[:, to].astype(f32)).astype(bf16)
        lift_ref[:, to] = lift
        second_grad = second_grad + dot_nn(lift, up())
    sums = mlp_back_tail(
        grad, live, hidden_ref[...], second_grad, norms_ref, wo_ref, branch_ref, hgrad_ref, agrad_ref
    )
    add_sums(sums_ref, sums + (gain0, shift0, table_sum))


def last_kernel(groups, *refs):
    mgrad_refs, (x_ref, hgrad_ref, norms_ref, wq_ref, out_ref, sums_ref) = (
        refs[:groups],
        refs[groups:],
    )
    grad, gain0, shift0 = head_back(
        mgrad_refs, wq_ref, x_ref[...].astype(f32), hgrad_ref[...], norms_ref
    )
    out_ref[...] = grad
    add_sums(sums_ref, (gain0, shift0))


def pair_grad_kernel(left0, left1, right0, right1, out_ref):
    out_ref[...] = (dot_tn(left0[...], right0[...]) + dot_tn(left1[...], right1[...])).astype(bf16)


def pair_grads(left0, left1, right0, right1, start, size, step=384, hold=()):
    tokens = left0.shape[0]
    width = right0.shape[1]
    first = start // step
    cols = pl.BlockSpec((tokens, step), lambda i: (0, first + i))
    return call(
        pair_grad_kernel,
        (size // step,),
        [cols] * 2 + [whole_spec(right0)] * 2,
        [rows_spec(step, width)],
        [sds((size, width), bf16)],
        4 * tokens * size * width,
        [left0, left1, right0, right1],
        hold=hold,
    )[0]


def place_blocks(cube, halves, place_ref, total_ref, own_ref, other_ref):
    rows, width = own_ref.shape[1:]
    pairs = own_ref.shape[0]
    share = width // halves
    cut = [(order, slice(order * share, (order + 1) * share)) for order in range(halves)]
    for chip in range(pairs):
        if cube.inner == 0:
            for order, lanes in cut:
                own_ref[0, :, lanes] = total_ref[:, lanes].astype(bf16)
            continue
        even = total_ref[pl.ds(2 * chip * rows, rows), :].astype(bf16)
        odd = total_ref[pl.ds((2 * chip + 1) * rows, rows), :].astype(bf16)
        first = place_ref[2] == 0
        own = jnp.where(first, even, odd)
        other = jnp.where(first, odd, even)
        for order, lanes in cut:
            at = cube.place(2 * chip, order) ^ place_ref[order]
            own_ref[at, :, lanes] = own[:, lanes]
            other_ref[at, :, lanes] = other[:, lanes]


def out_grad_kernel(cube, place_ref, left0, left1, *refs):
    rights0, (right1, own_ref, other_ref, total_ref) = refs[:-4], refs[-4:]
    at = 0
    for right0 in rights0:
        to = slice(at, at + right0.shape[1])
        total_ref[:, to] = dot_tn(left0[...], right0[...]) + dot_tn(left1[...], right1[:, to])
        at += right0.shape[1]
    place_blocks(cube, 1, place_ref, total_ref, own_ref, other_ref)


def block_shapes(cube, high, width):
    shape = (cube.pairs, high // cube.count, width)
    return [sds(shape, bf16)] * 2, [pl.BlockSpec(shape, lambda i: (0, 0, 0))] * 2


def out_grads(cube, place, left0, left1, rights0, right1, hold=()):
    tokens, high = left0.shape
    width = right1.shape[1]
    shapes, specs = block_shapes(cube, high, width)
    args = [left0, left1, *rights0, right1]
    return call(
        functools.partial(out_grad_kernel, cube),
        (1,),
        [pl.BlockSpec(memory_space=pltpu.SMEM)] + [whole_spec(a) for a in args],
        specs,
        shapes,
        4 * tokens * high * width,
        [place, *args],
        scratch=[pltpu.VMEM((high, width), f32)],
        hold=hold,
    )


def qkv_grad_kernel(cube, groups, place_ref, *refs):
    lefts0, (left1, right0, right1, own_ref, other_ref, total_ref) = refs[:groups], refs[groups:]
    part = pl.program_id(0)
    high = left1.shape[2]
    at = 0
    for left0 in lefts0:
        to = pl.ds(at, left0.shape[2])
        total = dot_tn(left0[0], right0[...]) + dot_tn(left1[0, :, to], right1[...])
        total_ref[pl.ds(pl.multiple_of(part * high + at, 8), left0.shape[2]), :] = total
        at += left0.shape[2]

    @pl.when(part == pl.num_programs(0) - 1)
    def _():
        place_blocks(cube, 2, place_ref, total_ref, own_ref, other_ref)


def qkv_grads(cube, place, lefts0, left1, right0, right1, hold=()):
    parts, tokens, high = left1.shape
    width = right0.shape[1]
    specs = [
        pl.BlockSpec((1, tokens, a.shape[2]), lambda i: (i, 0, 0)) for a in (*lefts0, left1)
    ]
    shapes, out_specs = block_shapes(cube, parts * high, width)
    return call(
        functools.partial(qkv_grad_kernel, cube, len(lefts0)),
        (parts,),
        [pl.BlockSpec(memory_space=pltpu.SMEM)] + specs + [whole_spec(right0)] * 2,
        out_specs,
        shapes,
        4 * tokens * parts * high * width,
        [place, *lefts0, left1, right0, right1],
        scratch=[pltpu.VMEM((parts * high, width), f32)],
        hold=hold,
    )


def lane_index(shape):
    return lax.broadcasted_iota(jnp.int32, shape, len(shape) - 1)


def split_three(values):
    high = values.astype(bf16)
    rest = values - high.astype(f32)
    middle = rest.astype(bf16)
    low = (rest - middle.astype(f32)).astype(bf16)
    return high, middle, low


def own_lanes(lane, head):
    return (lane < HEAD) if head == 0 else (lane >= HEAD)


def attend_kernel(
    block, q_ref, k_ref, v_ref, live_col_ref, live_row_ref, out_ref, logs_ref, mask_ref
):
    seq = q_ref.shape[0]
    count = seq // block

    @pl.when(pl.program_id(0) == 0)
    def _():
        query = lax.broadcasted_iota(jnp.int32, (block, block), 0)
        key = lax.broadcasted_iota(jnp.int32, (block, block), 1)
        for i in range(count):
            alive = live_row_ref[:, i * block : (i + 1) * block] > 0.5
            visible = (key <= query) & (alive | (key == query))
            mask_ref[i] = jnp.where(visible, 0.0, masked_score)

    lane = lane_index((seq, LANES))
    q = q_ref[...] * 0.125
    k = k_ref[...]
    v = v_ref[...]
    bias = ((live_col_ref[...] - 1.0) * 1e9).astype(bf16)
    zero = jnp.zeros((seq, LANES), bf16)
    one = jnp.ones((seq, LANES), bf16)
    parts = []
    for head in range(2):
        mine = own_lanes(lane, head)
        spare = (1 - head) * HEAD
        parts.append(
            (
                jnp.where(mine, q, zero),
                jnp.where(mine, q, jnp.where(lane == spare, one, zero)),
                jnp.where(mine, k, jnp.where(lane == spare, bias, zero)),
                jnp.where(mine, v, one),
            )
        )
    low = lane_index((block, LANES)) < HEAD
    for i in range(count):
        at = slice(i * block, (i + 1) * block)
        before = slice(0, i * block)
        outs, logs = [], []
        for head in range(2):
            q_plain, q_bias, k_bias, v_ones = parts[head]
            diag = dot_nt(q_plain[at], k[at]) + mask_ref[i]
            top = jnp.max(diag, axis=-1, keepdims=True)
            if i > 0:
                off = dot_nt(q_bias[at], k_bias[before])
                top = jnp.maximum(top, jnp.max(off, axis=-1, keepdims=True))
            total = dot_nn(jnp.exp(diag - top).astype(bf16), v_ones[at])
            if i > 0:
                total += dot_nn(jnp.exp(off - top).astype(bf16), v_ones[before])
            spare = (1 - head) * HEAD
            weight = total[:, spare : spare + 1]
            outs.append(total * (1.0 / weight))
            logs.append(top + jnp.log(weight))
        out_ref[at, :] = jnp.where(low, outs[0], outs[1]).astype(bf16)
        logs_ref[at, :] = jnp.where(low, logs[0], logs[1])


def attend(mixed, live_col, live_row, first=0, count=None, hold=(), block=256):
    seq, triple = mixed.shape
    pairs = triple // 3 // LANES
    count = pairs if count is None else count
    width = count * LANES
    block = min(block, seq)

    def cols(offset):
        return pl.BlockSpec((seq, LANES), lambda h: (0, offset + h))

    return call(
        functools.partial(attend_kernel, block),
        (count,),
        [cols(first), cols(first + pairs), cols(first + 2 * pairs), whole_spec(live_col), whole_spec(live_row)],
        [cols(0), cols(0)],
        [sds((seq, width), bf16), sds((seq, width), f32)],
        4 * seq * seq * width,
        [mixed, mixed, mixed, live_col, live_row],
        scratch=[pltpu.VMEM((seq // block, block, block), f32)],
        hold=hold,
    )


def attend_back_kernel(
    block, q_ref, k_ref, v_ref, grad_ref, att_ref, logs_ref, live_col_ref, out_ref,
    mask_ref, dk_ref, dv_ref,
):
    seq = q_ref.shape[0]
    count = seq // block

    @pl.when(pl.program_id(0) == 0)
    def _():
        key = lax.broadcasted_iota(jnp.int32, (block, block), 0)
        query = lax.broadcasted_iota(jnp.int32, (block, block), 1)
        for i in range(count):
            alive = live_col_ref[i * block : (i + 1) * block, :] > 0.5
            visible = (key <= query) & (alive | (key == query))
            mask_ref[i] = jnp.where(visible, 0.0, masked_score)

    lane = lane_index((seq, LANES))
    q = q_ref[...] * 0.125
    k = k_ref[...]
    v = v_ref[...]
    grad = grad_ref[...]
    logs = logs_ref[...]
    dots = grad.astype(f32) * att_ref[...].astype(f32)
    bias = ((live_col_ref[...] - 1.0) * 1e9).astype(bf16)
    zero = jnp.zeros((seq, LANES), bf16)
    one = jnp.ones((seq, LANES), bf16)
    parts = []
    for head in range(2):
        mine = own_lanes(lane, head)
        spare = (1 - head) * HEAD
        log_terms = split_three(-logs[:, head * HEAD : head * HEAD + 1])
        dot_terms = split_three(-jnp.sum(jnp.where(mine, dots, 0.0), axis=-1, keepdims=True))
        q_more, k_more, k_diag, g_more, v_more = (
            jnp.where(lane == spare, one, zero),
            jnp.where(lane == spare, bias, zero),
            zero,
            zero,
            zero,
        )
        for place in range(3):
            here = lane == spare + 1 + place
            q_more = jnp.where(here, log_terms[place], q_more)
            k_more = jnp.where(here, one, k_more)
            k_diag = jnp.where(here, one, k_diag)
            g_more = jnp.where(here, dot_terms[place], g_more)
            v_more = jnp.where(here, one, v_more)
        parts.append(
            dict(
                q=jnp.where(mine, q, q_more),
                k=jnp.where(mine, k, k_more),
                kd=jnp.where(mine, k, k_diag),
                g=jnp.where(mine, grad, g_more),
                v=jnp.where(mine, v, v_more),
                q0=jnp.where(mine, q, zero),
                k0=jnp.where(mine, k, zero),
                g0=jnp.where(mine, grad, zero),
            )
        )
    for i in range(count):
        at = slice(i * block, (i + 1) * block)
        dq = jnp.zeros((block, LANES), f32)
        for j in range(i + 1):
            to = slice(j * block, (j + 1) * block)
            dk = jnp.zeros((block, LANES), f32)
            dv = jnp.zeros((block, LANES), f32)
            for head in range(2):
                part = parts[head]
                if j == i:
                    score = dot_nt(part["kd"][to], part["q"][at]) + mask_ref[i]
                else:
                    score = dot_nt(part["k"][to], part["q"][at])
                soft = jnp.exp(score)
                change = (soft * dot_nt(part["v"][to], part["g"][at])).astype(bf16)
                dv += dot_nn(soft.astype(bf16), part["g0"][at])
                dk += dot_nn(change, part["q0"][at])
                dq += dot_tn(change, part["k0"][to])
            if j == i:
                dk_ref[to, :] = dk
                dv_ref[to, :] = dv
            else:
                dk_ref[to, :] += dk
                dv_ref[to, :] += dv
        out_ref[0, at, :] = (dq * 0.125).astype(bf16)
    out_ref[1] = dk_ref[...].astype(bf16)
    out_ref[2] = dv_ref[...].astype(bf16)


def attend_back(mixed, att_grad, att, logs, live_col, first=0, count=None, hold=(), block=256):
    seq, triple = mixed.shape
    pairs = triple // 3 // LANES
    count = pairs if count is None else count
    width = count * LANES
    block = min(block, seq)

    def cols(offset):
        return pl.BlockSpec((seq, LANES), lambda h: (0, offset + h))

    return call(
        functools.partial(attend_back_kernel, block),
        (count,),
        [cols(first), cols(first + pairs), cols(first + 2 * pairs)]
        + [cols(first), cols(first), cols(first), whole_spec(live_col)],
        [pl.BlockSpec((3, seq, LANES), lambda h: (0, 0, h))],
        [sds((3, seq, width), bf16)],
        10 * seq * seq * width,
        [mixed, mixed, mixed, att_grad, att, logs, live_col],
        scratch=[
            pltpu.VMEM((seq // block, block, block), f32),
            pltpu.VMEM((seq, LANES), f32),
            pltpu.VMEM((seq, LANES), f32),
        ],
        hold=hold,
    )[0]


def all_masks(bits):
    masks = [0]
    for bit in bits:
        masks += [m | (1 << bit) for m in masks]
    return masks


class Cube:
    def __init__(self):
        inner = lax.axis_size(AXES[1])
        self.count = lax.axis_size(AXES[0]) * inner
        self.bits = self.count.bit_length() - 1
        self.inner = inner.bit_length() - 1
        self.pairs = self.count >> (self.inner > 0)
        self.me = lax.axis_index(AXES)
        self.outer = list(range(self.inner, self.bits))
        self.rest = list(range(1, self.inner))
        self.turns = list(zip(self.outer, self.outer[::-1]))

    def send(self, value, mask):
        return lax.ppermute(value, AXES, [(d, d ^ mask) for d in range(self.count)])

    def send_all(self, value, bits):
        return [self.send(value, mask) for mask in all_masks(bits)[1:]]

    def place(self, device, order):
        bits = [pair[order] for pair in self.turns] + self.rest[::-1]
        found = 0
        for bit in bits:
            found = found * 2 + ((device >> bit) & 1)
        return found

    def places(self):
        return jnp.stack([self.place(self.me, 0), self.place(self.me, 1), self.me & 1, self.me])

    def order(self):
        return sorted(range(self.count), key=lambda d: (d & (self.inner > 0), self.place(d, 0)))

    def turned(self, value):
        count = len(self.turns)
        shape = value.shape
        value = value.reshape((2,) * count + (-1,) + shape[1:])
        axes = tuple(range(count))[::-1] + tuple(range(count, value.ndim))
        return value.transpose(axes).reshape(shape)


class Gather:
    def __init__(self, cube, block, split):
        self.cube, self.split = cube, split
        self.value = block[None]

    def line(self, make=None):
        got = self.cube.send_all(self.value, self.cube.rest)
        if make is not None:
            got = after(got, make)
        self.value = jnp.concatenate([self.value, *got], axis=0)
        self.halves = self.split(self.value)
        self.turns = self.cube.turns[::-1]
        return self.value

    def turn(self, *others):
        if self.turns:
            bits = self.turns.pop(0)
            got = [self.cube.send(v, 1 << bit) for v, bit in zip(self.halves, bits)]
            if others:
                got = after(got, others)
            self.halves = [jnp.concatenate(pair, axis=0) for pair in zip(self.halves, got)]
        return self.halves


def after(value, others):
    return lax.optimization_barrier((value, others))[0]


def across(cube, value):
    return [cube.send(value, 1)] if cube.inner else []


class Scatter:
    def __init__(self, cube, own, other, split, join):
        self.cube, self.own, self.other, self.split, self.join = cube, own, other, split, join
        self.todo = ["core"] * (cube.inner > 0) + list(cube.turns) + ["line"] * (len(cube.rest) > 0)
        self.halves = None if cube.inner else split(*own)
        self.now, self.got = None, []

    def finish(self):
        if self.now == "core":
            self.halves = self.split(
                *[(a.astype(f32) + b.astype(f32)).astype(bf16) for a, b in zip(self.own, self.got)]
            )
        elif self.now == "line":
            total = self.kept.astype(f32)
            for other in self.got:
                total = total + other.astype(f32)
            self.total = total
            self.now, self.got = None, []
            return [total]
        elif self.now:
            self.halves = [
                (a.astype(f32) + b.astype(f32)).astype(bf16) for a, b in zip(self.kept, self.got)
            ]
        self.now, self.got = None, []
        return []

    def step(self, *others):
        if others and self.got:
            self.got = after(self.got, others)
        ended = self.finish()
        if not self.todo:
            return ended
        self.now = self.todo.pop(0)
        if self.now == "core":
            sent, masks = self.other, [1] * len(self.other)
        elif self.now == "line":
            value = self.join(*self.halves)
            masks = all_masks(self.cube.rest)
            sent, masks = [value[i] for i in range(1, len(masks))], masks[1:]
            self.kept = value[0]
        else:
            middle = self.halves[0].shape[0] // 2
            sent, masks = [v[middle:] for v in self.halves], [1 << bit for bit in self.now]
            self.kept = [v[:middle] for v in self.halves]
        self.got = [self.cube.send(v, mask) for v, mask in zip(sent, masks)]
        return sent

    def result(self):
        while self.now or self.todo:
            self.step()
        if self.cube.rest:
            return self.total
        return self.join(*self.halves)[0].astype(f32)


def add_kernel(count, share, place_ref, *refs):
    total = refs[0][...]
    for ref in refs[1:count]:
        total = total + ref[...]
    if share:
        width = total.shape[1]
        turn = (width - place_ref[3] * share) % width
        total = pltpu.roll(total, turn, 1)[:, : refs[count].shape[1]]
    refs[count][...] = total


def add_up(place, values, hold, share=0):
    shape = values[0].shape
    if share:
        shape = (shape[0], -(-share // LANES) * LANES)
    return call(
        functools.partial(add_kernel, len(values), share), (1,),
        [pl.BlockSpec(memory_space=pltpu.SMEM)] + [whole_spec(v) for v in values],
        [pl.BlockSpec(shape, lambda i: (0, 0))], [sds(shape, f32)], 0, [place, *values], hold=hold,
    )[0]


def set_down_kernel(cube, rows, share, place_ref, *refs):
    sources, (out_ref, norms_ref) = refs[:-2], refs[-2:]
    per = len(sources) // 2
    half = out_ref.shape[2] // 2
    extra = sources[0].shape[1] - rows
    empty = jnp.zeros((extra, half), f32)
    norms = jnp.zeros(norms_ref.shape, f32)
    for device in range(cube.count):
        for order in range(2):
            at = cube.place(device, order) ^ place_ref[order]
            block = sources[order * per][at]
            if per > 1:
                own = ((device & 1) ^ place_ref[2]) == 0
                block = jnp.where(own, block, sources[order * per + 1][at])
            block = block.astype(f32)
            out_ref[device, :, order * half : (order + 1) * half] = block[:rows].astype(bf16)
            if order * half < share:
                line = [block[rows:], empty]
                line = jnp.concatenate(line[::-1] if order else line, axis=1)
                norms = norms + (pltpu.roll(line, device * share, 1) if device else line)
    norms_ref[...] = norms


def set_down(cube, place, sources, rows, share):
    _, extra, half = sources[0].shape
    shape = (cube.count, rows, 2 * half)
    norms = (extra - rows, 2 * half)
    blocks, norms = call(
        functools.partial(set_down_kernel, cube, rows, share), (1,),
        [pl.BlockSpec(memory_space=pltpu.SMEM)] + [whole_spec(a) for a in sources],
        [pl.BlockSpec(shape, lambda i: (0, 0, 0)), pl.BlockSpec(norms, lambda i: (0, 0))],
        [sds(shape, bf16), sds(norms, f32)], 0, [place, *sources],
    )
    return blocks.reshape(cube.count * rows, 2 * half), norms


def embed_kernel(share, pass_ref, table_ref, out_ref):
    total = jnp.zeros(out_ref.shape, f32)
    row = lax.broadcasted_iota(jnp.int32, table_ref.shape[1:], 0)
    for device in range(table_ref.shape[0]):
        line = jnp.where(row == pass_ref[0], table_ref[device].astype(f32), 0.0)
        line = jnp.sum(line, axis=0, keepdims=True)
        total = total + (pltpu.roll(line, device * share, 1) if device else line)
    out_ref[...] = total


def embed(pass_index, table, share):
    width = table.shape[2]
    return call(
        functools.partial(embed_kernel, share), (1,),
        [pl.BlockSpec(memory_space=pltpu.SMEM), whole_spec(table)],
        [pl.BlockSpec((1, width), lambda i: (0, 0))], [sds((1, width), f32)], 0,
        [pass_index, table],
    )[0]


def body(
    tokens, row_lengths, live_mask, pass_index,
    w_qkv, w_out, w_up, w_down, norm_gains, norm_shifts, pass_table, cotangent,
):
    _, seq, width = tokens.shape
    cube = Cube()
    place = cube.places()
    ff = w_up.shape[1] * cube.count
    block = min(256, seq)
    grid = (seq // block,)
    passes = pass_table.shape[0]

    def split_lanes(v):
        half = v.shape[2] // 2
        return [v[:, :, :half], v[:, :, half:]]

    high = w_up.shape[1]
    share = w_out.shape[1]

    def wide_rows(v):
        return jnp.pad(v, ((0, -v.shape[0] % 8), (0, width - v.shape[1])))

    packed = jnp.concatenate([w_up.T, w_down, w_out.T, wide_rows(pass_table)], axis=0)
    packed = lax.all_gather(packed, AXES, axis=0, tiled=False)

    gains_shifts = wide_rows(jnp.concatenate([norm_gains, norm_shifts], axis=0))
    part_q = Gather(cube, jnp.concatenate([w_qkv.T, gains_shifts], axis=0), split_lanes)
    part_q.line()
    for _ in cube.turns:
        part_q.turn()
    low, other_half = part_q.halves
    sources = [low, *across(cube, low), other_half, *across(cube, other_half)]
    wq, norms = set_down(cube, place, sources, w_qkv.shape[1], share)
    chosen = jnp.where(jnp.arange(passes, dtype=jnp.int32) == pass_index[0], 1.0, 0.0).astype(f32)

    positions = jnp.arange(seq, dtype=jnp.int32)
    inside = positions < row_lengths[0]
    live = jnp.where(inside[None, :] & (live_mask[:, 0] > 0), 1.0, 0.0).astype(f32)
    live_cols = [live[0][:, None], live[1][:, None]]
    live_rows = [live[0][None, :], live[1][None, :]]

    x = tokens[0]
    given = cotangent[0]
    rows_w = rows_spec(block, width)
    rows_f = rows_spec(block, ff)
    rows_q = rows_spec(block, 3 * width)
    rows_1 = rows_spec(block, 1)
    rows_3 = pl.BlockSpec((3, block, width), lambda i: (0, i, 0))
    sums_spec = pl.BlockSpec((8, width), lambda i: (0, 0))
    wide = sds((seq, width), f32)
    thin = sds((seq, width), bf16)
    tall = sds((seq, ff), bf16)
    triple = sds((seq, 3 * width), bf16)
    sums_shape = sds((8, width), f32)
    unit = 2 * seq * width

    mixed0, normed0 = call(
        first_kernel, grid,
        [rows_w, whole_spec(norms), whole_spec(wq)],
        [rows_q, rows_w], [triple, thin], unit * 3 * width, [x, norms, wq],
    )
    pairs = width // LANES
    third = pairs // 3 if pairs % 3 == 0 else pairs
    att0, logs0 = attend(mixed0, live_cols[0], live_rows[0])
    packed = after(packed, att0)
    wo = packed[:, 2 * high : 2 * high + share].reshape(width, width)
    emb = embed(pass_index, packed[:, 2 * high + share :], share)
    order, share = cube.order(), high
    if cube.count == 1 or 768 % high or high % 16:
        blocks = [packed[:, at : at + high] for at in (0, high)]
        turned = [
            jnp.take(v, jnp.asarray(order, jnp.int32) ^ cube.me, axis=0).reshape(ff, width)
            for v in blocks
        ]
        packed, share = jnp.concatenate(turned, axis=0)[None], ff
    smem = pl.BlockSpec(memory_space=pltpu.SMEM)
    hidden0, second0, act0, slope0, later, mixed1, normed1 = call(
        functools.partial(middle_kernel, order, share), grid,
        [smem, whole_spec(packed), rows_w, rows_w, rows_1]
        + [whole_spec(a) for a in (norms, emb, wo, wq)],
        [rows_w, rows_w, rows_f, rows_f, rows_w, rows_q, rows_w],
        [wide, thin, tall, tall, wide, triple, thin],
        unit * (4 * width + 2 * ff),
        [place, packed, att0, x, live_cols[0], norms, emb, wo, wq],
    )
    att1, logs1 = attend(mixed1, live_cols[1], live_rows[1])
    result, second1, act1, drop1, lift1, branch1, hgrad1, agrad1, sums1 = call(
        functools.partial(turn_kernel, order, share), grid,
        [smem, whole_spec(packed), rows_w, rows_w, rows_1, whole_spec(norms), rows_w]
        + [whole_spec(wo)],
        [rows_w, rows_w, rows_f, rows_w, rows_f, rows_w, rows_w, rows_w, sums_spec],
        [thin, thin, tall, thin, tall, thin, wide, thin, sums_shape],
        unit * (2 * width + 4 * ff),
        [place, packed, att1, later, live_cols[1], norms, given, wo],
    )
    mgrad1 = attend_back(mixed1, agrad1, att1, logs1, live_cols[1])
    drop0, lift0, branch0, hgrad0, agrad0, sums0 = call(
        functools.partial(back_kernel, order, share), grid,
        [smem, whole_spec(packed), rows_3, rows_w, rows_w, whole_spec(norms), rows_1, rows_w, rows_f]
        + [whole_spec(a) for a in (wq, wo)],
        [rows_w, rows_f, rows_w, rows_w, rows_w, sums_spec],
        [thin, tall, thin, wide, thin, sums_shape],
        unit * (4 * width + 2 * ff),
        [place, packed, mgrad1, later, hgrad1, norms, live_cols[0], hidden0, slope0, wq, wo],
    )
    share = cube.pairs * high
    start = w_up.shape[1] // 2

    def split_down(v):
        v = v.reshape(cube.pairs, high, width)
        return [v[:, :start], cube.turned(v[:, start:])]

    def split_up_out(v, out):
        low, turned = split_down(v)
        return [jnp.concatenate([low, out], axis=1), turned]

    def join_rows(low, high):
        return jnp.concatenate([low, high], axis=1)

    def join_lanes(low, high):
        return jnp.concatenate([low, high], axis=2)

    def both(left0, left1, right0, right1, hold):
        other = [
            pair_grads(left0, left1, right0, right1, at, share, hold=hold)
            for at in range(share, ff, share)
        ]
        return pair_grads(left0, left1, right0, right1, 0, share, hold=hold + other), other

    up_other = [
        pair_grads(lift0, lift1, second0, second1, at, share) for at in range(share, ff, share)
    ]
    own, other = both(act0, act1, drop0, drop1, up_other)
    down = Scatter(cube, [own], other, split_down, join_rows)
    down.step()
    hold = [own] + down.step(own)
    out_own, out_other = out_grads(cube, place, branch0, branch1, [att0], att1, hold)
    up_own = pair_grads(lift0, lift1, second0, second1, 0, share, hold=[out_own])
    up_out = Scatter(cube, [up_own, out_own], [*up_other, out_other], split_up_out, join_rows)
    up_out.step()
    hold = [up_own] + up_out.step(up_own) + down.step(up_own)
    groups = []
    for first in range(0, pairs, third):
        group = attend_back(mixed0, agrad0, att0, logs0, live_cols[0], first, third, hold)
        groups.append(group)
        hold = [group] + up_out.step(group) + down.step(group)
    own, other = qkv_grads(cube, place, groups, mgrad1, normed0, normed1, hold)
    up_out.step(own)
    qkv = Scatter(cube, [own], [other], split_lanes, join_lanes)
    qkv.step()
    hold = qkv.step()
    specs_g = [
        pl.BlockSpec((3, block, a.shape[2]), lambda i: (0, i, 0)) for a in groups
    ]
    input_grad, sums_last = call(
        functools.partial(last_kernel, len(groups)), grid,
        specs_g + [rows_w, rows_w, whole_spec(norms), whole_spec(wq)],
        [rows_w, sums_spec], [wide, sums_shape], unit * 3 * width,
        [*groups, x, hgrad0, norms, wq],
        hold=hold,
    )

    gain0 = sums0[2] + sums_last[0]
    shift0 = sums0[3] + sums_last[1]
    gain1 = sums0[0] + sums1[0]
    shift1 = sums0[1] + sums1[1]
    table = chosen[:, None] * sums0[4][None, :]
    small_grad = jnp.concatenate([jnp.stack([gain0, gain1, shift0, shift1]), table], axis=0)
    small_grad = jnp.pad(small_grad, ((0, -small_grad.shape[0] % 8), (0, 0)))
    for bits in ([0] if cube.inner else [], cube.outer):
        if bits:
            small_grad = add_up(place, [small_grad, *cube.send_all(small_grad, bits)], qkv.step())
    small_grad = add_up(
        place, [small_grad, *cube.send_all(small_grad, cube.rest)], [], width // cube.count
    )
    share = width // cube.count
    small = small_grad[:, :share]
    down = down.result()
    up_out = up_out.result()
    qkv = qkv.result().T
    low_end = high // 2
    out_end = low_end + w_out.shape[1]
    up = jnp.concatenate([up_out[:low_end], up_out[out_end:]], axis=0).T
    out = up_out[low_end:out_end].T
    return (
        result[None], input_grad[None], qkv, out, up, down,
        small[:2], small[2], small[3], small[4 : 4 + passes],
    )


def solution(mesh):
    placed = (
        P(AXES, None, None),
        P(AXES),
        P(None, AXES, None),
        P(AXES),
        P(None, AXES),
        P(None, AXES),
        P(None, AXES),
        P(AXES, None),
        P(None, AXES),
        P(None, AXES),
        P(None, AXES),
        P(AXES, None, None),
    )
    return jax.shard_map(
        body,
        mesh=mesh,
        in_specs=placed,
        out_specs=(
            P(AXES, None, None),
            P(AXES, None, None),
            P(None, AXES),
            P(None, AXES),
            P(None, AXES),
            P(AXES, None),
            P(None, AXES),
            P(AXES),
            P(AXES),
            P(None, AXES),
        ),
        check_vma=False,
    )
```

```python
import functools

import jax
import jax.numpy as jnp
from jax import lax
from jax.experimental import pallas as pl
from jax.experimental.pallas import tpu as pltpu
from jax.sharding import PartitionSpec as P

HEAD = 64
LANES = 128
AXES = ("dp", "fsdp")
bf16 = jnp.bfloat16
f32 = jnp.float32

norm_epsilon = 1e-05
masked_score = -1000000000.0
curve_one = 0.7978845608028654
curve_three = 0.7978845608028654 * 0.044715

VMEM_LIMIT = 60 * 1024 * 1024


def dot_nn(left, right):
    return lax.dot_general(left, right, (((1,), (0,)), ((), ())), preferred_element_type=f32)


def dot_nt(left, right):
    return lax.dot_general(left, right, (((1,), (1,)), ((), ())), preferred_element_type=f32)


def dot_tn(left, right):
    return lax.dot_general(left, right, (((0,), (0,)), ((), ())), preferred_element_type=f32)


def normalize(values):
    center = jnp.mean(values, axis=-1, keepdims=True)
    centered = values - center
    spread = jnp.mean(centered * centered, axis=-1, keepdims=True)
    scale = lax.rsqrt(spread + norm_epsilon)
    return centered * scale, scale


def norm_back(grad, gain, xhat, scale):
    gained = grad * gain
    first = jnp.mean(gained, axis=-1, keepdims=True)
    second = jnp.mean(gained * xhat, axis=-1, keepdims=True)
    return scale * (gained - first - xhat * second)


def gelu_pair(lifted):
    square = lifted * lifted
    cubic = curve_three * square
    half = 0.5 + 0.5 * jnp.tanh(lifted * (curve_one + cubic))
    value = lifted * half
    slope = half + value * ((1.0 - half) * (2.0 * curve_one + 6.0 * cubic))
    return value, slope


def call(kernel, grid, in_specs, out_specs, out_shape, flops, args, scratch=(), hold=()):
    moved = sum(a.size * a.dtype.itemsize for a in args)
    moved += sum(o.size * o.dtype.itemsize for o in out_shape)
    given, held = len(args), len(hold)

    def run(*refs):
        kernel(*refs[:given], *refs[given + held :])

    return pl.pallas_call(
        run,
        grid=grid,
        in_specs=list(in_specs) + [pl.BlockSpec(memory_space=pl.ANY)] * held,
        out_specs=out_specs,
        out_shape=out_shape,
        scratch_shapes=list(scratch),
        compiler_params=pltpu.CompilerParams(
            dimension_semantics=("arbitrary",) * len(grid), vmem_limit_bytes=VMEM_LIMIT
        ),
        cost_estimate=pl.CostEstimate(
            flops=flops // 4096, bytes_accessed=moved // 4096, transcendentals=0
        ),
    )(*args, *hold)


def rows_spec(block_rows, width):
    return pl.BlockSpec((block_rows, width), lambda i: (i, 0))


def whole_spec(array):
    zeros = (0,) * len(array.shape)
    return pl.BlockSpec(array.shape, lambda i: zeros, pipeline_mode=pl.Buffered(1))


def sds(shape, dtype):
    return jax.ShapeDtypeStruct(shape, dtype)


def head_part(x, gain, shift, w_qkv, mixed_ref, xhat_ref):
    xhat, _ = normalize(x)
    normed = (xhat * gain + shift).astype(bf16)
    xhat_ref[...] = xhat.astype(bf16)
    mixed_ref[...] = dot_nt(normed, w_qkv[...]).astype(bf16)


def first_kernel(x_ref, norms_ref, wq_ref, mixed_ref, xhat_ref):
    head_part(
        x_ref[...].astype(f32), norms_ref[0:1, :], norms_ref[2:3, :], wq_ref, mixed_ref, xhat_ref
    )


def ff_chunks(order, place_ref, packed_ref, share):
    found = []
    if share >= 768:
        for at in range(0, share, 768):
            up, down = pl.ds(at, 768), pl.ds(share + at, 768)
            found.append((lambda r=up: packed_ref[0, r, :], lambda r=down: packed_ref[0, r, :], pl.ds(at, 768)))
        return found
    per = 768 // share
    for first in range(0, len(order), per):

        def rows(at, first=first):
            return jnp.concatenate(
                [
                    packed_ref[place_ref[3] ^ mask, pl.ds(at, share), :]
                    for mask in order[first : first + per]
                ],
                axis=0,
            )

        found.append(
            (functools.partial(rows, 0), functools.partial(rows, share), pl.ds(first * share, 768))
        )
    return found


def middle_kernel(order, share, place_ref, packed_ref, *refs):
    chunks = ff_chunks(order, place_ref, packed_ref, share)
    atts, refs = refs[:-13], refs[-13:]
    (
        x_ref, live_ref, norms_ref, emb_ref, wo_ref, wq_ref,
        hidden_ref, second_ref, act_ref, slope_ref, later_ref, mixed_ref, xhat_ref,
    ) = refs
    live = live_ref[...]
    branch, at = 0.0, 0
    for ref in atts:
        branch = branch + dot_nt(ref[...], wo_ref[:, at : at + ref.shape[1]])
        at += ref.shape[1]
    hidden = x_ref[...].astype(f32) + live * branch
    hidden_ref[...] = hidden
    xhat, _ = normalize(hidden)
    second = (xhat * norms_ref[1:2, :] + norms_ref[3:4, :]).astype(bf16)
    second_ref[...] = second
    total = jnp.zeros_like(hidden)
    for up, down, to in chunks:
        value, slope = gelu_pair(dot_nt(second, up()))
        value = value.astype(bf16)
        act_ref[:, to] = value
        slope_ref[:, to] = slope.astype(bf16)
        total = total + dot_nn(value, down())
    later = hidden + live * total + emb_ref[...]
    later_ref[...] = later
    head_part(later, norms_ref[0:1, :], norms_ref[2:3, :], wq_ref, mixed_ref, xhat_ref)


def mlp_back_tail(
    grad, live, hidden, second_grad, norms_ref, wo_ref, branch_ref, hgrad_ref, agrad_ref
):
    xhat, scale = normalize(hidden)
    hgrad = grad + norm_back(second_grad, norms_ref[1:2, :], xhat, scale)
    hgrad_ref[...] = hgrad
    branch = (live * hgrad).astype(bf16)
    branch_ref[...] = branch
    agrad_ref[...] = dot_nn(branch, wo_ref[...]).astype(bf16)
    gain_sum = jnp.sum(second_grad * xhat, axis=0, keepdims=True)
    shift_sum = jnp.sum(second_grad, axis=0, keepdims=True)
    return gain_sum, shift_sum


def add_sums(sums_ref, sums):
    @pl.when(pl.program_id(0) == 0)
    def _():
        sums_ref[...] = jnp.zeros_like(sums_ref)

    for place, value in enumerate(sums):
        sums_ref[place : place + 1, :] += value


def turn_kernel(order, share, place_ref, packed_ref, *refs):
    chunks = ff_chunks(order, place_ref, packed_ref, share)
    (
        att_ref, x_ref, live_ref, norms_ref, grad_ref, wo_ref,
        out_ref, second_ref, act_ref, drop_ref, lift_ref, branch_ref, hgrad_ref, agrad_ref, sums_ref,
    ) = refs
    live = live_ref[...]
    hidden = x_ref[...] + live * dot_nt(att_ref[...], wo_ref[...])
    xhat, _ = normalize(hidden)
    second = (xhat * norms_ref[1:2, :] + norms_ref[3:4, :]).astype(bf16)
    second_ref[...] = second
    grad = grad_ref[...]
    drop = (live * grad).astype(bf16)
    drop_ref[...] = drop
    total = jnp.zeros_like(hidden)
    second_grad = jnp.zeros_like(hidden)
    for up, down, to in chunks:
        up, down = up(), down()
        value, slope = gelu_pair(dot_nt(second, up))
        value = value.astype(bf16)
        act_ref[:, to] = value
        total = total + dot_nn(value, down)
        lift = (dot_nt(drop, down) * slope).astype(bf16)
        lift_ref[:, to] = lift
        second_grad = second_grad + dot_nn(lift, up)
    out_ref[...] = (hidden + live * total).astype(bf16)
    sums = mlp_back_tail(
        grad, live, hidden, second_grad, norms_ref, wo_ref, branch_ref, hgrad_ref, agrad_ref
    )
    add_sums(sums_ref, sums)


def head_back(mixed_grad_refs, wq_ref, x, hgrad, norms_ref):
    width = x.shape[1]
    normed_grad = jnp.zeros_like(x)
    for part in range(3):
        at = part * width
        for ref in mixed_grad_refs:
            normed_grad += dot_nn(ref[part], wq_ref[at : at + ref.shape[2], :])
            at += ref.shape[2]
    xhat, scale = normalize(x)
    return hgrad + norm_back(normed_grad, norms_ref[0:1, :], xhat, scale)


def back_kernel(order, share, place_ref, packed_ref, *refs):
    chunks = ff_chunks(order, place_ref, packed_ref, share)
    (
        mgrad_ref, later_ref, hgrad1_ref, norms_ref, live_ref, hidden_ref, slope_ref, wq_ref, wo_ref,
        drop_ref, lift_ref, branch_ref, hgrad_ref, agrad_ref, sums_ref,
    ) = refs
    grad = head_back([mgrad_ref], wq_ref, later_ref[...], hgrad1_ref[...], norms_ref)
    table_sum = jnp.sum(grad, axis=0, keepdims=True)
    live = live_ref[...]
    drop = (live * grad).astype(bf16)
    drop_ref[...] = drop
    second_grad = jnp.zeros_like(grad)
    for up, down, to in chunks:
        lift = (dot_nt(drop, down()) * slope_ref[:, to].astype(f32)).astype(bf16)
        lift_ref[:, to] = lift
        second_grad = second_grad + dot_nn(lift, up())
    sums = mlp_back_tail(
        grad, live, hidden_ref[...], second_grad, norms_ref, wo_ref, branch_ref, hgrad_ref, agrad_ref
    )
    add_sums(sums_ref, sums + (table_sum,))


def last_kernel(groups, *refs):
    mgrad_refs, (x_ref, hgrad_ref, norms_ref, wq_ref, out_ref) = refs[:groups], refs[groups:]
    out_ref[...] = head_back(
        mgrad_refs, wq_ref, x_ref[...].astype(f32), hgrad_ref[...], norms_ref
    )


def both_layers(left0, left1, right0, right1):
    return dot_tn(left0[...], right0[...]) + dot_tn(left1[...], right1[...])


def pair_grad_kernel(left0, left1, right0, right1, out_ref):
    out_ref[...] = both_layers(left0, left1, right0, right1).astype(bf16)


def pair_grads(left0, left1, right0, right1, start, size, hold=()):
    tokens = left0.shape[0]
    width = right0.shape[1]
    step = 384 if size % 384 == 0 else size
    first = start // step
    cols = pl.BlockSpec((tokens, step), lambda i: (0, first + i))
    return call(
        pair_grad_kernel,
        (size // step,),
        [cols] * 2 + [whole_spec(right0)] * 2,
        [rows_spec(step, width)],
        [sds((size, width), bf16)],
        4 * tokens * size * width,
        [left0, left1, right0, right1],
        hold=hold,
    )[0]


def blocks_spec(shape, index):
    return pl.BlockSpec(shape, lambda i: (index(i), 0, 0))


def other_grad_kernel(high, left0, left1, right0, right1, *refs):
    extra, out_ref = refs[:-1], refs[-1]
    total = both_layers(left0, left1, right0, right1).astype(bf16)
    for place in range(out_ref.shape[0]):
        out_ref[place, :high, :] = total[place * high : (place + 1) * high]
        for ref in extra:
            out_ref[place, high:, :] = ref[place]


def other_grads(cube, high, left0, left1, right0, right1, extra=(), hold=()):
    tokens = left0.shape[0]
    width = right0.shape[1]
    lines, turns = cube.count_line, cube.count_turns
    first = turns
    cols = pl.BlockSpec((tokens, lines * high), lambda i: (0, first + i))
    rows = high + sum(a.shape[1] for a in extra)
    return call(
        functools.partial(other_grad_kernel, high),
        (turns,),
        [cols] * 2
        + [whole_spec(right0)] * 2
        + [blocks_spec((lines,) + a.shape[1:], lambda i: i) for a in extra],
        [blocks_spec((lines, rows, width), lambda i: i)],
        [sds((cube.pairs, rows, width), bf16)],
        4 * tokens * cube.pairs * high * width,
        [left0, left1, right0, right1, *extra],
        hold=hold,
    )[0]


def own_grad_kernel(high, left0, left1, right0, right1, got, *refs):
    extra, (low_keep, low_send, late_keep, late_send) = refs[:-4], refs[-4:]
    middle = high // 2
    half = pl.num_programs(0) // 2
    step = pl.program_id(0)
    total = both_layers(left0, left1, right0, right1)

    def low_part(ref):
        for place in range(ref.shape[0]):
            at = place * high
            ref[place, :middle, :] = (
                total[at : at + middle] + got[place, :middle, :].astype(f32)
            ).astype(bf16)
            for more in extra:
                ref[place, middle:, :] = (
                    more[place].astype(f32) + got[place, high:, :].astype(f32)
                ).astype(bf16)

    def late_part(ref):
        for place in range(ref.shape[0]):
            at = place * high
            ref[place] = (
                total[at + middle : at + high] + got[place, middle:high, :].astype(f32)
            ).astype(bf16)

    @pl.when(step < half)
    def _():
        low_part(low_keep)

    @pl.when(step >= half)
    def _():
        low_part(low_send)

    @pl.when(step % 2 == 0)
    def _():
        late_part(late_keep)

    @pl.when(step % 2 == 1)
    def _():
        late_part(late_send)


def own_grads(cube, high, left0, left1, right0, right1, got, extra=(), hold=()):
    tokens = left0.shape[0]
    width = right0.shape[1]
    lines, turns = cube.count_line, cube.count_turns
    half = turns // 2
    cols = pl.BlockSpec((tokens, lines * high), lambda i: (0, i))
    low = high // 2 + sum(a.shape[1] for a in extra)
    late = high - high // 2

    def turned(i):
        found = 0
        for bit in range(1, turns.bit_length() - 1):
            found = found + (((i >> bit) & 1) << (turns.bit_length() - 2 - bit))
        return found

    def first_keep(i):
        return jnp.minimum(i, half - 1)

    def first_send(i):
        return jnp.maximum(i - half, 0)

    return call(
        functools.partial(own_grad_kernel, high),
        (turns,),
        [cols] * 2
        + [whole_spec(right0)] * 2
        + [blocks_spec((lines,) + a.shape[1:], lambda i: i) for a in (got, *extra)],
        [
            blocks_spec((lines, low, width), first_keep),
            blocks_spec((lines, low, width), first_send),
            blocks_spec((lines, late, width), turned),
            blocks_spec((lines, late, width), turned),
        ],
        [sds((cube.pairs // 2, n, width), bf16) for n in (low, low, late, late)],
        4 * tokens * cube.pairs * high * width,
        [left0, left1, right0, right1, got, *extra],
        hold=hold,
    )


def place_blocks(cube, place_ref, total_ref, own_ref, other_ref):
    rows = own_ref.shape[1]
    for chip in range(own_ref.shape[0]):
        if cube.inner == 0:
            own_ref[0] = total_ref[...].astype(bf16)
            continue
        even = total_ref[pl.ds(2 * chip * rows, rows), :].astype(bf16)
        odd = total_ref[pl.ds((2 * chip + 1) * rows, rows), :].astype(bf16)
        first = place_ref[2] == 0
        at = cube.place(2 * chip, 0) ^ place_ref[0]
        own_ref[at] = jnp.where(first, even, odd)
        other_ref[at] = jnp.where(first, odd, even)


def out_grad_kernel(cube, place_ref, left0, left1, right0, right1, own_ref, other_ref, total_ref):
    total_ref[...] = both_layers(left0, left1, right0, right1)
    place_blocks(cube, place_ref, total_ref, own_ref, other_ref)


def block_shapes(cube, rows, width):
    shape = (cube.pairs, rows, width)
    return [sds(shape, bf16)] * 2, [pl.BlockSpec(shape, lambda i: (0, 0, 0))] * 2


def out_grads(cube, place, left0, left1, right0, right1, hold=()):
    tokens, high = left0.shape
    width = right1.shape[1]
    shapes, specs = block_shapes(cube, high // cube.count, width)
    args = [left0, left1, right0, right1]
    return call(
        functools.partial(out_grad_kernel, cube),
        (1,),
        [pl.BlockSpec(memory_space=pltpu.SMEM)] + [whole_spec(a) for a in args],
        specs,
        shapes,
        4 * tokens * high * width,
        [place, *args],
        scratch=[pltpu.VMEM((high, width), f32)],
        hold=hold,
    )


def qkv_grad_kernel(cube, groups, passes, place_ref, pass_ref, *refs):
    lefts0, refs = refs[:groups], refs[groups:]
    left1, right0, right1, wq_ref, norms_ref, sums0_ref, sums1_ref, own_ref, other_ref = refs[:9]
    small_ref, total_ref = refs[9:]
    part = pl.program_id(0)
    high = left1.shape[2]
    width = right0.shape[1]
    gain, shift = norms_ref[0:1, :], norms_ref[2:3, :]
    ones = jnp.ones((8, right0.shape[0]), bf16)
    row = lax.broadcasted_iota(jnp.int32, (8, 1), 0)

    @pl.when(part == 0)
    def _():
        small_ref[...] = jnp.zeros_like(small_ref)
        small_ref[1:2, :] = sums0_ref[0:1, :] + sums1_ref[0:1, :]
        small_ref[3:4, :] = sums0_ref[1:2, :] + sums1_ref[1:2, :]
        for index in range(passes):
            small_ref[4 + index : 5 + index, :] = jnp.where(
                pass_ref[0] == index, sums0_ref[2:3, :], 0.0
            )

    at = 0
    gain_sum = jnp.zeros((1, width), f32)
    shift_sum = jnp.zeros((1, width), f32)
    for left0 in lefts0:
        to = pl.ds(at, left0.shape[2])
        rows = pl.ds(pl.multiple_of(part * high + at, 8), left0.shape[2])
        total = dot_tn(left0[0], right0[...]) + dot_tn(left1[0, :, to], right1[...])
        sums = dot_nn(ones, left0[0]) + dot_nn(ones, left1[0, :, to])
        terms = split_three(sums)
        three = jnp.where(row == 0, terms[0], jnp.where(row == 1, terms[1], terms[2]))
        three = jnp.where(row < 3, three, jnp.zeros_like(three))
        shifts = jnp.broadcast_to(shift, (8, width)).astype(bf16)
        weights = wq_ref[rows, :]
        gain_sum += jnp.sum(total * weights.astype(f32), axis=0, keepdims=True)
        shift_sum += jnp.sum(dot_nn(three, weights), axis=0, keepdims=True)
        total_ref[rows, :] = total * gain + dot_tn(three, shifts)
        at += left0.shape[2]
    small_ref[0:1, :] += gain_sum
    small_ref[2:3, :] += shift_sum

    @pl.when(part == pl.num_programs(0) - 1)
    def _():
        extra = 8
        rows = own_ref.shape[1] - extra
        share = width // cube.count
        half = width // 2
        small = small_ref[...]
        for chip in range(cube.pairs):
            found = []
            for device in range(2 * chip, 2 * chip + 1 + (cube.inner > 0)):
                block = total_ref[pl.ds(device * rows, rows), :]
                line = pltpu.roll(small, width - device * share, 1) if device else small
                line = jnp.concatenate([line[:8, :half], line[8:, :half]], axis=1)
                found.append(jnp.concatenate([block, line], axis=0).astype(bf16))
            if cube.inner == 0:
                own_ref[0] = found[0]
                continue
            first = place_ref[2] == 0
            own = jnp.where(first, found[0], found[1])
            other = jnp.where(first, found[1], found[0])
            for order in range(2):
                lanes = slice(order * half, (order + 1) * half)
                at = cube.place(2 * chip, order) ^ place_ref[order]
                own_ref[at, :, lanes] = own[:, lanes]
                other_ref[at, :, lanes] = other[:, lanes]


def qkv_grads(cube, passes, place, pass_index, lefts0, left1, right0, right1, kept, hold=()):
    parts, tokens, high = left1.shape
    width = right0.shape[1]
    specs = [
        pl.BlockSpec((1, tokens, a.shape[2]), lambda i: (i, 0, 0)) for a in (*lefts0, left1)
    ]
    shapes, out_specs = block_shapes(cube, parts * high // cube.count + 8, width)
    return call(
        functools.partial(qkv_grad_kernel, cube, len(lefts0), passes),
        (parts,),
        [pl.BlockSpec(memory_space=pltpu.SMEM)] * 2
        + specs
        + [whole_spec(a) for a in (right0, right1, *kept)],
        out_specs + [pl.BlockSpec((16, width), lambda i: (0, 0))],
        shapes + [sds((16, width), f32)],
        4 * tokens * parts * high * width,
        [place, pass_index, *lefts0, left1, right0, right1, *kept],
        scratch=[pltpu.VMEM((parts * high, width), f32)],
        hold=hold,
    )


def lane_index(shape):
    return lax.broadcasted_iota(jnp.int32, shape, len(shape) - 1)


def split_three(values):
    high = values.astype(bf16)
    rest = values - high.astype(f32)
    middle = rest.astype(bf16)
    low = (rest - middle.astype(f32)).astype(bf16)
    return high, middle, low


def own_lanes(lane, head):
    return (lane < HEAD) if head == 0 else (lane >= HEAD)


def attend_kernel(
    block, q_ref, k_ref, v_ref, live_col_ref, live_row_ref, out_ref, logs_ref, mask_ref
):
    seq = q_ref.shape[0]
    count = seq // block

    @pl.when(pl.program_id(0) == 0)
    def _():
        query = lax.broadcasted_iota(jnp.int32, (block, block), 0)
        key = lax.broadcasted_iota(jnp.int32, (block, block), 1)
        for i in range(count):
            alive = live_row_ref[:, i * block : (i + 1) * block] > 0.5
            visible = (key <= query) & (alive | (key == query))
            mask_ref[i] = jnp.where(visible, 0.0, masked_score)

    lane = lane_index((seq, LANES))
    q = q_ref[...] * 0.125
    k = k_ref[...]
    v = v_ref[...]
    bias = ((live_col_ref[...] - 1.0) * 1e9).astype(bf16)
    zero = jnp.zeros((seq, LANES), bf16)
    one = jnp.ones((seq, LANES), bf16)
    parts = []
    for head in range(2):
        mine = own_lanes(lane, head)
        spare = (1 - head) * HEAD
        parts.append(
            (
                jnp.where(mine, q, zero),
                jnp.where(mine, q, jnp.where(lane == spare, one, zero)),
                jnp.where(mine, k, jnp.where(lane == spare, bias, zero)),
                jnp.where(mine, v, one),
            )
        )
    low = lane_index((block, LANES)) < HEAD

    def score(i, head):
        at, before = slice(i * block, (i + 1) * block), slice(0, i * block)
        q_plain, q_bias, k_bias, _ = parts[head]
        diag = dot_nt(q_plain[at], k[at]) + mask_ref[i]
        return diag, dot_nt(q_bias[at], k_bias[before]) if i > 0 else None

    def soften(diag, off):
        top = jnp.max(diag, axis=-1, keepdims=True)
        if off is None:
            return top, jnp.exp(diag - top).astype(bf16), None
        top = jnp.maximum(top, jnp.max(off, axis=-1, keepdims=True))
        return top, jnp.exp(diag - top).astype(bf16), jnp.exp(off - top).astype(bf16)

    def finish(i, head, top, diag, off):
        at, before = slice(i * block, (i + 1) * block), slice(0, i * block)
        v_ones = parts[head][3]
        total = dot_nn(diag, v_ones[at])
        if i > 0:
            total += dot_nn(off, v_ones[before])
        spare = (1 - head) * HEAD
        weight = total[:, spare : spare + 1]
        found.append((total * (1.0 / weight), top + jnp.log(weight)))
        if head == 1:
            (out0, log0), (out1, log1) = found[-2:]
            out_ref[at, :] = jnp.where(low, out0, out1).astype(bf16)
            logs_ref[at, :] = jnp.where(low, log0, log1)

    found = []
    steps = [(i, head) for i in range(count) for head in range(2)]
    ahead, behind = score(*steps[0]), None
    for place, step in enumerate(steps):
        scored = ahead
        if place + 1 < len(steps):
            ahead = score(*steps[place + 1])
        softened = soften(*scored)
        if behind is not None:
            finish(*steps[place - 1], *behind)
        behind = softened
    finish(*steps[-1], *behind)


def attend(mixed, live_col, live_row, first=0, count=None, hold=(), block=256):
    seq, triple = mixed.shape
    pairs = triple // 3 // LANES
    count = pairs if count is None else count
    width = count * LANES
    block = min(block, seq)

    def cols(offset):
        return pl.BlockSpec((seq, LANES), lambda h: (0, offset + h))

    return call(
        functools.partial(attend_kernel, block),
        (count,),
        [cols(first), cols(first + pairs), cols(first + 2 * pairs), whole_spec(live_col), whole_spec(live_row)],
        [cols(0), cols(0)],
        [sds((seq, width), bf16), sds((seq, width), f32)],
        4 * seq * seq * width,
        [mixed, mixed, mixed, live_col, live_row],
        scratch=[pltpu.VMEM((seq // block, block, block), f32)],
        hold=hold,
    )


def attend_back_kernel(
    block, q_ref, k_ref, v_ref, grad_ref, att_ref, logs_ref, live_col_ref, out_ref,
    mask_ref, dk_ref, dv_ref,
):
    seq = q_ref.shape[0]
    count = seq // block

    @pl.when(pl.program_id(0) == 0)
    def _():
        key = lax.broadcasted_iota(jnp.int32, (block, block), 0)
        query = lax.broadcasted_iota(jnp.int32, (block, block), 1)
        for i in range(count):
            alive = live_col_ref[i * block : (i + 1) * block, :] > 0.5
            visible = (key <= query) & (alive | (key == query))
            mask_ref[i] = jnp.where(visible, 0.0, masked_score)

    lane = lane_index((seq, LANES))
    q = q_ref[...] * 0.125
    k = k_ref[...]
    v = v_ref[...]
    grad = grad_ref[...]
    logs = logs_ref[...]
    dots = grad.astype(f32) * att_ref[...].astype(f32)
    bias = ((live_col_ref[...] - 1.0) * 1e9).astype(bf16)
    zero = jnp.zeros((seq, LANES), bf16)
    one = jnp.ones((seq, LANES), bf16)
    parts = []
    for head in range(2):
        mine = own_lanes(lane, head)
        spare = (1 - head) * HEAD
        log_terms = split_three(-logs[:, head * HEAD : head * HEAD + 1])
        dot_terms = split_three(-jnp.sum(jnp.where(mine, dots, 0.0), axis=-1, keepdims=True))
        q_more, k_more, k_diag, g_more, v_more = (
            jnp.where(lane == spare, one, zero),
            jnp.where(lane == spare, bias, zero),
            zero,
            zero,
            zero,
        )
        for place in range(3):
            here = lane == spare + 1 + place
            q_more = jnp.where(here, log_terms[place], q_more)
            k_more = jnp.where(here, one, k_more)
            k_diag = jnp.where(here, one, k_diag)
            g_more = jnp.where(here, dot_terms[place], g_more)
            v_more = jnp.where(here, one, v_more)
        parts.append(
            dict(
                q=jnp.where(mine, q, q_more),
                k=jnp.where(mine, k, k_more),
                kd=jnp.where(mine, k, k_diag),
                g=jnp.where(mine, grad, g_more),
                v=jnp.where(mine, v, v_more),
                q0=jnp.where(mine, q, zero),
                k0=jnp.where(mine, k, zero),
                g0=jnp.where(mine, grad, zero),
            )
        )
    def rows(i):
        return slice(i * block, (i + 1) * block)

    def score(i, j, head):
        part = parts[head]
        first = dot_nt(part["kd" if j == i else "k"][rows(j)], part["q"][rows(i)])
        return first, dot_nt(part["v"][rows(j)], part["g"][rows(i)])

    def soften(i, j, head, scores, change):
        if j == i:
            scores = scores + mask_ref[i]
        soft = jnp.exp(scores)
        return soft.astype(bf16), (soft * change).astype(bf16)

    def add(name, value):
        totals[name] = totals[name] + value if name in totals else value

    def finish(i, j, head, soft, change):
        part = parts[head]
        add("v", dot_nn(soft, part["g0"][rows(i)]))
        add("k", dot_nn(change, part["q0"][rows(i)]))
        add("q", dot_tn(change, part["k0"][rows(j)]))
        if head == 1:
            for name, ref in (("v", dv_ref), ("k", dk_ref)):
                if j == i:
                    ref[rows(j), :] = totals.pop(name)
                else:
                    ref[rows(j), :] += totals.pop(name)
            if j == i:
                out_ref[0, rows(i), :] = (totals.pop("q") * 0.125).astype(bf16)

    totals = {}
    steps = [(i, j, head) for i in range(count) for j in range(i + 1) for head in range(2)]
    ahead, behind = score(*steps[0]), None
    for place, step in enumerate(steps):
        scored = ahead
        if place + 1 < len(steps):
            ahead = score(*steps[place + 1])
        softened = soften(*step, *scored)
        if behind is not None:
            finish(*steps[place - 1], *behind)
        behind = softened
    finish(*steps[-1], *behind)
    out_ref[1] = dk_ref[...].astype(bf16)
    out_ref[2] = dv_ref[...].astype(bf16)


def attend_back(mixed, att_grad, att, logs, live_col, first=0, count=None, hold=(), block=256):
    seq, triple = mixed.shape
    pairs = triple // 3 // LANES
    count = pairs if count is None else count
    width = count * LANES
    block = min(block, seq)

    def cols(offset):
        return pl.BlockSpec((seq, LANES), lambda h: (0, offset + h))

    return call(
        functools.partial(attend_back_kernel, block),
        (count,),
        [cols(first), cols(first + pairs), cols(first + 2 * pairs)]
        + [cols(first), cols(first), cols(first), whole_spec(live_col)],
        [pl.BlockSpec((3, seq, LANES), lambda h: (0, 0, h))],
        [sds((3, seq, width), bf16)],
        10 * seq * seq * width,
        [mixed, mixed, mixed, att_grad, att, logs, live_col],
        scratch=[
            pltpu.VMEM((seq // block, block, block), f32),
            pltpu.VMEM((seq, LANES), f32),
            pltpu.VMEM((seq, LANES), f32),
        ],
        hold=hold,
    )[0]


def all_masks(bits):
    masks = [0]
    for bit in bits:
        masks += [m | (1 << bit) for m in masks]
    return masks


class Cube:
    def __init__(self):
        inner = lax.axis_size(AXES[1])
        self.count = lax.axis_size(AXES[0]) * inner
        self.bits = self.count.bit_length() - 1
        self.inner = inner.bit_length() - 1
        self.pairs = self.count >> (self.inner > 0)
        self.me = lax.axis_index(AXES)
        self.outer = list(range(self.inner, self.bits))
        self.rest = list(range(1, self.inner))
        self.turns = list(zip(self.outer, self.outer[::-1]))
        self.count_turns = 1 << len(self.outer)
        self.count_line = 1 << len(self.rest)

    def send(self, value, mask):
        return lax.ppermute(value, AXES, [(d, d ^ mask) for d in range(self.count)])

    def send_all(self, value, bits):
        return [self.send(value, mask) for mask in all_masks(bits)[1:]]

    def place(self, device, order):
        bits = [pair[order] for pair in self.turns] + self.rest[::-1]
        found = 0
        for bit in bits:
            found = found * 2 + ((device >> bit) & 1)
        return found

    def places(self):
        return jnp.stack([self.place(self.me, 0), self.place(self.me, 1), self.me & 1, self.me])

    def order(self):
        return sorted(range(self.count), key=lambda d: (d & (self.inner > 0), self.place(d, 0)))

    def turned(self, value):
        count = len(self.turns)
        shape = value.shape
        value = value.reshape((2,) * count + (-1,) + shape[1:])
        axes = tuple(range(count))[::-1] + tuple(range(count, value.ndim))
        return value.transpose(axes).reshape(shape)


class Gather:
    def __init__(self, cube, block, split):
        self.cube, self.split = cube, split
        self.value = block[None]

    def line(self, make=None):
        got = self.cube.send_all(self.value, self.cube.rest)
        if make is not None:
            got = after(got, make)
        self.value = jnp.concatenate([self.value, *got], axis=0)
        self.halves = self.split(self.value)
        self.turns = self.cube.turns[::-1]
        return self.value

    def turn(self, *others):
        if self.turns:
            bits = self.turns.pop(0)
            got = [self.cube.send(v, 1 << bit) for v, bit in zip(self.halves, bits)]
            if others:
                got = after(got, others)
            self.halves = [jnp.concatenate(pair, axis=0) for pair in zip(self.halves, got)]
        return self.halves


def after(value, others):
    return lax.optimization_barrier((value, others))[0]


def across(cube, value):
    return [cube.send(value, 1)] if cube.inner else []


def turn_sum_kernel(count, *refs):
    for half in range(count):
        keep, got = refs[2 * half], refs[2 * half + 1]
        first, second = refs[2 * count + 2 * half], refs[2 * count + 2 * half + 1]
        total = (keep[...].astype(f32) + got[...].astype(f32)).astype(bf16)
        middle = first.shape[0]
        first[...] = total[:middle]
        second[...] = total[middle:]


def join_kernel(lanes, *refs):
    low, low_got, late, late_got = refs[:4]
    for place, out in enumerate(refs[4:]):
        first = (low[place].astype(f32) + low_got[place].astype(f32)).astype(bf16)
        second = (late[place].astype(f32) + late_got[place].astype(f32)).astype(bf16)
        if lanes:
            out[:, : first.shape[1]] = first
            out[:, first.shape[1] :] = second
        else:
            out[: first.shape[0], :] = first
            out[first.shape[0] :, :] = second


class Scatter:
    def __init__(self, cube, keep, send, lanes):
        self.cube, self.keep, self.sent, self.lanes = cube, list(keep), list(send), lanes
        self.todo = list(cube.turns)
        self.got, self.total = [], None
        if self.todo:
            self.go()
        else:
            self.total = jnp.concatenate(self.keep, axis=2 if lanes else 1)[0].astype(f32)

    def go(self):
        bits = self.todo.pop(0)
        self.got = [self.cube.send(v, 1 << bit) for v, bit in zip(self.sent, bits)]
        self.last = not self.todo

    def step(self, *others):
        if self.total is not None:
            return []
        got = after(self.got, others) if others else self.got
        if self.sent is None:
            total = self.keep.astype(f32)
            for other in got:
                total = total + other.astype(f32)
            self.total = total
            return [total]
        pairs = [v for pair in zip(self.keep, got) for v in pair]
        small = all(v.shape[1] % 16 == 0 or v.shape[1] == 72 for v in self.keep)
        if not self.last:
            middle = self.keep[0].shape[0] // 2
            if small:
                shapes = [sds((middle,) + v.shape[1:], bf16) for v in self.keep for _ in range(2)]
                made = call(
                    functools.partial(turn_sum_kernel, 2), (1,), [whole_spec(v) for v in pairs],
                    [whole_spec(v) for v in shapes], shapes, 0, pairs,
                )
            else:
                made = []
                for keep, other in zip(self.keep, got):
                    total = (keep.astype(f32) + other.astype(f32)).astype(bf16)
                    made += [total[:middle], total[middle:]]
            self.keep, self.sent = list(made[0::2]), list(made[1::2])
            self.go()
            return self.sent
        masks = all_masks(self.cube.rest)
        if small:
            first, second = [v.shape[1:] for v in self.keep]
            shape = (first[0], first[1] + second[1]) if self.lanes else (first[0] + second[0], first[1])
            shapes = [sds(shape, bf16)] * len(masks)
            made = call(
                functools.partial(join_kernel, self.lanes), (1,), [whole_spec(v) for v in pairs],
                [whole_spec(v) for v in shapes], shapes, 0, pairs,
            )
        else:
            total = [
                (a.astype(f32) + b.astype(f32)).astype(bf16) for a, b in zip(self.keep, got)
            ]
            total = jnp.concatenate(total, axis=2 if self.lanes else 1)
            made = [total[i] for i in range(len(masks))]
        self.keep, sent = made[0], list(made[1:])
        self.got = [self.cube.send(v, mask) for v, mask in zip(sent, masks[1:])]
        self.sent = None
        return sent

    def result(self):
        while self.total is None:
            self.step()
        return self.total


def after(value, others):
    return lax.optimization_barrier((value, others))[0]


def across(cube, value):
    return [cube.send(value, 1)] if cube.inner else []


def set_down_kernel(cube, sizes, share, place_ref, pass_ref, *refs):
    sources, (wq_ref, wo_ref, norms_ref, emb_ref) = refs[:-4], refs[-4:]
    per = len(sources) // 2
    half = wq_ref.shape[2] // 2
    mid = sizes[0] + sizes[1]
    extra = sources[0].shape[1] - mid
    row = lax.broadcasted_iota(jnp.int32, (extra, 1), 0)
    picked = (row < 8) | (row == 8 + pass_ref[0])
    empty = jnp.zeros((extra, half), f32)
    small = jnp.zeros((extra, 2 * half), f32)
    for device in range(cube.count):
        for order in range(2):
            at = cube.place(device, order) ^ place_ref[order]
            block = sources[order * per][at]
            if per > 1:
                own = ((device & 1) ^ place_ref[2]) == 0
                block = jnp.where(own, block, sources[order * per + 1][at])
            block = block.astype(f32)
            lanes = slice(order * half, (order + 1) * half)
            wq_ref[device, :, lanes] = block[: sizes[0]].astype(bf16)
            wo_ref[device, :, lanes] = block[sizes[0] : mid].astype(bf16)
            if order * half < share:
                line = [jnp.where(picked, block[mid:], 0.0), empty]
                line = jnp.concatenate(line[::-1] if order else line, axis=1)
                small = small + (pltpu.roll(line, device * share, 1) if device else line)
    norms_ref[...] = small[:8]
    emb_ref[...] = jnp.sum(small[8:], axis=0, keepdims=True)


def set_down(cube, place, pass_index, sources, sizes, share):
    width = 2 * sources[0].shape[2]
    shapes = [(cube.count, n, width) for n in sizes]
    wq, wo, norms, emb = call(
        functools.partial(set_down_kernel, cube, sizes, share), (1,),
        [pl.BlockSpec(memory_space=pltpu.SMEM)] * 2 + [whole_spec(a) for a in sources],
        [pl.BlockSpec(n, lambda i: (0, 0, 0)) for n in shapes]
        + [pl.BlockSpec((n, width), lambda i: (0, 0)) for n in (8, 1)],
        [sds(n, bf16) for n in shapes] + [sds((n, width), f32) for n in (8, 1)], 0,
        [place, pass_index, *sources],
    )
    return wq.reshape(-1, width), wo.reshape(-1, width), norms, emb


def body(
    tokens, row_lengths, live_mask, pass_index,
    w_qkv, w_out, w_up, w_down, norm_gains, norm_shifts, pass_table, cotangent,
):
    _, seq, width = tokens.shape
    cube = Cube()
    place = cube.places()
    ff = w_up.shape[1] * cube.count
    block = min(256, seq)
    grid = (seq // block,)
    passes = pass_table.shape[0]

    def split_lanes(v):
        half = v.shape[2] // 2
        return [v[:, :, :half], v[:, :, half:]]

    high = w_up.shape[1]
    share = w_out.shape[1]

    def wide_rows(v):
        return jnp.pad(v, ((0, -v.shape[0] % 8), (0, width - v.shape[1])))

    packed = jnp.concatenate([w_up.T, w_down], axis=0)
    packed = lax.all_gather(packed, AXES, axis=0, tiled=False)

    gains_shifts = wide_rows(jnp.concatenate([norm_gains, norm_shifts], axis=0))
    early = [w_qkv.T, w_out.T, gains_shifts, wide_rows(pass_table)]
    part_q = Gather(cube, jnp.concatenate(early, axis=0), split_lanes)
    part_q.line()
    for _ in cube.turns:
        part_q.turn()
    low, late = part_q.halves
    sources = [low, *across(cube, low), late, *across(cube, late)]
    sizes = (w_qkv.shape[1], w_out.shape[1])
    wq, wo, norms, emb = set_down(cube, place, pass_index, sources, sizes, share)

    positions = jnp.arange(seq, dtype=jnp.int32)
    inside = positions < row_lengths[0]
    live = jnp.where(inside[None, :] & (live_mask[:, 0] > 0), 1.0, 0.0).astype(f32)
    live_cols = [live[0][:, None], live[1][:, None]]
    live_rows = [live[0][None, :], live[1][None, :]]

    x = tokens[0]
    given = cotangent[0]
    rows_w = rows_spec(block, width)
    rows_f = rows_spec(block, ff)
    rows_q = rows_spec(block, 3 * width)
    rows_1 = rows_spec(block, 1)
    rows_3 = pl.BlockSpec((3, block, width), lambda i: (0, i, 0))
    sums_spec = pl.BlockSpec((8, width), lambda i: (0, 0))
    wide = sds((seq, width), f32)
    thin = sds((seq, width), bf16)
    tall = sds((seq, ff), bf16)
    triple = sds((seq, 3 * width), bf16)
    sums_shape = sds((8, width), f32)
    unit = 2 * seq * width

    mixed0, xhat0 = call(
        first_kernel, grid,
        [rows_w, whole_spec(norms), whole_spec(wq)],
        [rows_q, rows_w], [triple, thin], unit * 3 * width, [x, norms, wq],
    )
    pairs = width // LANES
    third = pairs // 3 if pairs % 3 == 0 else pairs
    att0, logs0 = attend(mixed0, live_cols[0], live_rows[0])
    packed = after(packed, att0)
    order, share = cube.order(), high
    if cube.count == 1 or 768 % high or high % 16:
        blocks = [packed[:, at : at + high] for at in (0, high)]
        turned = [
            jnp.take(v, jnp.asarray(order, jnp.int32) ^ cube.me, axis=0).reshape(ff, width)
            for v in blocks
        ]
        packed, share = jnp.concatenate(turned, axis=0)[None], ff
    smem = pl.BlockSpec(memory_space=pltpu.SMEM)
    hidden0, second0, act0, slope0, later, mixed1, xhat1 = call(
        functools.partial(middle_kernel, order, share), grid,
        [smem, whole_spec(packed), rows_w, rows_w, rows_1]
        + [whole_spec(a) for a in (norms, emb, wo, wq)],
        [rows_w, rows_w, rows_f, rows_f, rows_w, rows_q, rows_w],
        [wide, thin, tall, tall, wide, triple, thin],
        unit * (4 * width + 2 * ff),
        [place, packed, att0, x, live_cols[0], norms, emb, wo, wq],
    )
    att1, logs1 = attend(mixed1, live_cols[1], live_rows[1])
    result, second1, act1, drop1, lift1, branch1, hgrad1, agrad1, sums1 = call(
        functools.partial(turn_kernel, order, share), grid,
        [smem, whole_spec(packed), rows_w, rows_w, rows_1, whole_spec(norms), rows_w]
        + [whole_spec(wo)],
        [rows_w, rows_w, rows_f, rows_w, rows_f, rows_w, rows_w, rows_w, sums_spec],
        [thin, thin, tall, thin, tall, thin, wide, thin, sums_shape],
        unit * (2 * width + 4 * ff),
        [place, packed, att1, later, live_cols[1], norms, given, wo],
    )
    mgrad1 = attend_back(mixed1, agrad1, att1, logs1, live_cols[1])
    drop0, lift0, branch0, hgrad0, agrad0, sums0 = call(
        functools.partial(back_kernel, order, share), grid,
        [smem, whole_spec(packed), rows_3, rows_w, rows_w, whole_spec(norms), rows_1, rows_w, rows_f]
        + [whole_spec(a) for a in (wq, wo)],
        [rows_w, rows_f, rows_w, rows_w, rows_w, sums_spec],
        [thin, tall, thin, wide, thin, sums_shape],
        unit * (4 * width + 2 * ff),
        [place, packed, mgrad1, later, hgrad1, norms, live_cols[0], hidden0, slope0, wq, wo],
    )
    chips = cube.pairs * high
    fast = len(cube.turns) == 2 and (cube.count_line * high) % LANES == 0 and high % 32 == 0
    out_own, out_other = out_grads(cube, place, branch0, branch1, att0, att1)
    up_args = (lift0, lift1, second0, second1)
    down_args = (act0, act1, drop0, drop1)

    def split_rows(v):
        start = high // 2
        return [v[:, :start], cube.turned(v[:, start:])]

    def turn_halves(halves):
        middle = cube.pairs // 2
        return [v[:middle] for v in halves], [v[middle:] for v in halves]

    if fast:
        up_other = other_grads(cube, high, *up_args, extra=[out_other])
        (up_got,) = across(cube, up_other)
        down_other = other_grads(cube, high, *down_args, hold=[up_other])
        (down_got,) = across(cube, down_other)
        made = own_grads(cube, high, *up_args, up_got, extra=[out_own], hold=[down_other])
        up_out = Scatter(cube, made[0::2], made[1::2], False)
        made = own_grads(cube, high, *down_args, down_got, hold=made)
        down = Scatter(cube, made[0::2], made[1::2], False)
    else:
        found = []
        for args, more, more_other in ((up_args, out_own, out_other), (down_args, None, None)):
            own = pair_grads(*args, 0, chips)
            if cube.inner:
                got = across(cube, pair_grads(*args, chips, chips))[0]
                own = (own.astype(f32) + got.astype(f32)).astype(bf16)
                if more is not None:
                    got = across(cube, more_other)[0]
                    more = (more.astype(f32) + got.astype(f32)).astype(bf16)
            halves = split_rows(own.reshape(cube.pairs, high, width))
            if more is not None:
                halves[0] = jnp.concatenate([halves[0], more], axis=1)
            keep, send = turn_halves(halves) if cube.turns else (halves, [])
            found.append(Scatter(cube, keep, send, False))
        up_out, down = found
        made = send
    hold = made
    groups = []
    for first in range(0, pairs, third):
        group = attend_back(mixed0, agrad0, att0, logs0, live_cols[0], first, third, hold)
        groups.append(group)
        hold = [group]
        if first == 0:
            hold = hold + up_out.step(group)
        elif first == third:
            hold = hold + down.step(group) + up_out.step(group)
        else:
            hold = hold + down.step(group) + up_out.step(group)
    own, other, small = qkv_grads(
        cube, passes, place, pass_index, groups, mgrad1, xhat0, xhat1,
        [wq, norms, sums0, sums1], hold,
    )
    got = across(cube, other)
    if got:
        own = (own.astype(f32) + got[0].astype(f32)).astype(bf16)
    halves = split_lanes(own)
    keep, send = turn_halves(halves) if cube.turns else (halves, [])
    qkv = Scatter(cube, keep, send, True)
    hold = send
    specs_g = [
        pl.BlockSpec((3, block, a.shape[2]), lambda i: (0, i, 0)) for a in groups
    ]
    input_grad = call(
        functools.partial(last_kernel, len(groups)), grid,
        specs_g + [rows_w, rows_w, whole_spec(norms), whole_spec(wq)],
        [rows_w], [wide], unit * 3 * width,
        [*groups, x, hgrad0, norms, wq],
        hold=hold,
    )[0]
    qkv.step(input_grad)
    down = down.result()
    up_out = up_out.result()
    qkv = qkv.result()
    share = w_out.shape[1]
    count = w_qkv.shape[1]
    if cube.count > 1:
        half = width // 2
        small = jnp.concatenate([qkv[count:, :share], qkv[count:, half : half + share]], axis=0)
    qkv = qkv[:count].T
    low_end = high // 2
    out_end = low_end + share
    up = jnp.concatenate([up_out[:low_end], up_out[out_end:]], axis=0).T
    out = up_out[low_end:out_end].T
    return (
        result[None], input_grad[None], qkv, out, up, down,
        small[:2], small[2], small[3], small[4 : 4 + passes],
    )


def solution(mesh):
    placed = (
        P(AXES, None, None),
        P(AXES),
        P(None, AXES, None),
        P(AXES),
        P(None, AXES),
        P(None, AXES),
        P(None, AXES),
        P(AXES, None),
        P(None, AXES),
        P(None, AXES),
        P(None, AXES),
        P(AXES, None, None),
    )
    return jax.shard_map(
        body,
        mesh=mesh,
        in_specs=placed,
        out_specs=(
            P(AXES, None, None),
            P(AXES, None, None),
            P(None, AXES),
            P(None, AXES),
            P(None, AXES),
            P(AXES, None),
            P(None, AXES),
            P(AXES),
            P(AXES),
            P(None, AXES),
        ),
        check_vma=False,
    )
```

```python
import functools

import jax
import jax.numpy as jnp
from jax import lax
from jax.experimental import pallas as pl
from jax.experimental.pallas import tpu as pltpu
from jax.sharding import PartitionSpec as P

HEAD = 64
LANES = 128
AXES = ("dp", "fsdp")
bf16 = jnp.bfloat16
f32 = jnp.float32

norm_epsilon = 1e-05
masked_score = -1000000000.0
curve_one = 0.7978845608028654
curve_three = 0.7978845608028654 * 0.044715

MIB = 1024 * 1024
VMEM_LIMIT = 52
LATE_LIMIT = 47


def dot_nn(left, right):
    return lax.dot_general(left, right, (((1,), (0,)), ((), ())), preferred_element_type=f32)


def dot_nt(left, right):
    return lax.dot_general(left, right, (((1,), (1,)), ((), ())), preferred_element_type=f32)


def dot_tn(left, right):
    return lax.dot_general(left, right, (((0,), (0,)), ((), ())), preferred_element_type=f32)


def normalize(values):
    center = jnp.mean(values, axis=-1, keepdims=True)
    centered = values - center
    spread = jnp.mean(centered * centered, axis=-1, keepdims=True)
    scale = lax.rsqrt(spread + norm_epsilon)
    return centered * scale, scale


def norm_back(grad, gain, xhat, scale):
    gained = grad * gain
    first = jnp.mean(gained, axis=-1, keepdims=True)
    second = jnp.mean(gained * xhat, axis=-1, keepdims=True)
    return scale * (gained - first - xhat * second)


def gelu_pair(lifted):
    square = lifted * lifted
    cubic = curve_three * square
    half = 0.5 + 0.5 * jnp.tanh(lifted * (curve_one + cubic))
    value = lifted * half
    slope = half + value * ((1.0 - half) * (2.0 * curve_one + 6.0 * cubic))
    return value, slope


def call(
    kernel, grid, in_specs, out_specs, out_shape, flops, args, scratch=(), hold=(), room=VMEM_LIMIT
):
    moved = sum(a.size * a.dtype.itemsize for a in args)
    moved += sum(o.size * o.dtype.itemsize for o in out_shape)
    given, held = len(args), len(hold)

    def run(*refs):
        kernel(*refs[:given], *refs[given + held :])

    return pl.pallas_call(
        run,
        grid=grid,
        in_specs=list(in_specs) + [pl.BlockSpec(memory_space=pl.ANY)] * held,
        out_specs=out_specs,
        out_shape=out_shape,
        scratch_shapes=list(scratch),
        compiler_params=pltpu.CompilerParams(
            dimension_semantics=("arbitrary",) * len(grid), vmem_limit_bytes=room * MIB
        ),
        cost_estimate=pl.CostEstimate(
            flops=flops, bytes_accessed=moved, transcendentals=0
        ),
    )(*args, *hold)


def rows_spec(block_rows, width):
    return pl.BlockSpec((block_rows, width), lambda i: (i, 0))


def whole_spec(array):
    zeros = (0,) * len(array.shape)
    return pl.BlockSpec(array.shape, lambda i: zeros, pipeline_mode=pl.Buffered(1))


def sds(shape, dtype):
    return jax.ShapeDtypeStruct(shape, dtype)


def head_part(x, gain, shift, w_qkv, mixed_ref, xhat_ref):
    xhat, _ = normalize(x)
    normed = (xhat * gain + shift).astype(bf16)
    xhat_ref[...] = xhat.astype(bf16)
    mixed_ref[...] = dot_nt(normed, w_qkv[...]).astype(bf16)


def first_kernel(x_ref, norms_ref, wq_ref, mixed_ref, xhat_ref):
    head_part(
        x_ref[...].astype(f32), norms_ref[0:1, :], norms_ref[2:3, :], wq_ref, mixed_ref, xhat_ref
    )


def ff_chunks(order, place_ref, packed_ref, share):
    found = []
    if share >= 768:
        for at in range(0, share, 768):
            up, down = pl.ds(at, 768), pl.ds(share + at, 768)
            found.append((lambda r=up: packed_ref[0, r, :], lambda r=down: packed_ref[0, r, :], pl.ds(at, 768)))
        return found
    per = 768 // share
    for first in range(0, len(order), per):

        def rows(at, first=first):
            return jnp.concatenate(
                [
                    packed_ref[place_ref[3] ^ mask, pl.ds(at, share), :]
                    for mask in order[first : first + per]
                ],
                axis=0,
            )

        found.append(
            (functools.partial(rows, 0), functools.partial(rows, share), pl.ds(first * share, 768))
        )
    return found


def middle_kernel(order, share, place_ref, packed_ref, *refs):
    chunks = ff_chunks(order, place_ref, packed_ref, share)
    atts, refs = refs[:-13], refs[-13:]
    (
        x_ref, live_ref, norms_ref, emb_ref, wo_ref, wq_ref,
        hidden_ref, second_ref, act_ref, slope_ref, later_ref, mixed_ref, xhat_ref,
    ) = refs
    live = live_ref[...]
    branch, at = 0.0, 0
    for ref in atts:
        branch = branch + dot_nt(ref[...], wo_ref[:, at : at + ref.shape[1]])
        at += ref.shape[1]
    hidden = x_ref[...].astype(f32) + live * branch
    hidden_ref[...] = hidden
    xhat, _ = normalize(hidden)
    second = (xhat * norms_ref[1:2, :] + norms_ref[3:4, :]).astype(bf16)
    second_ref[...] = second
    total = jnp.zeros_like(hidden)
    for up, down, to in chunks:
        value, slope = gelu_pair(dot_nt(second, up()))
        value = value.astype(bf16)
        act_ref[:, to] = value
        slope_ref[:, to] = slope.astype(bf16)
        total = total + dot_nn(value, down())
    later = hidden + live * total + emb_ref[...]
    later_ref[...] = later
    head_part(later, norms_ref[0:1, :], norms_ref[2:3, :], wq_ref, mixed_ref, xhat_ref)


def mlp_back_tail(
    grad, live, hidden, second_grad, norms_ref, wo_ref, branch_ref, hgrad_ref, agrad_ref
):
    xhat, scale = normalize(hidden)
    hgrad = grad + norm_back(second_grad, norms_ref[1:2, :], xhat, scale)
    hgrad_ref[...] = hgrad
    branch = (live * hgrad).astype(bf16)
    branch_ref[...] = branch
    agrad_ref[...] = dot_nn(branch, wo_ref[...]).astype(bf16)
    gain_sum = jnp.sum(second_grad * xhat, axis=0, keepdims=True)
    shift_sum = jnp.sum(second_grad, axis=0, keepdims=True)
    return gain_sum, shift_sum


def add_sums(sums_ref, sums):
    @pl.when(pl.program_id(0) == 0)
    def _():
        sums_ref[...] = jnp.zeros_like(sums_ref)

    for place, value in enumerate(sums):
        sums_ref[place : place + 1, :] += value


def turn_kernel(order, share, place_ref, packed_ref, *refs):
    chunks = ff_chunks(order, place_ref, packed_ref, share)
    (
        att_ref, x_ref, live_ref, norms_ref, grad_ref, wo_ref,
        out_ref, second_ref, act_ref, drop_ref, lift_ref, branch_ref, hgrad_ref, agrad_ref, sums_ref,
    ) = refs
    live = live_ref[...]
    hidden = x_ref[...] + live * dot_nt(att_ref[...], wo_ref[...])
    xhat, _ = normalize(hidden)
    second = (xhat * norms_ref[1:2, :] + norms_ref[3:4, :]).astype(bf16)
    second_ref[...] = second
    grad = grad_ref[...]
    drop = (live * grad).astype(bf16)
    drop_ref[...] = drop
    total = jnp.zeros_like(hidden)
    second_grad = jnp.zeros_like(hidden)
    for up, down, to in chunks:
        up, down = up(), down()
        value, slope = gelu_pair(dot_nt(second, up))
        value = value.astype(bf16)
        act_ref[:, to] = value
        total = total + dot_nn(value, down)
        lift = (dot_nt(drop, down) * slope).astype(bf16)
        lift_ref[:, to] = lift
        second_grad = second_grad + dot_nn(lift, up)
    out_ref[...] = (hidden + live * total).astype(bf16)
    sums = mlp_back_tail(
        grad, live, hidden, second_grad, norms_ref, wo_ref, branch_ref, hgrad_ref, agrad_ref
    )
    add_sums(sums_ref, sums)


def head_back(mixed_grad_refs, wq_ref, x, hgrad, norms_ref):
    width = x.shape[1]
    normed_grad = jnp.zeros_like(x)
    for part in range(3):
        at = part * width
        for ref in mixed_grad_refs:
            normed_grad += dot_nn(ref[part], wq_ref[at : at + ref.shape[2], :])
            at += ref.shape[2]
    xhat, scale = normalize(x)
    return hgrad + norm_back(normed_grad, norms_ref[0:1, :], xhat, scale)


def back_kernel(order, share, place_ref, packed_ref, *refs):
    chunks = ff_chunks(order, place_ref, packed_ref, share)
    (
        mgrad_ref, later_ref, hgrad1_ref, norms_ref, live_ref, hidden_ref, slope_ref, wq_ref, wo_ref,
        drop_ref, lift_ref, branch_ref, hgrad_ref, agrad_ref, sums_ref,
    ) = refs
    grad = head_back([mgrad_ref], wq_ref, later_ref[...], hgrad1_ref[...], norms_ref)
    table_sum = jnp.sum(grad, axis=0, keepdims=True)
    live = live_ref[...]
    drop = (live * grad).astype(bf16)
    drop_ref[...] = drop
    second_grad = jnp.zeros_like(grad)
    for up, down, to in chunks:
        lift = (dot_nt(drop, down()) * slope_ref[:, to].astype(f32)).astype(bf16)
        lift_ref[:, to] = lift
        second_grad = second_grad + dot_nn(lift, up())
    sums = mlp_back_tail(
        grad, live, hidden_ref[...], second_grad, norms_ref, wo_ref, branch_ref, hgrad_ref, agrad_ref
    )
    add_sums(sums_ref, sums + (table_sum,))


def last_kernel(groups, *refs):
    mgrad_refs, (x_ref, hgrad_ref, norms_ref, wq_ref, out_ref) = refs[:groups], refs[groups:]
    out_ref[...] = head_back(
        mgrad_refs, wq_ref, x_ref[...].astype(f32), hgrad_ref[...], norms_ref
    )


def both_layers(left0, left1, right0, right1):
    return dot_tn(left0[...], right0[...]) + dot_tn(left1[...], right1[...])


def pair_grad_kernel(left0, left1, right0, right1, out_ref):
    out_ref[...] = both_layers(left0, left1, right0, right1).astype(bf16)


def pair_grads(left0, left1, right0, right1, start, size, hold=()):
    tokens = left0.shape[0]
    width = right0.shape[1]
    step = 384 if size % 384 == 0 else size
    first = start // step
    cols = pl.BlockSpec((tokens, step), lambda i: (0, first + i))
    return call(
        pair_grad_kernel,
        (size // step,),
        [cols] * 2 + [whole_spec(right0)] * 2,
        [rows_spec(step, width)],
        [sds((size, width), bf16)],
        4 * tokens * size * width,
        [left0, left1, right0, right1],
        hold=hold, room=LATE_LIMIT,
    )[0]


def blocks_spec(shape, index):
    return pl.BlockSpec(shape, lambda i: (index(i), 0, 0))


def other_grad_kernel(high, left0, left1, right0, right1, *refs):
    extra, out_ref = refs[:-1], refs[-1]
    total = both_layers(left0, left1, right0, right1).astype(bf16)
    for place in range(out_ref.shape[0]):
        out_ref[place, :high, :] = total[place * high : (place + 1) * high]
        for ref in extra:
            out_ref[place, high:, :] = ref[place]


def other_grads(cube, high, left0, left1, right0, right1, extra=(), hold=()):
    tokens = left0.shape[0]
    width = right0.shape[1]
    lines, turns = cube.count_line, cube.count_turns
    first = turns
    cols = pl.BlockSpec((tokens, lines * high), lambda i: (0, first + i))
    rows = high + sum(a.shape[1] for a in extra)
    return call(
        functools.partial(other_grad_kernel, high),
        (turns,),
        [cols] * 2
        + [whole_spec(right0)] * 2
        + [blocks_spec((lines,) + a.shape[1:], lambda i: i) for a in extra],
        [blocks_spec((lines, rows, width), lambda i: i)],
        [sds((cube.pairs, rows, width), bf16)],
        4 * tokens * cube.pairs * high * width,
        [left0, left1, right0, right1, *extra],
        hold=hold, room=LATE_LIMIT,
    )[0]


def own_grad_kernel(high, left0, left1, right0, right1, got, *refs):
    extra, (low_keep, low_send, late_keep, late_send) = refs[:-4], refs[-4:]
    middle = high // 2
    half = pl.num_programs(0) // 2
    step = pl.program_id(0)
    total = both_layers(left0, left1, right0, right1)

    def low_part(ref):
        for place in range(ref.shape[0]):
            at = place * high
            ref[place, :middle, :] = (
                total[at : at + middle] + got[place, :middle, :].astype(f32)
            ).astype(bf16)
            for more in extra:
                ref[place, middle:, :] = (
                    more[place].astype(f32) + got[place, high:, :].astype(f32)
                ).astype(bf16)

    def late_part(ref):
        for place in range(ref.shape[0]):
            at = place * high
            ref[place] = (
                total[at + middle : at + high] + got[place, middle:high, :].astype(f32)
            ).astype(bf16)

    @pl.when(step < half)
    def _():
        low_part(low_keep)

    @pl.when(step >= half)
    def _():
        low_part(low_send)

    @pl.when(step % 2 == 0)
    def _():
        late_part(late_keep)

    @pl.when(step % 2 == 1)
    def _():
        late_part(late_send)


def own_grads(cube, high, left0, left1, right0, right1, got, extra=(), hold=()):
    tokens = left0.shape[0]
    width = right0.shape[1]
    lines, turns = cube.count_line, cube.count_turns
    half = turns // 2
    cols = pl.BlockSpec((tokens, lines * high), lambda i: (0, i))
    low = high // 2 + sum(a.shape[1] for a in extra)
    late = high - high // 2

    def turned(i):
        found = 0
        for bit in range(1, turns.bit_length() - 1):
            found = found + (((i >> bit) & 1) << (turns.bit_length() - 2 - bit))
        return found

    def first_keep(i):
        return jnp.minimum(i, half - 1)

    def first_send(i):
        return jnp.maximum(i - half, 0)

    return call(
        functools.partial(own_grad_kernel, high),
        (turns,),
        [cols] * 2
        + [whole_spec(right0)] * 2
        + [blocks_spec((lines,) + a.shape[1:], lambda i: i) for a in (got, *extra)],
        [
            blocks_spec((lines, low, width), first_keep),
            blocks_spec((lines, low, width), first_send),
            blocks_spec((lines, late, width), turned),
            blocks_spec((lines, late, width), turned),
        ],
        [sds((cube.pairs // 2, n, width), bf16) for n in (low, low, late, late)],
        4 * tokens * cube.pairs * high * width,
        [left0, left1, right0, right1, got, *extra],
        hold=hold, room=LATE_LIMIT,
    )


def place_blocks(cube, place_ref, total_ref, own_ref, other_ref):
    rows = own_ref.shape[1]
    for chip in range(own_ref.shape[0]):
        if cube.inner == 0:
            own_ref[0] = total_ref[...].astype(bf16)
            continue
        even = total_ref[pl.ds(2 * chip * rows, rows), :].astype(bf16)
        odd = total_ref[pl.ds((2 * chip + 1) * rows, rows), :].astype(bf16)
        first = place_ref[2] == 0
        at = cube.place(2 * chip, 0) ^ place_ref[0]
        own_ref[at] = jnp.where(first, even, odd)
        other_ref[at] = jnp.where(first, odd, even)


def out_grad_kernel(cube, place_ref, left0, left1, right0, right1, own_ref, other_ref, total_ref):
    total_ref[...] = both_layers(left0, left1, right0, right1)
    place_blocks(cube, place_ref, total_ref, own_ref, other_ref)


def block_shapes(cube, rows, width):
    shape = (cube.pairs, rows, width)
    return [sds(shape, bf16)] * 2, [pl.BlockSpec(shape, lambda i: (0, 0, 0))] * 2


def out_grads(cube, place, left0, left1, right0, right1, hold=()):
    tokens, high = left0.shape
    width = right1.shape[1]
    shapes, specs = block_shapes(cube, high // cube.count, width)
    args = [left0, left1, right0, right1]
    return call(
        functools.partial(out_grad_kernel, cube),
        (1,),
        [pl.BlockSpec(memory_space=pltpu.SMEM)] + [whole_spec(a) for a in args],
        specs,
        shapes,
        4 * tokens * high * width,
        [place, *args],
        scratch=[pltpu.VMEM((high, width), f32)],
        hold=hold, room=LATE_LIMIT,
    )


def qkv_grad_kernel(cube, groups, passes, place_ref, pass_ref, *refs):
    lefts0, refs = refs[:groups], refs[groups:]
    left1, right0, right1, wq_ref, sums0_ref, sums1_ref, own_ref, other_ref = refs[:8]
    small_ref, total_ref, count_ref = refs[8:]
    part = pl.program_id(0)
    high = left1.shape[2]
    width = right0.shape[1]
    row = lax.broadcasted_iota(jnp.int32, (8, 1), 0)

    @pl.when(part == 0)
    def _():
        small_ref[...] = jnp.zeros_like(small_ref)
        small_ref[1:2, :] = sums0_ref[0:1, :] + sums1_ref[0:1, :]
        small_ref[3:4, :] = sums0_ref[1:2, :] + sums1_ref[1:2, :]
        for index in range(passes):
            small_ref[4 + index : 5 + index, :] = jnp.where(
                pass_ref[0] == index, sums0_ref[2:3, :], 0.0
            )

    at = 0
    gain_sum = jnp.zeros((1, width), f32)
    shift_sum = jnp.zeros((1, width), f32)
    for left0 in lefts0:
        to = pl.ds(at, left0.shape[2])
        rows = pl.ds(pl.multiple_of(part * high + at, 8), left0.shape[2])
        total = dot_tn(left0[0], right0[...]) + dot_tn(left1[0, :, to], right1[...])
        total_ref[rows, :] = total
        sums = jnp.sum(left0[0].astype(f32) + left1[0, :, to].astype(f32), axis=0, keepdims=True)
        count_ref[pl.ds(part, 1), to] = sums
        terms = split_three(jnp.broadcast_to(sums, (8, left0.shape[2])))
        three = jnp.where(row == 0, terms[0], jnp.where(row == 1, terms[1], terms[2]))
        three = jnp.where(row < 3, three, jnp.zeros_like(three))
        weights = wq_ref[to, :]
        gain_sum += jnp.sum(total * weights.astype(f32), axis=0, keepdims=True)
        shift_sum += jnp.sum(dot_nn(three, weights), axis=0, keepdims=True)
        at += left0.shape[2]
    small_ref[0:1, :] += gain_sum
    small_ref[2:3, :] += shift_sum

    @pl.when(part == pl.num_programs(0) - 1)
    def _():
        extra = 16
        rows = own_ref.shape[1] - extra
        share = width // cube.count
        half = width // 2
        small = small_ref[...]
        counts = jnp.concatenate([count_ref[p : p + 1, :] for p in range(3)], axis=1)
        counts = jnp.broadcast_to(counts, (8, counts.shape[1]))
        for chip in range(cube.pairs):
            found = []
            for device in range(2 * chip, 2 * chip + 1 + (cube.inner > 0)):
                block = total_ref[pl.ds(device * rows, rows), :]
                line = pltpu.roll(small, width - device * share, 1) if device else small
                line = jnp.concatenate([line[:8, :half], line[8:, :half]], axis=1)
                own = counts
                if device:
                    own = pltpu.roll(counts, counts.shape[1] - device * rows, 1)
                found.append(jnp.concatenate([block, line, own[:, :width]], axis=0).astype(bf16))
            if cube.inner == 0:
                own_ref[0] = found[0]
                continue
            first = place_ref[2] == 0
            own = jnp.where(first, found[0], found[1])
            other = jnp.where(first, found[1], found[0])
            for order in range(2):
                lanes = slice(order * half, (order + 1) * half)
                at = cube.place(2 * chip, order) ^ place_ref[order]
                own_ref[at, :, lanes] = own[:, lanes]
                other_ref[at, :, lanes] = other[:, lanes]


def qkv_grads(cube, passes, place, pass_index, lefts0, left1, right0, right1, kept, hold=()):
    parts, tokens, high = left1.shape
    width = right0.shape[1]
    specs = [
        pl.BlockSpec((1, tokens, a.shape[2]), lambda i: (i, 0, 0)) for a in (*lefts0, left1)
    ]
    shapes, out_specs = block_shapes(cube, parts * high // cube.count + 16, width)
    return call(
        functools.partial(qkv_grad_kernel, cube, len(lefts0), passes),
        (parts,),
        [pl.BlockSpec(memory_space=pltpu.SMEM)] * 2
        + specs
        + [whole_spec(a) for a in (right0, right1)]
        + [rows_spec(high, width)]
        + [whole_spec(a) for a in kept[1:]],
        out_specs + [pl.BlockSpec((16, width), lambda i: (0, 0))],
        shapes + [sds((16, width), f32)],
        4 * tokens * parts * high * width,
        [place, pass_index, *lefts0, left1, right0, right1, *kept],
        scratch=[pltpu.VMEM((parts * high, width), f32), pltpu.VMEM((8, high), f32)],
        hold=hold,
        room=LATE_LIMIT,
    )


def lane_index(shape):
    return lax.broadcasted_iota(jnp.int32, shape, len(shape) - 1)


def split_three(values):
    high = values.astype(bf16)
    rest = values - high.astype(f32)
    middle = rest.astype(bf16)
    low = (rest - middle.astype(f32)).astype(bf16)
    return high, middle, low


def own_lanes(lane, head):
    return (lane < HEAD) if head == 0 else (lane >= HEAD)


def attend_kernel(
    block, q_ref, k_ref, v_ref, live_col_ref, live_row_ref, out_ref, logs_ref, mask_ref
):
    seq = q_ref.shape[0]
    count = seq // block

    @pl.when(pl.program_id(0) == 0)
    def _():
        query = lax.broadcasted_iota(jnp.int32, (block, block), 0)
        key = lax.broadcasted_iota(jnp.int32, (block, block), 1)
        for i in range(count):
            alive = live_row_ref[:, i * block : (i + 1) * block] > 0.5
            visible = (key <= query) & (alive | (key == query))
            mask_ref[i] = jnp.where(visible, 0.0, masked_score)

    lane = lane_index((seq, LANES))
    q = q_ref[...] * 0.125
    k = k_ref[...]
    v = v_ref[...]
    bias = ((live_col_ref[...] - 1.0) * 1e9).astype(bf16)
    zero = jnp.zeros((seq, LANES), bf16)
    one = jnp.ones((seq, LANES), bf16)
    parts = []
    for head in range(2):
        mine = own_lanes(lane, head)
        spare = (1 - head) * HEAD
        parts.append(
            (
                jnp.where(mine, q, zero),
                jnp.where(mine, q, jnp.where(lane == spare, one, zero)),
                jnp.where(mine, k, jnp.where(lane == spare, bias, zero)),
                jnp.where(mine, v, one),
            )
        )
    low = lane_index((block, LANES)) < HEAD

    def score(i, head):
        at, before = slice(i * block, (i + 1) * block), slice(0, i * block)
        q_plain, q_bias, k_bias, _ = parts[head]
        diag = dot_nt(q_plain[at], k[at]) + mask_ref[i]
        return diag, dot_nt(q_bias[at], k_bias[before]) if i > 0 else None

    def soften(diag, off):
        top = jnp.max(diag, axis=-1, keepdims=True)
        if off is None:
            return top, jnp.exp(diag - top).astype(bf16), None
        top = jnp.maximum(top, jnp.max(off, axis=-1, keepdims=True))
        return top, jnp.exp(diag - top).astype(bf16), jnp.exp(off - top).astype(bf16)

    def finish(i, head, top, diag, off):
        at, before = slice(i * block, (i + 1) * block), slice(0, i * block)
        v_ones = parts[head][3]
        total = dot_nn(diag, v_ones[at])
        if i > 0:
            total += dot_nn(off, v_ones[before])
        spare = (1 - head) * HEAD
        weight = total[:, spare : spare + 1]
        found.append((total * (1.0 / weight), top + jnp.log(weight)))
        if head == 1:
            (out0, log0), (out1, log1) = found[-2:]
            out_ref[at, :] = jnp.where(low, out0, out1).astype(bf16)
            logs_ref[at, :] = jnp.where(low, log0, log1)

    found = []
    steps = [(i, head) for i in range(count) for head in range(2)]
    ahead, behind = score(*steps[0]), None
    for place, step in enumerate(steps):
        scored = ahead
        if place + 1 < len(steps):
            ahead = score(*steps[place + 1])
        softened = soften(*scored)
        if behind is not None:
            finish(*steps[place - 1], *behind)
        behind = softened
    finish(*steps[-1], *behind)


def attend(mixed, live_col, live_row, first=0, count=None, hold=(), block=256):
    seq, triple = mixed.shape
    pairs = triple // 3 // LANES
    count = pairs if count is None else count
    width = count * LANES
    block = min(block, seq)

    def cols(offset):
        return pl.BlockSpec((seq, LANES), lambda h: (0, offset + h))

    return call(
        functools.partial(attend_kernel, block),
        (count,),
        [cols(first), cols(first + pairs), cols(first + 2 * pairs), whole_spec(live_col), whole_spec(live_row)],
        [cols(0), cols(0)],
        [sds((seq, width), bf16), sds((seq, width), f32)],
        4 * seq * seq * width,
        [mixed, mixed, mixed, live_col, live_row],
        scratch=[pltpu.VMEM((seq // block, block, block), f32)],
        hold=hold, room=VMEM_LIMIT,
    )


def attend_back_kernel(
    block, q_ref, k_ref, v_ref, grad_ref, att_ref, logs_ref, live_col_ref, out_ref,
    mask_ref, dk_ref, dv_ref,
):
    seq = q_ref.shape[0]
    count = seq // block

    @pl.when(pl.program_id(0) == 0)
    def _():
        key = lax.broadcasted_iota(jnp.int32, (block, block), 0)
        query = lax.broadcasted_iota(jnp.int32, (block, block), 1)
        for i in range(count):
            alive = live_col_ref[i * block : (i + 1) * block, :] > 0.5
            visible = (key <= query) & (alive | (key == query))
            mask_ref[i] = jnp.where(visible, 0.0, masked_score)

    lane = lane_index((seq, LANES))
    q = q_ref[...] * 0.125
    k = k_ref[...]
    v = v_ref[...]
    grad = grad_ref[...]
    logs = logs_ref[...]
    dots = grad.astype(f32) * att_ref[...].astype(f32)
    bias = ((live_col_ref[...] - 1.0) * 1e9).astype(bf16)
    zero = jnp.zeros((seq, LANES), bf16)
    one = jnp.ones((seq, LANES), bf16)
    parts = []
    for head in range(2):
        mine = own_lanes(lane, head)
        spare = (1 - head) * HEAD
        log_terms = split_three(-logs[:, head * HEAD : head * HEAD + 1])
        dot_terms = split_three(-jnp.sum(jnp.where(mine, dots, 0.0), axis=-1, keepdims=True))
        q_more, k_more, k_diag, g_more, v_more = (
            jnp.where(lane == spare, one, zero),
            jnp.where(lane == spare, bias, zero),
            zero,
            zero,
            zero,
        )
        for place in range(3):
            here = lane == spare + 1 + place
            q_more = jnp.where(here, log_terms[place], q_more)
            k_more = jnp.where(here, one, k_more)
            k_diag = jnp.where(here, one, k_diag)
            g_more = jnp.where(here, dot_terms[place], g_more)
            v_more = jnp.where(here, one, v_more)
        parts.append(
            dict(
                q=jnp.where(mine, q, q_more),
                k=jnp.where(mine, k, k_more),
                kd=jnp.where(mine, k, k_diag),
                g=jnp.where(mine, grad, g_more),
                v=jnp.where(mine, v, v_more),
                q0=jnp.where(mine, q, zero),
                k0=jnp.where(mine, k, zero),
                g0=jnp.where(mine, grad, zero),
            )
        )
    def rows(i):
        return slice(i * block, (i + 1) * block)

    def score(i, j, head):
        part = parts[head]
        first = dot_nt(part["kd" if j == i else "k"][rows(j)], part["q"][rows(i)])
        return first, dot_nt(part["v"][rows(j)], part["g"][rows(i)])

    def soften(i, j, head, scores, change):
        if j == i:
            scores = scores + mask_ref[i]
        soft = jnp.exp(scores)
        return soft.astype(bf16), (soft * change).astype(bf16)

    def add(name, value):
        totals[name] = totals[name] + value if name in totals else value

    def finish(i, j, head, soft, change):
        part = parts[head]
        add("v", dot_nn(soft, part["g0"][rows(i)]))
        add("k", dot_nn(change, part["q0"][rows(i)]))
        add("q", dot_tn(change, part["k0"][rows(j)]))
        if head == 1:
            for name, ref in (("v", dv_ref), ("k", dk_ref)):
                if j == i:
                    ref[rows(j), :] = totals.pop(name)
                else:
                    ref[rows(j), :] += totals.pop(name)
            if j == i:
                out_ref[0, rows(i), :] = (totals.pop("q") * 0.125).astype(bf16)

    totals = {}
    steps = [(i, j, head) for i in range(count) for j in range(i + 1) for head in range(2)]
    ahead, behind = score(*steps[0]), None
    for place, step in enumerate(steps):
        scored = ahead
        if place + 1 < len(steps):
            ahead = score(*steps[place + 1])
        softened = soften(*step, *scored)
        if behind is not None:
            finish(*steps[place - 1], *behind)
        behind = softened
    finish(*steps[-1], *behind)
    out_ref[1] = dk_ref[...].astype(bf16)
    out_ref[2] = dv_ref[...].astype(bf16)


def attend_back(mixed, att_grad, att, logs, live_col, first=0, count=None, hold=(), block=256, room=VMEM_LIMIT):
    seq, triple = mixed.shape
    pairs = triple // 3 // LANES
    count = pairs if count is None else count
    width = count * LANES
    block = min(block, seq)

    def cols(offset):
        return pl.BlockSpec((seq, LANES), lambda h: (0, offset + h))

    return call(
        functools.partial(attend_back_kernel, block),
        (count,),
        [cols(first), cols(first + pairs), cols(first + 2 * pairs)]
        + [cols(first), cols(first), cols(first), whole_spec(live_col)],
        [pl.BlockSpec((3, seq, LANES), lambda h: (0, 0, h))],
        [sds((3, seq, width), bf16)],
        10 * seq * seq * width,
        [mixed, mixed, mixed, att_grad, att, logs, live_col],
        scratch=[
            pltpu.VMEM((seq // block, block, block), f32),
            pltpu.VMEM((seq, LANES), f32),
            pltpu.VMEM((seq, LANES), f32),
        ],
        hold=hold, room=room,
    )[0]


def all_masks(bits):
    masks = [0]
    for bit in bits:
        masks += [m | (1 << bit) for m in masks]
    return masks


class Cube:
    def __init__(self):
        inner = lax.axis_size(AXES[1])
        self.count = lax.axis_size(AXES[0]) * inner
        self.bits = self.count.bit_length() - 1
        self.inner = inner.bit_length() - 1
        self.pairs = self.count >> (self.inner > 0)
        self.me = lax.axis_index(AXES)
        self.outer = list(range(self.inner, self.bits))
        self.rest = list(range(1, self.inner))
        self.turns = list(zip(self.outer, self.outer[::-1]))
        self.count_turns = 1 << len(self.outer)
        self.count_line = 1 << len(self.rest)

    def send(self, value, mask):
        return lax.ppermute(value, AXES, [(d, d ^ mask) for d in range(self.count)])

    def send_all(self, value, bits):
        return [self.send(value, mask) for mask in all_masks(bits)[1:]]

    def place(self, device, order):
        bits = [pair[order] for pair in self.turns] + self.rest[::-1]
        found = 0
        for bit in bits:
            found = found * 2 + ((device >> bit) & 1)
        return found

    def places(self):
        return jnp.stack([self.place(self.me, 0), self.place(self.me, 1), self.me & 1, self.me])

    def order(self):
        return sorted(range(self.count), key=lambda d: (d & (self.inner > 0), self.place(d, 0)))

    def turned(self, value):
        count = len(self.turns)
        shape = value.shape
        value = value.reshape((2,) * count + (-1,) + shape[1:])
        axes = tuple(range(count))[::-1] + tuple(range(count, value.ndim))
        return value.transpose(axes).reshape(shape)


class Gather:
    def __init__(self, cube, block, split):
        self.cube, self.split = cube, split
        self.value = block[None]

    def line(self, make=None):
        got = self.cube.send_all(self.value, self.cube.rest)
        if make is not None:
            got = after(got, make)
        self.value = jnp.concatenate([self.value, *got], axis=0)
        self.halves = self.split(self.value)
        self.turns = self.cube.turns[::-1]
        return self.value

    def turn(self, *others):
        if self.turns:
            bits = self.turns.pop(0)
            got = [self.cube.send(v, 1 << bit) for v, bit in zip(self.halves, bits)]
            if others:
                got = after(got, others)
            self.halves = [jnp.concatenate(pair, axis=0) for pair in zip(self.halves, got)]
        return self.halves


def after(value, others):
    return lax.optimization_barrier((value, others))[0]


def across(cube, value):
    return [cube.send(value, 1)] if cube.inner else []


def turn_sum_kernel(count, *refs):
    for half in range(count):
        keep, got = refs[2 * half], refs[2 * half + 1]
        first, second = refs[2 * count + 2 * half], refs[2 * count + 2 * half + 1]
        total = (keep[...].astype(f32) + got[...].astype(f32)).astype(bf16)
        middle = first.shape[0]
        first[...] = total[:middle]
        second[...] = total[middle:]


def join_kernel(lanes, *refs):
    low, low_got, late, late_got = refs[:4]
    for place, out in enumerate(refs[4:]):
        first = (low[place].astype(f32) + low_got[place].astype(f32)).astype(bf16)
        second = (late[place].astype(f32) + late_got[place].astype(f32)).astype(bf16)
        if lanes:
            out[:, : first.shape[1]] = first
            out[:, first.shape[1] :] = second
        else:
            out[: first.shape[0], :] = first
            out[first.shape[0] :, :] = second


class Scatter:
    def __init__(self, cube, keep, send, lanes):
        self.cube, self.keep, self.sent, self.lanes = cube, list(keep), list(send), lanes
        self.todo = list(cube.turns)
        self.got, self.total = [], None
        if self.todo:
            self.go()
        else:
            self.total = jnp.concatenate(self.keep, axis=2 if lanes else 1)[0].astype(f32)

    def go(self):
        bits = self.todo.pop(0)
        self.got = [self.cube.send(v, 1 << bit) for v, bit in zip(self.sent, bits)]
        self.last = not self.todo

    def step(self, *others):
        if self.total is not None:
            return []
        got = after(self.got, others) if others else self.got
        if self.sent is None:
            total = self.keep.astype(f32)
            for other in got:
                total = total + other.astype(f32)
            self.total = total
            return [total]
        pairs = [v for pair in zip(self.keep, got) for v in pair]
        small = all(v.shape[1] % 16 == 0 or v.shape[1] == 72 for v in self.keep)
        if not self.last:
            middle = self.keep[0].shape[0] // 2
            if small:
                shapes = [sds((middle,) + v.shape[1:], bf16) for v in self.keep for _ in range(2)]
                made = call(
                    functools.partial(turn_sum_kernel, 2), (1,), [whole_spec(v) for v in pairs],
                    [whole_spec(v) for v in shapes], shapes, 0, pairs, room=24,
                )
            else:
                made = []
                for keep, other in zip(self.keep, got):
                    total = (keep.astype(f32) + other.astype(f32)).astype(bf16)
                    made += [total[:middle], total[middle:]]
            self.keep, self.sent = list(made[0::2]), list(made[1::2])
            self.go()
            return self.sent
        masks = all_masks(self.cube.rest)
        if small:
            first, second = [v.shape[1:] for v in self.keep]
            shape = (first[0], first[1] + second[1]) if self.lanes else (first[0] + second[0], first[1])
            shapes = [sds(shape, bf16)] * len(masks)
            made = call(
                functools.partial(join_kernel, self.lanes), (1,), [whole_spec(v) for v in pairs],
                [whole_spec(v) for v in shapes], shapes, 0, pairs, room=24,
            )
        else:
            total = [
                (a.astype(f32) + b.astype(f32)).astype(bf16) for a, b in zip(self.keep, got)
            ]
            total = jnp.concatenate(total, axis=2 if self.lanes else 1)
            made = [total[i] for i in range(len(masks))]
        self.keep, sent = made[0], list(made[1:])
        self.got = [self.cube.send(v, mask) for v, mask in zip(sent, masks[1:])]
        self.sent = None
        return sent

    def result(self):
        while self.total is None:
            self.step()
        return self.total


def after(value, others):
    return lax.optimization_barrier((value, others))[0]


def across(cube, value):
    return [cube.send(value, 1)] if cube.inner else []


def set_down_kernel(cube, sizes, share, place_ref, pass_ref, *refs):
    sources, (wq_ref, wo_ref, norms_ref, emb_ref) = refs[:-4], refs[-4:]
    per = len(sources) // 2
    half = wq_ref.shape[2] // 2
    mid = sizes[0] + sizes[1]
    extra = sources[0].shape[1] - mid
    row = lax.broadcasted_iota(jnp.int32, (extra, 1), 0)
    picked = (row < 8) | (row == 8 + pass_ref[0])
    empty = jnp.zeros((extra, half), f32)
    small = jnp.zeros((extra, 2 * half), f32)
    for device in range(cube.count):
        for order in range(2):
            at = cube.place(device, order) ^ place_ref[order]
            block = sources[order * per][at]
            if per > 1:
                own = ((device & 1) ^ place_ref[2]) == 0
                block = jnp.where(own, block, sources[order * per + 1][at])
            block = block.astype(f32)
            lanes = slice(order * half, (order + 1) * half)
            wq_ref[device, :, lanes] = block[: sizes[0]].astype(bf16)
            wo_ref[device, :, lanes] = block[sizes[0] : mid].astype(bf16)
            if order * half < share:
                line = [jnp.where(picked, block[mid:], 0.0), empty]
                line = jnp.concatenate(line[::-1] if order else line, axis=1)
                small = small + (pltpu.roll(line, device * share, 1) if device else line)
    norms_ref[...] = small[:8]
    emb_ref[...] = jnp.sum(small[8:], axis=0, keepdims=True)


def set_down(cube, place, pass_index, sources, sizes, share):
    width = 2 * sources[0].shape[2]
    shapes = [(cube.count, n, width) for n in sizes]
    wq, wo, norms, emb = call(
        functools.partial(set_down_kernel, cube, sizes, share), (1,),
        [pl.BlockSpec(memory_space=pltpu.SMEM)] * 2 + [whole_spec(a) for a in sources],
        [pl.BlockSpec(n, lambda i: (0, 0, 0)) for n in shapes]
        + [pl.BlockSpec((n, width), lambda i: (0, 0)) for n in (8, 1)],
        [sds(n, bf16) for n in shapes] + [sds((n, width), f32) for n in (8, 1)], 0,
        [place, pass_index, *sources],
    )
    return wq.reshape(-1, width), wo.reshape(-1, width), norms, emb


def body(
    tokens, row_lengths, live_mask, pass_index,
    w_qkv, w_out, w_up, w_down, norm_gains, norm_shifts, pass_table, cotangent,
):
    _, seq, width = tokens.shape
    cube = Cube()
    place = cube.places()
    ff = w_up.shape[1] * cube.count
    block = min(256, seq)
    grid = (seq // block,)
    passes = pass_table.shape[0]

    def split_lanes(v):
        half = v.shape[2] // 2
        return [v[:, :, :half], v[:, :, half:]]

    high = w_up.shape[1]
    share = w_out.shape[1]

    def wide_rows(v):
        return jnp.pad(v, ((0, -v.shape[0] % 8), (0, width - v.shape[1])))

    packed = jnp.concatenate([w_up.T, w_down], axis=0)
    packed = lax.all_gather(packed, AXES, axis=0, tiled=False)

    gains_shifts = wide_rows(jnp.concatenate([norm_gains, norm_shifts], axis=0))
    early = [w_qkv.T, w_out.T, gains_shifts, wide_rows(pass_table)]
    part_q = Gather(cube, jnp.concatenate(early, axis=0), split_lanes)
    part_q.line()
    for _ in cube.turns:
        part_q.turn()
    low, late = part_q.halves
    sources = [low, *across(cube, low), late, *across(cube, late)]
    sizes = (w_qkv.shape[1], w_out.shape[1])
    wq, wo, norms, emb = set_down(cube, place, pass_index, sources, sizes, share)

    positions = jnp.arange(seq, dtype=jnp.int32)
    inside = positions < row_lengths[0]
    live = jnp.where(inside[None, :] & (live_mask[:, 0] > 0), 1.0, 0.0).astype(f32)
    live_cols = [live[0][:, None], live[1][:, None]]
    live_rows = [live[0][None, :], live[1][None, :]]

    x = tokens[0]
    given = cotangent[0]
    rows_w = rows_spec(block, width)
    rows_f = rows_spec(block, ff)
    rows_q = rows_spec(block, 3 * width)
    rows_1 = rows_spec(block, 1)
    rows_3 = pl.BlockSpec((3, block, width), lambda i: (0, i, 0))
    sums_spec = pl.BlockSpec((8, width), lambda i: (0, 0))
    wide = sds((seq, width), f32)
    thin = sds((seq, width), bf16)
    tall = sds((seq, ff), bf16)
    triple = sds((seq, 3 * width), bf16)
    sums_shape = sds((8, width), f32)
    unit = 2 * seq * width

    mixed0, xhat0 = call(
        first_kernel, grid,
        [rows_w, whole_spec(norms), whole_spec(wq)],
        [rows_q, rows_w], [triple, thin], unit * 3 * width, [x, norms, wq],
    )
    pairs = width // LANES
    third = pairs // 3 if pairs % 3 == 0 else pairs
    att0, logs0 = attend(mixed0, live_cols[0], live_rows[0])
    packed = after(packed, att0)
    order, share = cube.order(), high
    if cube.count == 1 or 768 % high or high % 16:
        blocks = [packed[:, at : at + high] for at in (0, high)]
        turned = [
            jnp.take(v, jnp.asarray(order, jnp.int32) ^ cube.me, axis=0).reshape(ff, width)
            for v in blocks
        ]
        packed, share = jnp.concatenate(turned, axis=0)[None], ff
    smem = pl.BlockSpec(memory_space=pltpu.SMEM)
    hidden0, second0, act0, slope0, later, mixed1, xhat1 = call(
        functools.partial(middle_kernel, order, share), grid,
        [smem, whole_spec(packed), rows_w, rows_w, rows_1]
        + [whole_spec(a) for a in (norms, emb, wo, wq)],
        [rows_w, rows_w, rows_f, rows_f, rows_w, rows_q, rows_w],
        [wide, thin, tall, tall, wide, triple, thin],
        unit * (4 * width + 2 * ff),
        [place, packed, att0, x, live_cols[0], norms, emb, wo, wq],
    )
    att1, logs1 = attend(mixed1, live_cols[1], live_rows[1])
    result, second1, act1, drop1, lift1, branch1, hgrad1, agrad1, sums1 = call(
        functools.partial(turn_kernel, order, share), grid,
        [smem, whole_spec(packed), rows_w, rows_w, rows_1, whole_spec(norms), rows_w]
        + [whole_spec(wo)],
        [rows_w, rows_w, rows_f, rows_w, rows_f, rows_w, rows_w, rows_w, sums_spec],
        [thin, thin, tall, thin, tall, thin, wide, thin, sums_shape],
        unit * (2 * width + 4 * ff),
        [place, packed, att1, later, live_cols[1], norms, given, wo],
    )
    mgrad1 = attend_back(mixed1, agrad1, att1, logs1, live_cols[1])
    drop0, lift0, branch0, hgrad0, agrad0, sums0 = call(
        functools.partial(back_kernel, order, share), grid,
        [smem, whole_spec(packed), rows_3, rows_w, rows_w, whole_spec(norms), rows_1, rows_w, rows_f]
        + [whole_spec(a) for a in (wq, wo)],
        [rows_w, rows_f, rows_w, rows_w, rows_w, sums_spec],
        [thin, tall, thin, wide, thin, sums_shape],
        unit * (4 * width + 2 * ff),
        [place, packed, mgrad1, later, hgrad1, norms, live_cols[0], hidden0, slope0, wq, wo],
    )
    chips = cube.pairs * high
    fast = len(cube.turns) == 2 and (cube.count_line * high) % LANES == 0 and high % 32 == 0
    out_own, out_other = out_grads(cube, place, branch0, branch1, att0, att1)
    up_args = (lift0, lift1, second0, second1)
    down_args = (act0, act1, drop0, drop1)

    def split_rows(v):
        start = high // 2
        return [v[:, :start], cube.turned(v[:, start:])]

    def turn_halves(halves):
        middle = cube.pairs // 2
        return [v[:middle] for v in halves], [v[middle:] for v in halves]

    if fast:
        up_other = other_grads(cube, high, *up_args, extra=[out_other])
        (up_got,) = across(cube, up_other)
        down_other = other_grads(cube, high, *down_args, hold=[up_other])
        (down_got,) = across(cube, down_other)
        made = own_grads(cube, high, *up_args, up_got, extra=[out_own], hold=[down_other])
        up_out = Scatter(cube, made[0::2], made[1::2], False)
        made = own_grads(cube, high, *down_args, down_got, hold=made)
        down = Scatter(cube, made[0::2], made[1::2], False)
    else:
        found = []
        for args, more, more_other in ((up_args, out_own, out_other), (down_args, None, None)):
            own = pair_grads(*args, 0, chips)
            if cube.inner:
                got = across(cube, pair_grads(*args, chips, chips))[0]
                own = (own.astype(f32) + got.astype(f32)).astype(bf16)
                if more is not None:
                    got = across(cube, more_other)[0]
                    more = (more.astype(f32) + got.astype(f32)).astype(bf16)
            halves = split_rows(own.reshape(cube.pairs, high, width))
            if more is not None:
                halves[0] = jnp.concatenate([halves[0], more], axis=1)
            keep, send = turn_halves(halves) if cube.turns else (halves, [])
            found.append(Scatter(cube, keep, send, False))
        up_out, down = found
        made = send
    hold = made
    groups = []
    for first in range(0, pairs, third):
        group = attend_back(
            mixed0, agrad0, att0, logs0, live_cols[0], first, third, hold, room=LATE_LIMIT
        )
        groups.append(group)
        hold = [group]
        if first == 0:
            hold = hold + up_out.step(group)
        elif first == third:
            hold = hold + down.step(group) + up_out.step(group)
        else:
            hold = hold + down.step(group) + up_out.step(group)
    own, other, small = qkv_grads(
        cube, passes, place, pass_index, groups, mgrad1, xhat0, xhat1,
        [wq, sums0, sums1], hold,
    )
    got = across(cube, other)
    if got:
        own = (own.astype(f32) + got[0].astype(f32)).astype(bf16)
    halves = split_lanes(own)
    keep, send = turn_halves(halves) if cube.turns else (halves, [])
    qkv = Scatter(cube, keep, send, True)
    hold = send
    specs_g = [
        pl.BlockSpec((3, block, a.shape[2]), lambda i: (0, i, 0)) for a in groups
    ]
    input_grad = call(
        functools.partial(last_kernel, len(groups)), grid,
        specs_g + [rows_w, rows_w, whole_spec(norms), whole_spec(wq)],
        [rows_w], [wide], unit * 3 * width,
        [*groups, x, hgrad0, norms, wq],
        hold=hold,
        room=LATE_LIMIT,
    )[0]
    qkv.step(input_grad)
    down = down.result()
    up_out = up_out.result()
    qkv = qkv.result()
    share = w_out.shape[1]
    count = w_qkv.shape[1]
    if cube.count > 1:
        half = width // 2
        ends = qkv[count : count + 8]
        small = jnp.concatenate([ends[:, :share], ends[:, half : half + share]], axis=0)
    counts = qkv[count + 8, :count]
    if cube.count == 1:
        counts = jnp.sum(
            sum(jnp.concatenate(v, axis=2) for v in (groups, [mgrad1])).astype(f32), axis=1
        ).reshape(-1)
    qkv = (qkv[:count] * norms[0:1] + counts[:, None] * norms[2:3]).T
    low_end = high // 2
    out_end = low_end + share
    up = jnp.concatenate([up_out[:low_end], up_out[out_end:]], axis=0).T
    out = up_out[low_end:out_end].T
    return (
        result[None], input_grad[None], qkv, out, up, down,
        small[:2], small[2], small[3], small[4 : 4 + passes],
    )


def solution(mesh):
    placed = (
        P(AXES, None, None),
        P(AXES),
        P(None, AXES, None),
        P(AXES),
        P(None, AXES),
        P(None, AXES),
        P(None, AXES),
        P(AXES, None),
        P(None, AXES),
        P(None, AXES),
        P(None, AXES),
        P(AXES, None, None),
    )
    return jax.shard_map(
        body,
        mesh=mesh,
        in_specs=placed,
        out_specs=(
            P(AXES, None, None),
            P(AXES, None, None),
            P(None, AXES),
            P(None, AXES),
            P(None, AXES),
            P(AXES, None),
            P(None, AXES),
            P(AXES),
            P(AXES),
            P(None, AXES),
        ),
        check_vma=False,
    )
```

```python
import functools

import jax
import jax.numpy as jnp
from jax import lax
from jax.experimental import pallas as pl
from jax.experimental.pallas import tpu as pltpu
from jax.sharding import PartitionSpec as P

HEAD = 64
LANES = 128
AXES = ("dp", "fsdp")
bf16 = jnp.bfloat16
f32 = jnp.float32

norm_epsilon = 1e-05
masked_score = -1000000000.0
curve_one = 0.7978845608028654
curve_three = 0.7978845608028654 * 0.044715

MIB = 1024 * 1024
VMEM_LIMIT = 52
LATE_LIMIT = 47


def dot_nn(left, right):
    return lax.dot_general(left, right, (((1,), (0,)), ((), ())), preferred_element_type=f32)


def dot_nt(left, right):
    return lax.dot_general(left, right, (((1,), (1,)), ((), ())), preferred_element_type=f32)


def dot_tn(left, right):
    return lax.dot_general(left, right, (((0,), (0,)), ((), ())), preferred_element_type=f32)


def normalize(values):
    center = jnp.mean(values, axis=-1, keepdims=True)
    centered = values - center
    spread = jnp.mean(centered * centered, axis=-1, keepdims=True)
    scale = lax.rsqrt(spread + norm_epsilon)
    return centered * scale, scale


def norm_back(grad, gain, xhat, scale):
    gained = grad * gain
    first = jnp.mean(gained, axis=-1, keepdims=True)
    second = jnp.mean(gained * xhat, axis=-1, keepdims=True)
    return scale * (gained - first - xhat * second)


def gelu_pair(lifted):
    square = lifted * lifted
    cubic = curve_three * square
    half = 0.5 + 0.5 * jnp.tanh(lifted * (curve_one + cubic))
    value = lifted * half
    slope = half + value * ((1.0 - half) * (2.0 * curve_one + 6.0 * cubic))
    return value, slope


def call(
    kernel, grid, in_specs, out_specs, out_shape, flops, args, scratch=(), hold=(), room=VMEM_LIMIT
):
    moved = sum(a.size * a.dtype.itemsize for a in args)
    moved += sum(o.size * o.dtype.itemsize for o in out_shape)
    given, held = len(args), len(hold)

    def run(*refs):
        kernel(*refs[:given], *refs[given + held :])

    return pl.pallas_call(
        run,
        grid=grid,
        in_specs=list(in_specs) + [pl.BlockSpec(memory_space=pl.ANY)] * held,
        out_specs=out_specs,
        out_shape=out_shape,
        scratch_shapes=list(scratch),
        compiler_params=pltpu.CompilerParams(
            dimension_semantics=("arbitrary",) * len(grid), vmem_limit_bytes=room * MIB
        ),
        cost_estimate=pl.CostEstimate(
            flops=flops, bytes_accessed=moved, transcendentals=0
        ),
    )(*args, *hold)


def rows_spec(block_rows, width):
    return pl.BlockSpec((block_rows, width), lambda i: (i, 0))


def whole_spec(array):
    zeros = (0,) * len(array.shape)
    return pl.BlockSpec(array.shape, lambda i: zeros, pipeline_mode=pl.Buffered(1))


def sds(shape, dtype):
    return jax.ShapeDtypeStruct(shape, dtype)


def head_part(x, gain, shift, w_qkv, mixed_ref, xhat_ref):
    xhat, _ = normalize(x)
    normed = (xhat * gain + shift).astype(bf16)
    xhat_ref[...] = xhat.astype(bf16)
    mixed_ref[...] = dot_nt(normed, w_qkv[...]).astype(bf16)


def first_kernel(x_ref, norms_ref, wq_ref, mixed_ref, xhat_ref):
    head_part(
        x_ref[...].astype(f32), norms_ref[0:1, :], norms_ref[2:3, :], wq_ref, mixed_ref, xhat_ref
    )


def ff_chunks(order, place_ref, packed_ref, share):
    found = []
    if share >= 768:
        for at in range(0, share, 768):
            up, down = pl.ds(at, 768), pl.ds(share + at, 768)
            found.append((lambda r=up: packed_ref[0, r, :], lambda r=down: packed_ref[0, r, :], pl.ds(at, 768)))
        return found
    per = 768 // share
    for first in range(0, len(order), per):

        def rows(at, first=first):
            return jnp.concatenate(
                [
                    packed_ref[place_ref[3] ^ mask, pl.ds(at, share), :]
                    for mask in order[first : first + per]
                ],
                axis=0,
            )

        found.append(
            (functools.partial(rows, 0), functools.partial(rows, share), pl.ds(first * share, 768))
        )
    return found


class Held:
    def __init__(self, order, share, place_ref, packed_ref, held_ref, sems):
        self.share, self.held = share, held_ref
        self.per = max(1, 768 // share)
        self.count = max(1, len(order) // self.per)
        self.copies = []
        for place in range(held_ref.shape[0]):
            device = place_ref[3] ^ order[place] if held_ref.shape[0] > 1 else 0
            self.copies.append(
                pltpu.make_async_copy(packed_ref.at[device], held_ref.at[place], sems.at[place])
            )

    def start(self):
        for copy in self.copies:
            copy.start()

    def chunks(self, wait):
        held, share, per = self.held, self.share, self.per
        width = held.shape[2]
        if share >= 768:
            for copy in self.copies if wait else ():
                copy.wait()
            for at in range(0, share, 768):
                yield held[0, at : at + 768, :], held[0, share + at : share + at + 768, :], pl.ds(at, 768)
            return
        for first in range(0, held.shape[0], per):
            for copy in self.copies[first : first + per] if wait else ():
                copy.wait()
            blocks = slice(first, first + per)
            yield (
                held[blocks, :share, :].reshape(768, width),
                held[blocks, share : 2 * share, :].reshape(768, width),
                pl.ds(first * share, 768),
            )


def twice(body):
    first = pl.program_id(0) == 0

    @pl.when(first)
    def _():
        body(True)

    @pl.when(jnp.logical_not(first))
    def _():
        body(False)


def middle_kernel(order, share, place_ref, packed_ref, *refs):
    chunks = ff_chunks(order, place_ref, packed_ref, share)
    atts, refs = refs[:-13], refs[-13:]
    (
        x_ref, live_ref, norms_ref, emb_ref, wo_ref, wq_ref,
        hidden_ref, second_ref, act_ref, slope_ref, later_ref, mixed_ref, xhat_ref,
    ) = refs
    live = live_ref[...]
    branch, at = 0.0, 0
    for ref in atts:
        branch = branch + dot_nt(ref[...], wo_ref[:, at : at + ref.shape[1]])
        at += ref.shape[1]
    hidden = x_ref[...].astype(f32) + live * branch
    hidden_ref[...] = hidden
    xhat, _ = normalize(hidden)
    second = (xhat * norms_ref[1:2, :] + norms_ref[3:4, :]).astype(bf16)
    second_ref[...] = second
    total = jnp.zeros_like(hidden)
    for up, down, to in chunks:
        value, slope = gelu_pair(dot_nt(second, up()))
        value = value.astype(bf16)
        act_ref[:, to] = value
        slope_ref[:, to] = slope.astype(bf16)
        total = total + dot_nn(value, down())
    later = hidden + live * total + emb_ref[...]
    later_ref[...] = later
    head_part(later, norms_ref[0:1, :], norms_ref[2:3, :], wq_ref, mixed_ref, xhat_ref)


def mlp_back_tail(
    grad, live, hidden, second_grad, norms_ref, wo_ref, branch_ref, hgrad_ref, agrad_ref
):
    xhat, scale = normalize(hidden)
    hgrad = grad + norm_back(second_grad, norms_ref[1:2, :], xhat, scale)
    hgrad_ref[...] = hgrad
    branch = (live * hgrad).astype(bf16)
    branch_ref[...] = branch
    agrad_ref[...] = dot_nn(branch, wo_ref[...]).astype(bf16)
    gain_sum = jnp.sum(second_grad * xhat, axis=0, keepdims=True)
    shift_sum = jnp.sum(second_grad, axis=0, keepdims=True)
    return gain_sum, shift_sum


def add_sums(sums_ref, sums):
    for place, value in enumerate(sums):
        sums_ref[place : place + 1, :] += value


def turn_kernel(order, share, place_ref, packed_ref, *refs):
    (
        att_ref, x_ref, live_ref, norms_ref, grad_ref, wo_ref,
        out_ref, second_ref, act_ref, drop_ref, lift_ref, branch_ref, hgrad_ref, agrad_ref, sums_ref,
        held_ref, sems,
    ) = refs
    weights = Held(order, share, place_ref, packed_ref, held_ref, sems)

    def body(first):
        if first:
            weights.start()
            sums_ref[...] = jnp.zeros_like(sums_ref)
        live = live_ref[...]
        hidden = x_ref[...] + live * dot_nt(att_ref[...], wo_ref[...])
        xhat, _ = normalize(hidden)
        second = (xhat * norms_ref[1:2, :] + norms_ref[3:4, :]).astype(bf16)
        second_ref[...] = second
        grad = grad_ref[...]
        drop = (live * grad).astype(bf16)
        drop_ref[...] = drop
        total = jnp.zeros_like(hidden)
        second_grad = jnp.zeros_like(hidden)
        for up, down, to in weights.chunks(first):
            value, slope = gelu_pair(dot_nt(second, up))
            value = value.astype(bf16)
            act_ref[:, to] = value
            lift = (dot_nt(drop, down) * slope).astype(bf16)
            lift_ref[:, to] = lift
            second_grad = second_grad + dot_nn(lift, up)
            total = total + dot_nn(value, down)
        out_ref[...] = (hidden + live * total).astype(bf16)
        sums = mlp_back_tail(
            grad, live, hidden, second_grad, norms_ref, wo_ref, branch_ref, hgrad_ref, agrad_ref
        )
        add_sums(sums_ref, sums)

    twice(body)


def head_back(mixed_grad_refs, wq_ref, x, hgrad, norms_ref):
    width = x.shape[1]
    normed_grad = jnp.zeros_like(x)
    for part in range(3):
        at = part * width
        for ref in mixed_grad_refs:
            normed_grad += dot_nn(ref[part], wq_ref[at : at + ref.shape[2], :])
            at += ref.shape[2]
    xhat, scale = normalize(x)
    return hgrad + norm_back(normed_grad, norms_ref[0:1, :], xhat, scale)


def back_kernel(order, share, place_ref, packed_ref, *refs):
    (
        mgrad_ref, later_ref, hgrad1_ref, norms_ref, live_ref, hidden_ref, slope_ref, wq_ref, wo_ref,
        drop_ref, lift_ref, branch_ref, hgrad_ref, agrad_ref, sums_ref, held_ref, sems,
    ) = refs
    weights = Held(order, share, place_ref, packed_ref, held_ref, sems)

    def body(first):
        if first:
            weights.start()
            sums_ref[...] = jnp.zeros_like(sums_ref)
        grad = head_back([mgrad_ref], wq_ref, later_ref[...], hgrad1_ref[...], norms_ref)
        table_sum = jnp.sum(grad, axis=0, keepdims=True)
        live = live_ref[...]
        drop = (live * grad).astype(bf16)
        drop_ref[...] = drop
        second_grad = jnp.zeros_like(grad)
        for up, down, to in weights.chunks(first):
            lift = (dot_nt(drop, down) * slope_ref[:, to].astype(f32)).astype(bf16)
            lift_ref[:, to] = lift
            second_grad = second_grad + dot_nn(lift, up)
        sums = mlp_back_tail(
            grad, live, hidden_ref[...], second_grad, norms_ref, wo_ref,
            branch_ref, hgrad_ref, agrad_ref,
        )
        add_sums(sums_ref, sums + (table_sum,))

    twice(body)


def last_kernel(groups, *refs):
    mgrad_refs, (x_ref, hgrad_ref, norms_ref, wq_ref, out_ref) = refs[:groups], refs[groups:]
    out_ref[...] = head_back(
        mgrad_refs, wq_ref, x_ref[...].astype(f32), hgrad_ref[...], norms_ref
    )


def both_layers(left0, left1, right0, right1):
    return dot_tn(left0[...], right0[...]) + dot_tn(left1[...], right1[...])


def pair_grad_kernel(left0, left1, right0, right1, out_ref):
    out_ref[...] = both_layers(left0, left1, right0, right1).astype(bf16)


def pair_grads(left0, left1, right0, right1, start, size, hold=()):
    tokens = left0.shape[0]
    width = right0.shape[1]
    step = 384 if size % 384 == 0 else size
    first = start // step
    cols = pl.BlockSpec((tokens, step), lambda i: (0, first + i))
    return call(
        pair_grad_kernel,
        (size // step,),
        [cols] * 2 + [whole_spec(right0)] * 2,
        [rows_spec(step, width)],
        [sds((size, width), bf16)],
        4 * tokens * size * width,
        [left0, left1, right0, right1],
        hold=hold, room=LATE_LIMIT,
    )[0]


def blocks_spec(shape, index):
    return pl.BlockSpec(shape, lambda i: (index(i), 0, 0))


def other_grad_kernel(high, left0, left1, right0, right1, *refs):
    extra, out_ref = refs[:-1], refs[-1]
    total = both_layers(left0, left1, right0, right1).astype(bf16)
    for place in range(out_ref.shape[0]):
        out_ref[place, :high, :] = total[place * high : (place + 1) * high]
        for ref in extra:
            out_ref[place, high:, :] = ref[place]


def other_grads(cube, high, left0, left1, right0, right1, extra=(), hold=()):
    tokens = left0.shape[0]
    width = right0.shape[1]
    lines, turns = cube.count_line, cube.count_turns
    first = turns
    cols = pl.BlockSpec((tokens, lines * high), lambda i: (0, first + i))
    rows = high + sum(a.shape[1] for a in extra)
    return call(
        functools.partial(other_grad_kernel, high),
        (turns,),
        [cols] * 2
        + [whole_spec(right0)] * 2
        + [blocks_spec((lines,) + a.shape[1:], lambda i: i) for a in extra],
        [blocks_spec((lines, rows, width), lambda i: i)],
        [sds((cube.pairs, rows, width), bf16)],
        4 * tokens * cube.pairs * high * width,
        [left0, left1, right0, right1, *extra],
        hold=hold, room=LATE_LIMIT,
    )[0]


def own_grad_kernel(high, left0, left1, right0, right1, got, *refs):
    extra, (low_keep, low_send, late_keep, late_send) = refs[:-4], refs[-4:]
    middle = high // 2
    half = pl.num_programs(0) // 2
    step = pl.program_id(0)
    total = both_layers(left0, left1, right0, right1)

    def low_part(ref):
        for place in range(ref.shape[0]):
            at = place * high
            ref[place, :middle, :] = (
                total[at : at + middle] + got[place, :middle, :].astype(f32)
            ).astype(bf16)
            for more in extra:
                ref[place, middle:, :] = (
                    more[place].astype(f32) + got[place, high:, :].astype(f32)
                ).astype(bf16)

    def late_part(ref):
        for place in range(ref.shape[0]):
            at = place * high
            ref[place] = (
                total[at + middle : at + high] + got[place, middle:high, :].astype(f32)
            ).astype(bf16)

    @pl.when(step < half)
    def _():
        low_part(low_keep)

    @pl.when(step >= half)
    def _():
        low_part(low_send)

    @pl.when(step % 2 == 0)
    def _():
        late_part(late_keep)

    @pl.when(step % 2 == 1)
    def _():
        late_part(late_send)


def own_grads(cube, high, left0, left1, right0, right1, got, extra=(), hold=()):
    tokens = left0.shape[0]
    width = right0.shape[1]
    lines, turns = cube.count_line, cube.count_turns
    half = turns // 2
    cols = pl.BlockSpec((tokens, lines * high), lambda i: (0, i))
    low = high // 2 + sum(a.shape[1] for a in extra)
    late = high - high // 2

    def turned(i):
        found = 0
        for bit in range(1, turns.bit_length() - 1):
            found = found + (((i >> bit) & 1) << (turns.bit_length() - 2 - bit))
        return found

    def first_keep(i):
        return jnp.minimum(i, half - 1)

    def first_send(i):
        return jnp.maximum(i - half, 0)

    return call(
        functools.partial(own_grad_kernel, high),
        (turns,),
        [cols] * 2
        + [whole_spec(right0)] * 2
        + [blocks_spec((lines,) + a.shape[1:], lambda i: i) for a in (got, *extra)],
        [
            blocks_spec((lines, low, width), first_keep),
            blocks_spec((lines, low, width), first_send),
            blocks_spec((lines, late, width), turned),
            blocks_spec((lines, late, width), turned),
        ],
        [sds((cube.pairs // 2, n, width), bf16) for n in (low, low, late, late)],
        4 * tokens * cube.pairs * high * width,
        [left0, left1, right0, right1, got, *extra],
        hold=hold, room=LATE_LIMIT,
    )


def place_blocks(cube, place_ref, total_ref, own_ref, other_ref):
    rows = own_ref.shape[1]
    for chip in range(own_ref.shape[0]):
        if cube.inner == 0:
            own_ref[0] = total_ref[...].astype(bf16)
            continue
        even = total_ref[pl.ds(2 * chip * rows, rows), :].astype(bf16)
        odd = total_ref[pl.ds((2 * chip + 1) * rows, rows), :].astype(bf16)
        first = place_ref[2] == 0
        at = cube.place(2 * chip, 0) ^ place_ref[0]
        own_ref[at] = jnp.where(first, even, odd)
        other_ref[at] = jnp.where(first, odd, even)


def out_grad_kernel(cube, place_ref, left0, left1, right0, right1, own_ref, other_ref, total_ref):
    total_ref[...] = both_layers(left0, left1, right0, right1)
    place_blocks(cube, place_ref, total_ref, own_ref, other_ref)


def block_shapes(cube, rows, width):
    shape = (cube.pairs, rows, width)
    return [sds(shape, bf16)] * 2, [pl.BlockSpec(shape, lambda i: (0, 0, 0))] * 2


def out_grads(cube, place, left0, left1, right0, right1, hold=()):
    tokens, high = left0.shape
    width = right1.shape[1]
    shapes, specs = block_shapes(cube, high // cube.count, width)
    args = [left0, left1, right0, right1]
    return call(
        functools.partial(out_grad_kernel, cube),
        (1,),
        [pl.BlockSpec(memory_space=pltpu.SMEM)] + [whole_spec(a) for a in args],
        specs,
        shapes,
        4 * tokens * high * width,
        [place, *args],
        scratch=[pltpu.VMEM((high, width), f32)],
        hold=hold, room=LATE_LIMIT,
    )


def qkv_grad_kernel(cube, groups, passes, place_ref, pass_ref, *refs):
    lefts0, refs = refs[:groups], refs[groups:]
    left1, right0, right1, wq_ref, sums0_ref, sums1_ref, own_ref, other_ref = refs[:8]
    small_ref, total_ref, count_ref = refs[8:]
    part = pl.program_id(0)
    high = left1.shape[2]
    width = right0.shape[1]
    row = lax.broadcasted_iota(jnp.int32, (8, 1), 0)

    @pl.when(part == 0)
    def _():
        small_ref[...] = jnp.zeros_like(small_ref)
        small_ref[1:2, :] = sums0_ref[0:1, :] + sums1_ref[0:1, :]
        small_ref[3:4, :] = sums0_ref[1:2, :] + sums1_ref[1:2, :]
        for index in range(passes):
            small_ref[4 + index : 5 + index, :] = jnp.where(
                pass_ref[0] == index, sums0_ref[2:3, :], 0.0
            )

    at = 0
    gain_sum = jnp.zeros((1, width), f32)
    shift_sum = jnp.zeros((1, width), f32)
    for left0 in lefts0:
        to = pl.ds(at, left0.shape[2])
        rows = pl.ds(pl.multiple_of(part * high + at, 8), left0.shape[2])
        total = dot_tn(left0[0], right0[...]) + dot_tn(left1[0, :, to], right1[...])
        total_ref[rows, :] = total
        sums = jnp.sum(left0[0].astype(f32) + left1[0, :, to].astype(f32), axis=0, keepdims=True)
        count_ref[pl.ds(part, 1), to] = sums
        terms = split_three(jnp.broadcast_to(sums, (8, left0.shape[2])))
        three = jnp.where(row == 0, terms[0], jnp.where(row == 1, terms[1], terms[2]))
        three = jnp.where(row < 3, three, jnp.zeros_like(three))
        weights = wq_ref[to, :]
        gain_sum += jnp.sum(total * weights.astype(f32), axis=0, keepdims=True)
        shift_sum += jnp.sum(dot_nn(three, weights), axis=0, keepdims=True)
        at += left0.shape[2]
    small_ref[0:1, :] += gain_sum
    small_ref[2:3, :] += shift_sum

    @pl.when(part == pl.num_programs(0) - 1)
    def _():
        extra = 8
        rows = own_ref.shape[1] - extra
        share = width // cube.count
        half = width // 2
        small = small_ref[...]
        counts = jnp.concatenate([count_ref[p : p + 1, :] for p in range(3)], axis=1)
        counts = jnp.broadcast_to(counts, (8, counts.shape[1]))
        for chip in range(cube.pairs):
            found = []
            for device in range(2 * chip, 2 * chip + 1 + (cube.inner > 0)):
                block = total_ref[pl.ds(device * rows, rows), :]
                line, own = small, counts
                if device:
                    line = pltpu.roll(small, width - device * share, 1)
                    own = pltpu.roll(counts, counts.shape[1] - device * rows, 1)
                line = [line[:8, :LANES], own[:, : half - LANES], line[8:, :half]]
                line = jnp.concatenate(line, axis=1)
                found.append(jnp.concatenate([block, line], axis=0).astype(bf16))
            if cube.inner == 0:
                own_ref[0] = found[0]
                continue
            first = place_ref[2] == 0
            own = jnp.where(first, found[0], found[1])
            other = jnp.where(first, found[1], found[0])
            for order in range(2):
                lanes = slice(order * half, (order + 1) * half)
                at = cube.place(2 * chip, order) ^ place_ref[order]
                own_ref[at, :, lanes] = own[:, lanes]
                other_ref[at, :, lanes] = other[:, lanes]


def qkv_grads(cube, passes, place, pass_index, lefts0, left1, right0, right1, kept, hold=()):
    parts, tokens, high = left1.shape
    width = right0.shape[1]
    specs = [
        pl.BlockSpec((1, tokens, a.shape[2]), lambda i: (i, 0, 0)) for a in (*lefts0, left1)
    ]
    shapes, out_specs = block_shapes(cube, parts * high // cube.count + 8, width)
    return call(
        functools.partial(qkv_grad_kernel, cube, len(lefts0), passes),
        (parts,),
        [pl.BlockSpec(memory_space=pltpu.SMEM)] * 2
        + specs
        + [whole_spec(a) for a in (right0, right1)]
        + [rows_spec(high, width)]
        + [whole_spec(a) for a in kept[1:]],
        out_specs + [pl.BlockSpec((16, width), lambda i: (0, 0))],
        shapes + [sds((16, width), f32)],
        4 * tokens * parts * high * width,
        [place, pass_index, *lefts0, left1, right0, right1, *kept],
        scratch=[pltpu.VMEM((parts * high, width), f32), pltpu.VMEM((8, high), f32)],
        hold=hold,
        room=LATE_LIMIT,
    )


def lane_index(shape):
    return lax.broadcasted_iota(jnp.int32, shape, len(shape) - 1)


def split_three(values):
    high = values.astype(bf16)
    rest = values - high.astype(f32)
    middle = rest.astype(bf16)
    low = (rest - middle.astype(f32)).astype(bf16)
    return high, middle, low


def own_lanes(lane, head):
    return (lane < HEAD) if head == 0 else (lane >= HEAD)


def attend_kernel(
    block, q_ref, k_ref, v_ref, live_col_ref, live_row_ref, out_ref, logs_ref, mask_ref
):
    seq = q_ref.shape[0]
    count = seq // block

    @pl.when(pl.program_id(0) == 0)
    def _():
        query = lax.broadcasted_iota(jnp.int32, (block, block), 0)
        key = lax.broadcasted_iota(jnp.int32, (block, block), 1)
        for i in range(count):
            alive = live_row_ref[:, i * block : (i + 1) * block] > 0.5
            visible = (key <= query) & (alive | (key == query))
            mask_ref[i] = jnp.where(visible, 0.0, masked_score)

    lane = lane_index((seq, LANES))
    q = q_ref[...] * 0.125
    k = k_ref[...]
    v = v_ref[...]
    bias = ((live_col_ref[...] - 1.0) * 1e9).astype(bf16)
    zero = jnp.zeros((seq, LANES), bf16)
    one = jnp.ones((seq, LANES), bf16)
    parts = []
    for head in range(2):
        mine = own_lanes(lane, head)
        spare = (1 - head) * HEAD
        parts.append(
            (
                jnp.where(mine, q, zero),
                jnp.where(mine, q, jnp.where(lane == spare, one, zero)),
                jnp.where(mine, k, jnp.where(lane == spare, bias, zero)),
                jnp.where(mine, v, one),
            )
        )
    low = lane_index((block, LANES)) < HEAD

    def score(i, head):
        at, before = slice(i * block, (i + 1) * block), slice(0, i * block)
        q_plain, q_bias, k_bias, _ = parts[head]
        diag = dot_nt(q_plain[at], k[at]) + mask_ref[i]
        return diag, dot_nt(q_bias[at], k_bias[before]) if i > 0 else None

    def soften(diag, off):
        top = jnp.max(diag, axis=-1, keepdims=True)
        if off is None:
            return top, jnp.exp(diag - top).astype(bf16), None
        top = jnp.maximum(top, jnp.max(off, axis=-1, keepdims=True))
        return top, jnp.exp(diag - top).astype(bf16), jnp.exp(off - top).astype(bf16)

    def finish(i, head, top, diag, off):
        at, before = slice(i * block, (i + 1) * block), slice(0, i * block)
        v_ones = parts[head][3]
        total = dot_nn(diag, v_ones[at])
        if i > 0:
            total += dot_nn(off, v_ones[before])
        spare = (1 - head) * HEAD
        weight = total[:, spare : spare + 1]
        found.append((total * (1.0 / weight), top + jnp.log(weight)))
        if head == 1:
            (out0, log0), (out1, log1) = found[-2:]
            out_ref[at, :] = jnp.where(low, out0, out1).astype(bf16)
            logs_ref[at, :] = jnp.where(low, log0, log1)

    found = []
    steps = [(i, head) for i in range(count) for head in range(2)]
    ahead, behind = score(*steps[0]), None
    for place, step in enumerate(steps):
        scored = ahead
        if place + 1 < len(steps):
            ahead = score(*steps[place + 1])
        softened = soften(*scored)
        if behind is not None:
            finish(*steps[place - 1], *behind)
        behind = softened
    finish(*steps[-1], *behind)


def attend(mixed, live_col, live_row, first=0, count=None, hold=(), block=256):
    seq, triple = mixed.shape
    pairs = triple // 3 // LANES
    count = pairs if count is None else count
    width = count * LANES
    block = min(block, seq)

    def cols(offset):
        return pl.BlockSpec((seq, LANES), lambda h: (0, offset + h))

    return call(
        functools.partial(attend_kernel, block),
        (count,),
        [cols(first), cols(first + pairs), cols(first + 2 * pairs), whole_spec(live_col), whole_spec(live_row)],
        [cols(0), cols(0)],
        [sds((seq, width), bf16), sds((seq, width), f32)],
        4 * seq * seq * width,
        [mixed, mixed, mixed, live_col, live_row],
        scratch=[pltpu.VMEM((seq // block, block, block), f32)],
        hold=hold, room=VMEM_LIMIT,
    )


def attend_back_kernel(
    block, q_ref, k_ref, v_ref, grad_ref, att_ref, logs_ref, live_col_ref, out_ref,
    mask_ref, dk_ref, dv_ref,
):
    seq = q_ref.shape[0]
    count = seq // block

    @pl.when(pl.program_id(0) == 0)
    def _():
        key = lax.broadcasted_iota(jnp.int32, (block, block), 0)
        query = lax.broadcasted_iota(jnp.int32, (block, block), 1)
        for i in range(count):
            alive = live_col_ref[i * block : (i + 1) * block, :] > 0.5
            visible = (key <= query) & (alive | (key == query))
            mask_ref[i] = jnp.where(visible, 0.0, masked_score)

    lane = lane_index((seq, LANES))
    q = q_ref[...] * 0.125
    k = k_ref[...]
    v = v_ref[...]
    grad = grad_ref[...]
    logs = logs_ref[...]
    dots = grad.astype(f32) * att_ref[...].astype(f32)
    bias = ((live_col_ref[...] - 1.0) * 1e9).astype(bf16)
    zero = jnp.zeros((seq, LANES), bf16)
    one = jnp.ones((seq, LANES), bf16)
    parts = []
    for head in range(2):
        mine = own_lanes(lane, head)
        spare = (1 - head) * HEAD
        log_terms = split_three(-logs[:, head * HEAD : head * HEAD + 1])
        dot_terms = split_three(-jnp.sum(jnp.where(mine, dots, 0.0), axis=-1, keepdims=True))
        q_more, k_more, k_diag, g_more, v_more = (
            jnp.where(lane == spare, one, zero),
            jnp.where(lane == spare, bias, zero),
            zero,
            zero,
            zero,
        )
        for place in range(3):
            here = lane == spare + 1 + place
            q_more = jnp.where(here, log_terms[place], q_more)
            k_more = jnp.where(here, one, k_more)
            k_diag = jnp.where(here, one, k_diag)
            g_more = jnp.where(here, dot_terms[place], g_more)
            v_more = jnp.where(here, one, v_more)
        parts.append(
            dict(
                q=jnp.where(mine, q, q_more),
                k=jnp.where(mine, k, k_more),
                kd=jnp.where(mine, k, k_diag),
                g=jnp.where(mine, grad, g_more),
                v=jnp.where(mine, v, v_more),
                q0=jnp.where(mine, q, zero),
                k0=jnp.where(mine, k, zero),
                g0=jnp.where(mine, grad, zero),
            )
        )
    def rows(i):
        return slice(i * block, (i + 1) * block)

    def score(i, j, head):
        part = parts[head]
        first = dot_nt(part["kd" if j == i else "k"][rows(j)], part["q"][rows(i)])
        return first, dot_nt(part["v"][rows(j)], part["g"][rows(i)])

    def soften(i, j, head, scores, change):
        if j == i:
            scores = scores + mask_ref[i]
        soft = jnp.exp(scores)
        return soft.astype(bf16), (soft * change).astype(bf16)

    def add(name, value):
        totals[name] = totals[name] + value if name in totals else value

    def finish(i, j, head, soft, change):
        part = parts[head]
        add("v", dot_nn(soft, part["g0"][rows(i)]))
        add("k", dot_nn(change, part["q0"][rows(i)]))
        add("q", dot_tn(change, part["k0"][rows(j)]))
        if head == 1:
            for name, ref in (("v", dv_ref), ("k", dk_ref)):
                if j == i:
                    ref[rows(j), :] = totals.pop(name)
                else:
                    ref[rows(j), :] += totals.pop(name)
            if j == i:
                out_ref[0, rows(i), :] = (totals.pop("q") * 0.125).astype(bf16)

    totals = {}
    steps = [(i, j, head) for i in range(count) for j in range(i + 1) for head in range(2)]
    ahead, behind = score(*steps[0]), None
    for place, step in enumerate(steps):
        scored = ahead
        if place + 1 < len(steps):
            ahead = score(*steps[place + 1])
        softened = soften(*step, *scored)
        if behind is not None:
            finish(*steps[place - 1], *behind)
        behind = softened
    finish(*steps[-1], *behind)
    out_ref[1] = dk_ref[...].astype(bf16)
    out_ref[2] = dv_ref[...].astype(bf16)


def attend_back(mixed, att_grad, att, logs, live_col, first=0, count=None, hold=(), block=256, room=VMEM_LIMIT):
    seq, triple = mixed.shape
    pairs = triple // 3 // LANES
    count = pairs if count is None else count
    width = count * LANES
    block = min(block, seq)

    def cols(offset):
        return pl.BlockSpec((seq, LANES), lambda h: (0, offset + h))

    return call(
        functools.partial(attend_back_kernel, block),
        (count,),
        [cols(first), cols(first + pairs), cols(first + 2 * pairs)]
        + [cols(first), cols(first), cols(first), whole_spec(live_col)],
        [pl.BlockSpec((3, seq, LANES), lambda h: (0, 0, h))],
        [sds((3, seq, width), bf16)],
        10 * seq * seq * width,
        [mixed, mixed, mixed, att_grad, att, logs, live_col],
        scratch=[
            pltpu.VMEM((seq // block, block, block), f32),
            pltpu.VMEM((seq, LANES), f32),
            pltpu.VMEM((seq, LANES), f32),
        ],
        hold=hold, room=room,
    )[0]


def all_masks(bits):
    masks = [0]
    for bit in bits:
        masks += [m | (1 << bit) for m in masks]
    return masks


class Cube:
    def __init__(self):
        inner = lax.axis_size(AXES[1])
        self.count = lax.axis_size(AXES[0]) * inner
        self.bits = self.count.bit_length() - 1
        self.inner = inner.bit_length() - 1
        self.pairs = self.count >> (self.inner > 0)
        self.me = lax.axis_index(AXES)
        self.outer = list(range(self.inner, self.bits))
        self.rest = list(range(1, self.inner))
        self.turns = list(zip(self.outer, self.outer[::-1]))
        self.count_turns = 1 << len(self.outer)
        self.count_line = 1 << len(self.rest)

    def send(self, value, mask):
        return lax.ppermute(value, AXES, [(d, d ^ mask) for d in range(self.count)])

    def send_all(self, value, bits):
        return [self.send(value, mask) for mask in all_masks(bits)[1:]]

    def place(self, device, order):
        bits = [pair[order] for pair in self.turns] + self.rest[::-1]
        found = 0
        for bit in bits:
            found = found * 2 + ((device >> bit) & 1)
        return found

    def places(self):
        return jnp.stack([self.place(self.me, 0), self.place(self.me, 1), self.me & 1, self.me])

    def order(self):
        return sorted(range(self.count), key=lambda d: (d & (self.inner > 0), self.place(d, 0)))

    def turned(self, value):
        count = len(self.turns)
        shape = value.shape
        value = value.reshape((2,) * count + (-1,) + shape[1:])
        axes = tuple(range(count))[::-1] + tuple(range(count, value.ndim))
        return value.transpose(axes).reshape(shape)


class Gather:
    def __init__(self, cube, block, split):
        self.cube, self.split = cube, split
        self.value = block[None]

    def line(self, make=None):
        got = self.cube.send_all(self.value, self.cube.rest)
        if make is not None:
            got = after(got, make)
        self.value = jnp.concatenate([self.value, *got], axis=0)
        self.halves = self.split(self.value)
        self.turns = self.cube.turns[::-1]
        return self.value

    def turn(self, *others):
        if self.turns:
            bits = self.turns.pop(0)
            got = [self.cube.send(v, 1 << bit) for v, bit in zip(self.halves, bits)]
            if others:
                got = after(got, others)
            self.halves = [jnp.concatenate(pair, axis=0) for pair in zip(self.halves, got)]
        return self.halves


def after(value, others):
    return lax.optimization_barrier((value, others))[0]


def across(cube, value):
    return [cube.send(value, 1)] if cube.inner else []


def turn_sum_kernel(count, *refs):
    for half in range(count):
        keep, got = refs[2 * half], refs[2 * half + 1]
        first, second = refs[2 * count + 2 * half], refs[2 * count + 2 * half + 1]
        total = (keep[...].astype(f32) + got[...].astype(f32)).astype(bf16)
        middle = first.shape[0]
        first[...] = total[:middle]
        second[...] = total[middle:]


def join_kernel(lanes, *refs):
    low, low_got, late, late_got = refs[:4]
    for place, out in enumerate(refs[4:]):
        first = (low[place].astype(f32) + low_got[place].astype(f32)).astype(bf16)
        second = (late[place].astype(f32) + late_got[place].astype(f32)).astype(bf16)
        if lanes:
            out[:, : first.shape[1]] = first
            out[:, first.shape[1] :] = second
        else:
            out[: first.shape[0], :] = first
            out[first.shape[0] :, :] = second


class Scatter:
    def __init__(self, cube, keep, send, lanes):
        self.cube, self.keep, self.sent, self.lanes = cube, list(keep), list(send), lanes
        self.todo = list(cube.turns)
        self.got, self.total = [], None
        if self.todo:
            self.go()
        else:
            self.total = jnp.concatenate(self.keep, axis=2 if lanes else 1)[0].astype(f32)

    def go(self):
        bits = self.todo.pop(0)
        self.got = [self.cube.send(v, 1 << bit) for v, bit in zip(self.sent, bits)]
        self.last = not self.todo

    def step(self, *others):
        if self.total is not None:
            return []
        got = after(self.got, others) if others else self.got
        if self.sent is None:
            total = self.keep.astype(f32)
            for other in got:
                total = total + other.astype(f32)
            self.total = total
            return [total]
        pairs = [v for pair in zip(self.keep, got) for v in pair]
        small = all(v.shape[1] % 16 == 0 or v.shape[1] == 72 for v in self.keep)
        if not self.last:
            middle = self.keep[0].shape[0] // 2
            if small:
                shapes = [sds((middle,) + v.shape[1:], bf16) for v in self.keep for _ in range(2)]
                made = call(
                    functools.partial(turn_sum_kernel, 2), (1,), [whole_spec(v) for v in pairs],
                    [whole_spec(v) for v in shapes], shapes, 0, pairs, room=24,
                )
            else:
                made = []
                for keep, other in zip(self.keep, got):
                    total = (keep.astype(f32) + other.astype(f32)).astype(bf16)
                    made += [total[:middle], total[middle:]]
            self.keep, self.sent = list(made[0::2]), list(made[1::2])
            self.go()
            return self.sent
        masks = all_masks(self.cube.rest)
        if small:
            first, second = [v.shape[1:] for v in self.keep]
            shape = (first[0], first[1] + second[1]) if self.lanes else (first[0] + second[0], first[1])
            shapes = [sds(shape, bf16)] * len(masks)
            made = call(
                functools.partial(join_kernel, self.lanes), (1,), [whole_spec(v) for v in pairs],
                [whole_spec(v) for v in shapes], shapes, 0, pairs, room=24,
            )
        else:
            total = [
                (a.astype(f32) + b.astype(f32)).astype(bf16) for a, b in zip(self.keep, got)
            ]
            total = jnp.concatenate(total, axis=2 if self.lanes else 1)
            made = [total[i] for i in range(len(masks))]
        self.keep, sent = made[0], list(made[1:])
        self.got = [self.cube.send(v, mask) for v, mask in zip(sent, masks[1:])]
        self.sent = None
        return sent

    def result(self):
        while self.total is None:
            self.step()
        return self.total


def after(value, others):
    return lax.optimization_barrier((value, others))[0]


def across(cube, value):
    return [cube.send(value, 1)] if cube.inner else []


def set_down_kernel(cube, sizes, share, place_ref, pass_ref, *refs):
    sources, (wq_ref, wo_ref, norms_ref, emb_ref) = refs[:-4], refs[-4:]
    per = len(sources) // 2
    half = wq_ref.shape[2] // 2
    mid = sizes[0] + sizes[1]
    extra = sources[0].shape[1] - mid
    row = lax.broadcasted_iota(jnp.int32, (extra, 1), 0)
    picked = (row < 8) | (row == 8 + pass_ref[0])
    empty = jnp.zeros((extra, half), f32)
    small = jnp.zeros((extra, 2 * half), f32)
    for device in range(cube.count):
        for order in range(2):
            at = cube.place(device, order) ^ place_ref[order]
            block = sources[order * per][at]
            if per > 1:
                own = ((device & 1) ^ place_ref[2]) == 0
                block = jnp.where(own, block, sources[order * per + 1][at])
            block = block.astype(f32)
            lanes = slice(order * half, (order + 1) * half)
            wq_ref[device, :, lanes] = block[: sizes[0]].astype(bf16)
            wo_ref[device, :, lanes] = block[sizes[0] : mid].astype(bf16)
            if order * half < share:
                line = [jnp.where(picked, block[mid:], 0.0), empty]
                line = jnp.concatenate(line[::-1] if order else line, axis=1)
                small = small + (pltpu.roll(line, device * share, 1) if device else line)
    norms_ref[...] = small[:8]
    emb_ref[...] = jnp.sum(small[8:], axis=0, keepdims=True)


def set_down(cube, place, pass_index, sources, sizes, share):
    width = 2 * sources[0].shape[2]
    shapes = [(cube.count, n, width) for n in sizes]
    wq, wo, norms, emb = call(
        functools.partial(set_down_kernel, cube, sizes, share), (1,),
        [pl.BlockSpec(memory_space=pltpu.SMEM)] * 2 + [whole_spec(a) for a in sources],
        [pl.BlockSpec(n, lambda i: (0, 0, 0)) for n in shapes]
        + [pl.BlockSpec((n, width), lambda i: (0, 0)) for n in (8, 1)],
        [sds(n, bf16) for n in shapes] + [sds((n, width), f32) for n in (8, 1)], 0,
        [place, pass_index, *sources],
    )
    return wq.reshape(-1, width), wo.reshape(-1, width), norms, emb


def body(
    tokens, row_lengths, live_mask, pass_index,
    w_qkv, w_out, w_up, w_down, norm_gains, norm_shifts, pass_table, cotangent,
):
    _, seq, width = tokens.shape
    cube = Cube()
    place = cube.places()
    ff = w_up.shape[1] * cube.count
    block = min(256, seq)
    grid = (seq // block,)
    passes = pass_table.shape[0]

    def split_lanes(v):
        half = v.shape[2] // 2
        return [v[:, :, :half], v[:, :, half:]]

    high = w_up.shape[1]
    share = w_out.shape[1]

    def wide_rows(v):
        return jnp.pad(v, ((0, -v.shape[0] % 8), (0, width - v.shape[1])))

    packed = jnp.concatenate([w_up.T, w_down], axis=0)
    packed = lax.all_gather(packed, AXES, axis=0, tiled=False)

    gains_shifts = wide_rows(jnp.concatenate([norm_gains, norm_shifts], axis=0))
    early = [w_qkv.T, w_out.T, gains_shifts, wide_rows(pass_table)]
    part_q = Gather(cube, jnp.concatenate(early, axis=0), split_lanes)
    part_q.line()
    for _ in cube.turns:
        part_q.turn()
    low, late = part_q.halves
    sources = [low, *across(cube, low), late, *across(cube, late)]
    sizes = (w_qkv.shape[1], w_out.shape[1])
    wq, wo, norms, emb = set_down(cube, place, pass_index, sources, sizes, share)

    positions = jnp.arange(seq, dtype=jnp.int32)
    inside = positions < row_lengths[0]
    live = jnp.where(inside[None, :] & (live_mask[:, 0] > 0), 1.0, 0.0).astype(f32)
    live_cols = [live[0][:, None], live[1][:, None]]
    live_rows = [live[0][None, :], live[1][None, :]]

    x = tokens[0]
    given = cotangent[0]
    rows_w = rows_spec(block, width)
    rows_f = rows_spec(block, ff)
    rows_q = rows_spec(block, 3 * width)
    rows_1 = rows_spec(block, 1)
    rows_3 = pl.BlockSpec((3, block, width), lambda i: (0, i, 0))
    sums_spec = pl.BlockSpec((8, width), lambda i: (0, 0))
    wide = sds((seq, width), f32)
    thin = sds((seq, width), bf16)
    tall = sds((seq, ff), bf16)
    triple = sds((seq, 3 * width), bf16)
    sums_shape = sds((8, width), f32)
    unit = 2 * seq * width

    mixed0, xhat0 = call(
        first_kernel, grid,
        [rows_w, whole_spec(norms), whole_spec(wq)],
        [rows_q, rows_w], [triple, thin], unit * 3 * width, [x, norms, wq],
    )
    pairs = width // LANES
    third = pairs // 3 if pairs % 3 == 0 else pairs
    att0, logs0 = attend(mixed0, live_cols[0], live_rows[0])
    packed = after(packed, att0)
    order, share = cube.order(), high
    if cube.count == 1 or 768 % high or high % 16:
        blocks = [packed[:, at : at + high] for at in (0, high)]
        turned = [
            jnp.take(v, jnp.asarray(order, jnp.int32) ^ cube.me, axis=0).reshape(ff, width)
            for v in blocks
        ]
        packed, share = jnp.concatenate(turned, axis=0)[None], ff
    smem = pl.BlockSpec(memory_space=pltpu.SMEM)
    anywhere = pl.BlockSpec(memory_space=pl.ANY)
    held = [pltpu.VMEM(packed.shape, bf16), pltpu.SemaphoreType.DMA((packed.shape[0],))]
    hidden0, second0, act0, slope0, later, mixed1, xhat1 = call(
        functools.partial(middle_kernel, order, share), grid,
        [smem, whole_spec(packed), rows_w, rows_w, rows_1]
        + [whole_spec(a) for a in (norms, emb, wo, wq)],
        [rows_w, rows_w, rows_f, rows_f, rows_w, rows_q, rows_w],
        [wide, thin, tall, tall, wide, triple, thin],
        unit * (4 * width + 2 * ff),
        [place, packed, att0, x, live_cols[0], norms, emb, wo, wq],
    )
    att1, logs1 = attend(mixed1, live_cols[1], live_rows[1])
    result, second1, act1, drop1, lift1, branch1, hgrad1, agrad1, sums1 = call(
        functools.partial(turn_kernel, order, share), grid,
        [smem, anywhere, rows_w, rows_w, rows_1, whole_spec(norms), rows_w]
        + [whole_spec(wo)],
        [rows_w, rows_w, rows_f, rows_w, rows_f, rows_w, rows_w, rows_w, sums_spec],
        [thin, thin, tall, thin, tall, thin, wide, thin, sums_shape],
        unit * (2 * width + 4 * ff),
        [place, packed, att1, later, live_cols[1], norms, given, wo], scratch=held,
    )
    mgrad1 = attend_back(mixed1, agrad1, att1, logs1, live_cols[1])
    drop0, lift0, branch0, hgrad0, agrad0, sums0 = call(
        functools.partial(back_kernel, order, share), grid,
        [smem, anywhere, rows_3, rows_w, rows_w, whole_spec(norms), rows_1, rows_w, rows_f]
        + [whole_spec(a) for a in (wq, wo)],
        [rows_w, rows_f, rows_w, rows_w, rows_w, sums_spec],
        [thin, tall, thin, wide, thin, sums_shape],
        unit * (4 * width + 2 * ff),
        [place, packed, mgrad1, later, hgrad1, norms, live_cols[0], hidden0, slope0, wq, wo],
        scratch=held,
    )
    chips = cube.pairs * high
    fast = len(cube.turns) == 2 and (cube.count_line * high) % LANES == 0 and high % 32 == 0
    out_own, out_other = out_grads(cube, place, branch0, branch1, att0, att1)
    up_args = (lift0, lift1, second0, second1)
    down_args = (act0, act1, drop0, drop1)

    def split_rows(v):
        start = high // 2
        return [v[:, :start], cube.turned(v[:, start:])]

    def turn_halves(halves):
        middle = cube.pairs // 2
        return [v[:middle] for v in halves], [v[middle:] for v in halves]

    if fast:
        up_other = other_grads(cube, high, *up_args, extra=[out_other])
        (up_got,) = across(cube, up_other)
        down_other = other_grads(cube, high, *down_args, hold=[up_other])
        (down_got,) = across(cube, down_other)
        made = own_grads(cube, high, *up_args, up_got, extra=[out_own], hold=[down_other])
        up_out = Scatter(cube, made[0::2], made[1::2], False)
        made = own_grads(cube, high, *down_args, down_got, hold=made)
        down = Scatter(cube, made[0::2], made[1::2], False)
    else:
        found = []
        for args, more, more_other in ((up_args, out_own, out_other), (down_args, None, None)):
            own = pair_grads(*args, 0, chips)
            if cube.inner:
                got = across(cube, pair_grads(*args, chips, chips))[0]
                own = (own.astype(f32) + got.astype(f32)).astype(bf16)
                if more is not None:
                    got = across(cube, more_other)[0]
                    more = (more.astype(f32) + got.astype(f32)).astype(bf16)
            halves = split_rows(own.reshape(cube.pairs, high, width))
            if more is not None:
                halves[0] = jnp.concatenate([halves[0], more], axis=1)
            keep, send = turn_halves(halves) if cube.turns else (halves, [])
            found.append(Scatter(cube, keep, send, False))
        up_out, down = found
        made = send
    hold = made
    groups = []
    for first in range(0, pairs, third):
        group = attend_back(
            mixed0, agrad0, att0, logs0, live_cols[0], first, third, hold, room=LATE_LIMIT
        )
        groups.append(group)
        hold = [group]
        if first == 0:
            hold = hold + up_out.step(group)
        elif first == third:
            hold = hold + down.step(group) + up_out.step(group)
        else:
            hold = hold + down.step(group) + up_out.step(group)
    own, other, small = qkv_grads(
        cube, passes, place, pass_index, groups, mgrad1, xhat0, xhat1,
        [wq, sums0, sums1], hold,
    )
    got = across(cube, other)
    if got:
        own = (own.astype(f32) + got[0].astype(f32)).astype(bf16)
    halves = split_lanes(own)
    keep, send = turn_halves(halves) if cube.turns else (halves, [])
    qkv = Scatter(cube, keep, send, True)
    hold = send
    specs_g = [
        pl.BlockSpec((3, block, a.shape[2]), lambda i: (0, i, 0)) for a in groups
    ]
    input_grad = call(
        functools.partial(last_kernel, len(groups)), grid,
        specs_g + [rows_w, rows_w, whole_spec(norms), whole_spec(wq)],
        [rows_w], [wide], unit * 3 * width,
        [*groups, x, hgrad0, norms, wq],
        hold=hold,
        room=LATE_LIMIT,
    )[0]
    qkv.step(input_grad)
    down = down.result()
    up_out = up_out.result()
    qkv = qkv.result()
    share = w_out.shape[1]
    count = w_qkv.shape[1]
    if cube.count > 1:
        half = width // 2
        ends = qkv[count : count + 8]
        small = jnp.concatenate([ends[:, :share], ends[:, half : half + share]], axis=0)
    counts = qkv[count, LANES : LANES + count]
    if cube.count == 1:
        counts = jnp.sum(
            sum(jnp.concatenate(v, axis=2) for v in (groups, [mgrad1])).astype(f32), axis=1
        ).reshape(-1)
    qkv = (qkv[:count] * norms[0:1] + counts[:, None] * norms[2:3]).T
    low_end = high // 2
    out_end = low_end + share
    up = jnp.concatenate([up_out[:low_end], up_out[out_end:]], axis=0).T
    out = up_out[low_end:out_end].T
    return (
        result[None], input_grad[None], qkv, out, up, down,
        small[:2], small[2], small[3], small[4 : 4 + passes],
    )


def solution(mesh):
    placed = (
        P(AXES, None, None),
        P(AXES),
        P(None, AXES, None),
        P(AXES),
        P(None, AXES),
        P(None, AXES),
        P(None, AXES),
        P(AXES, None),
        P(None, AXES),
        P(None, AXES),
        P(None, AXES),
        P(AXES, None, None),
    )
    return jax.shard_map(
        body,
        mesh=mesh,
        in_specs=placed,
        out_specs=(
            P(AXES, None, None),
            P(AXES, None, None),
            P(None, AXES),
            P(None, AXES),
            P(None, AXES),
            P(AXES, None),
            P(None, AXES),
            P(AXES),
            P(AXES),
            P(None, AXES),
        ),
        check_vma=False,
    )
```

```python
import functools

import jax
import jax.numpy as jnp
from jax import lax
from jax.experimental import pallas as pl
from jax.experimental.pallas import tpu as pltpu
from jax.sharding import PartitionSpec as P

HEAD = 64
LANES = 128
AXES = ("dp", "fsdp")
bf16 = jnp.bfloat16
f32 = jnp.float32

norm_epsilon = 1e-05
masked_score = -1000000000.0
curve_one = 0.7978845608028654
curve_three = 0.7978845608028654 * 0.044715

MIB = 1024 * 1024
VMEM_LIMIT = 52
LATE_LIMIT = 47


def dot_nn(left, right):
    return lax.dot_general(left, right, (((1,), (0,)), ((), ())), preferred_element_type=f32)


def dot_nt(left, right):
    return lax.dot_general(left, right, (((1,), (1,)), ((), ())), preferred_element_type=f32)


def dot_tn(left, right):
    return lax.dot_general(left, right, (((0,), (0,)), ((), ())), preferred_element_type=f32)


def normalize(values):
    center = jnp.mean(values, axis=-1, keepdims=True)
    centered = values - center
    spread = jnp.mean(centered * centered, axis=-1, keepdims=True)
    scale = lax.rsqrt(spread + norm_epsilon)
    return centered * scale, scale


def norm_back(grad, gain, xhat, scale):
    gained = grad * gain
    first = jnp.mean(gained, axis=-1, keepdims=True)
    second = jnp.mean(gained * xhat, axis=-1, keepdims=True)
    return scale * (gained - first - xhat * second)


def gelu_pair(lifted):
    square = lifted * lifted
    cubic = curve_three * square
    half = 0.5 + 0.5 * jnp.tanh(lifted * (curve_one + cubic))
    value = lifted * half
    slope = half + value * ((1.0 - half) * (2.0 * curve_one + 6.0 * cubic))
    return value, slope


def call(
    kernel, grid, in_specs, out_specs, out_shape, flops, args, scratch=(), hold=(), room=VMEM_LIMIT
):
    moved = sum(a.size * a.dtype.itemsize for a in args)
    moved += sum(o.size * o.dtype.itemsize for o in out_shape)
    given, held = len(args), len(hold)

    def run(*refs):
        kernel(*refs[:given], *refs[given + held :])

    return pl.pallas_call(
        run,
        grid=grid,
        in_specs=list(in_specs) + [pl.BlockSpec(memory_space=pl.ANY)] * held,
        out_specs=out_specs,
        out_shape=out_shape,
        scratch_shapes=list(scratch),
        compiler_params=pltpu.CompilerParams(
            dimension_semantics=("arbitrary",) * len(grid), vmem_limit_bytes=room * MIB
        ),
        cost_estimate=pl.CostEstimate(
            flops=flops, bytes_accessed=moved, transcendentals=0
        ),
    )(*args, *hold)


def rows_spec(block_rows, width):
    return pl.BlockSpec((block_rows, width), lambda i: (i, 0))


def whole_spec(array):
    zeros = (0,) * len(array.shape)
    return pl.BlockSpec(array.shape, lambda i: zeros, pipeline_mode=pl.Buffered(1))


def sds(shape, dtype):
    return jax.ShapeDtypeStruct(shape, dtype)


def head_part(x, gain, shift, w_qkv, mixed_ref, xhat_ref):
    xhat, _ = normalize(x)
    normed = (xhat * gain + shift).astype(bf16)
    xhat_ref[...] = xhat.astype(bf16)
    mixed_ref[...] = dot_nt(normed, w_qkv[...]).astype(bf16)


def first_kernel(x_ref, norms_ref, wq_ref, mixed_ref, xhat_ref):
    head_part(
        x_ref[...].astype(f32), norms_ref[0:1, :], norms_ref[2:3, :], wq_ref, mixed_ref, xhat_ref
    )


def ff_chunks(order, place_ref, packed_ref, share):
    found = []
    if share >= 768:
        for at in range(0, share, 768):
            up, down = pl.ds(at, 768), pl.ds(share + at, 768)
            found.append((lambda r=up: packed_ref[0, r, :], lambda r=down: packed_ref[0, r, :], pl.ds(at, 768)))
        return found
    per = 768 // share
    for first in range(0, len(order), per):

        def rows(at, first=first):
            return jnp.concatenate(
                [
                    packed_ref[place_ref[3] ^ mask, pl.ds(at, share), :]
                    for mask in order[first : first + per]
                ],
                axis=0,
            )

        found.append(
            (functools.partial(rows, 0), functools.partial(rows, share), pl.ds(first * share, 768))
        )
    return found


def middle_kernel(order, share, place_ref, packed_ref, *refs):
    chunks = ff_chunks(order, place_ref, packed_ref, share)
    atts, refs = refs[:-13], refs[-13:]
    (
        x_ref, live_ref, norms_ref, emb_ref, wo_ref, wq_ref,
        hidden_ref, second_ref, act_ref, slope_ref, later_ref, mixed_ref, xhat_ref,
    ) = refs
    live = live_ref[...]
    branch, at = 0.0, 0
    for ref in atts:
        branch = branch + dot_nt(ref[...], wo_ref[:, at : at + ref.shape[1]])
        at += ref.shape[1]
    hidden = x_ref[...].astype(f32) + live * branch
    hidden_ref[...] = hidden
    xhat, _ = normalize(hidden)
    second = (xhat * norms_ref[1:2, :] + norms_ref[3:4, :]).astype(bf16)
    second_ref[...] = second
    total = jnp.zeros_like(hidden)
    for up, down, to in chunks:
        value, slope = gelu_pair(dot_nt(second, up()))
        value = value.astype(bf16)
        act_ref[:, to] = value
        slope_ref[:, to] = slope.astype(bf16)
        total = total + dot_nn(value, down())
    later = hidden + live * total + emb_ref[...]
    later_ref[...] = later
    head_part(later, norms_ref[0:1, :], norms_ref[2:3, :], wq_ref, mixed_ref, xhat_ref)


def mlp_back_tail(
    grad, live, hidden, second_grad, norms_ref, wo_ref, branch_ref, hgrad_ref, agrad_ref
):
    xhat, scale = normalize(hidden)
    hgrad = grad + norm_back(second_grad, norms_ref[1:2, :], xhat, scale)
    hgrad_ref[...] = hgrad
    branch = (live * hgrad).astype(bf16)
    branch_ref[...] = branch
    agrad_ref[...] = dot_nn(branch, wo_ref[...]).astype(bf16)
    gain_sum = jnp.sum(second_grad * xhat, axis=0, keepdims=True)
    shift_sum = jnp.sum(second_grad, axis=0, keepdims=True)
    return gain_sum, shift_sum


def add_sums(sums_ref, sums):
    @pl.when(pl.program_id(0) == 0)
    def _():
        sums_ref[...] = jnp.zeros_like(sums_ref)

    for place, value in enumerate(sums):
        sums_ref[place : place + 1, :] += value


def turn_kernel(order, share, place_ref, packed_ref, *refs):
    chunks = ff_chunks(order, place_ref, packed_ref, share)
    (
        att_ref, x_ref, live_ref, norms_ref, grad_ref, wo_ref,
        out_ref, second_ref, act_ref, drop_ref, lift_ref, branch_ref, hgrad_ref, agrad_ref, sums_ref,
    ) = refs
    live = live_ref[...]
    hidden = x_ref[...] + live * dot_nt(att_ref[...], wo_ref[...])
    xhat, _ = normalize(hidden)
    second = (xhat * norms_ref[1:2, :] + norms_ref[3:4, :]).astype(bf16)
    second_ref[...] = second
    grad = grad_ref[...]
    drop = (live * grad).astype(bf16)
    drop_ref[...] = drop
    total = jnp.zeros_like(hidden)
    second_grad = jnp.zeros_like(hidden)
    for up, down, to in chunks:
        up, down = up(), down()
        value, slope = gelu_pair(dot_nt(second, up))
        value = value.astype(bf16)
        act_ref[:, to] = value
        total = total + dot_nn(value, down)
        lift = (dot_nt(drop, down) * slope).astype(bf16)
        lift_ref[:, to] = lift
        second_grad = second_grad + dot_nn(lift, up)
    out_ref[...] = (hidden + live * total).astype(bf16)
    sums = mlp_back_tail(
        grad, live, hidden, second_grad, norms_ref, wo_ref, branch_ref, hgrad_ref, agrad_ref
    )
    add_sums(sums_ref, sums)


def head_back(mixed_grad_refs, wq_ref, x, hgrad, norms_ref):
    width = x.shape[1]
    normed_grad = jnp.zeros_like(x)
    for part in range(3):
        at = part * width
        for ref in mixed_grad_refs:
            normed_grad += dot_nn(ref[part], wq_ref[at : at + ref.shape[2], :])
            at += ref.shape[2]
    xhat, scale = normalize(x)
    return hgrad + norm_back(normed_grad, norms_ref[0:1, :], xhat, scale)


def back_kernel(order, share, place_ref, packed_ref, *refs):
    chunks = ff_chunks(order, place_ref, packed_ref, share)
    (
        mgrad_ref, later_ref, hgrad1_ref, norms_ref, live_ref, hidden_ref, slope_ref, wq_ref, wo_ref,
        drop_ref, lift_ref, branch_ref, hgrad_ref, agrad_ref, sums_ref,
    ) = refs
    grad = head_back([mgrad_ref], wq_ref, later_ref[...], hgrad1_ref[...], norms_ref)
    table_sum = jnp.sum(grad, axis=0, keepdims=True)
    live = live_ref[...]
    drop = (live * grad).astype(bf16)
    drop_ref[...] = drop
    second_grad = jnp.zeros_like(grad)
    for up, down, to in chunks:
        lift = (dot_nt(drop, down()) * slope_ref[:, to].astype(f32)).astype(bf16)
        lift_ref[:, to] = lift
        second_grad = second_grad + dot_nn(lift, up())
    sums = mlp_back_tail(
        grad, live, hidden_ref[...], second_grad, norms_ref, wo_ref, branch_ref, hgrad_ref, agrad_ref
    )
    add_sums(sums_ref, sums + (table_sum,))


def last_kernel(groups, *refs):
    mgrad_refs, (x_ref, hgrad_ref, norms_ref, wq_ref, out_ref) = refs[:groups], refs[groups:]
    out_ref[...] = head_back(
        mgrad_refs, wq_ref, x_ref[...].astype(f32), hgrad_ref[...], norms_ref
    )


def both_layers(left0, left1, right0, right1):
    return dot_tn(left0[...], right0[...]) + dot_tn(left1[...], right1[...])


def pair_grad_kernel(left0, left1, right0, right1, out_ref):
    out_ref[...] = both_layers(left0, left1, right0, right1).astype(bf16)


def pair_grads(left0, left1, right0, right1, start, size, hold=()):
    tokens = left0.shape[0]
    width = right0.shape[1]
    step = 384 if size % 384 == 0 else size
    first = start // step
    cols = pl.BlockSpec((tokens, step), lambda i: (0, first + i))
    return call(
        pair_grad_kernel,
        (size // step,),
        [cols] * 2 + [whole_spec(right0)] * 2,
        [rows_spec(step, width)],
        [sds((size, width), bf16)],
        4 * tokens * size * width,
        [left0, left1, right0, right1],
        hold=hold, room=LATE_LIMIT,
    )[0]


def blocks_spec(shape, index):
    return pl.BlockSpec(shape, lambda i: (index(i), 0, 0))


def other_grad_kernel(high, left0, left1, right0, right1, *refs):
    extra, out_ref = refs[:-1], refs[-1]
    total = both_layers(left0, left1, right0, right1).astype(bf16)
    for place in range(out_ref.shape[0]):
        out_ref[place, :high, :] = total[place * high : (place + 1) * high]
        for ref in extra:
            out_ref[place, high:, :] = ref[place]


def other_grads(cube, high, left0, left1, right0, right1, extra=(), hold=()):
    tokens = left0.shape[0]
    width = right0.shape[1]
    lines, turns = cube.count_line, cube.count_turns
    first = turns
    cols = pl.BlockSpec((tokens, lines * high), lambda i: (0, first + i))
    rows = high + sum(a.shape[1] for a in extra)
    return call(
        functools.partial(other_grad_kernel, high),
        (turns,),
        [cols] * 2
        + [whole_spec(right0)] * 2
        + [blocks_spec((lines,) + a.shape[1:], lambda i: i) for a in extra],
        [blocks_spec((lines, rows, width), lambda i: i)],
        [sds((cube.pairs, rows, width), bf16)],
        4 * tokens * cube.pairs * high * width,
        [left0, left1, right0, right1, *extra],
        hold=hold, room=LATE_LIMIT,
    )[0]


def own_grad_kernel(high, left0, left1, right0, right1, got, *refs):
    extra, (low_keep, low_send, late_keep, late_send) = refs[:-4], refs[-4:]
    middle = high // 2
    half = pl.num_programs(0) // 2
    step = pl.program_id(0)
    total = both_layers(left0, left1, right0, right1)

    def low_part(ref):
        for place in range(ref.shape[0]):
            at = place * high
            ref[place, :middle, :] = (
                total[at : at + middle] + got[place, :middle, :].astype(f32)
            ).astype(bf16)
            for more in extra:
                ref[place, middle:, :] = (
                    more[place].astype(f32) + got[place, high:, :].astype(f32)
                ).astype(bf16)

    def late_part(ref):
        for place in range(ref.shape[0]):
            at = place * high
            ref[place] = (
                total[at + middle : at + high] + got[place, middle:high, :].astype(f32)
            ).astype(bf16)

    @pl.when(step < half)
    def _():
        low_part(low_keep)

    @pl.when(step >= half)
    def _():
        low_part(low_send)

    @pl.when(step % 2 == 0)
    def _():
        late_part(late_keep)

    @pl.when(step % 2 == 1)
    def _():
        late_part(late_send)


def own_grads(cube, high, left0, left1, right0, right1, got, extra=(), hold=()):
    tokens = left0.shape[0]
    width = right0.shape[1]
    lines, turns = cube.count_line, cube.count_turns
    half = turns // 2
    cols = pl.BlockSpec((tokens, lines * high), lambda i: (0, i))
    low = high // 2 + sum(a.shape[1] for a in extra)
    late = high - high // 2

    def turned(i):
        found = 0
        for bit in range(1, turns.bit_length() - 1):
            found = found + (((i >> bit) & 1) << (turns.bit_length() - 2 - bit))
        return found

    def first_keep(i):
        return jnp.minimum(i, half - 1)

    def first_send(i):
        return jnp.maximum(i - half, 0)

    return call(
        functools.partial(own_grad_kernel, high),
        (turns,),
        [cols] * 2
        + [whole_spec(right0)] * 2
        + [blocks_spec((lines,) + a.shape[1:], lambda i: i) for a in (got, *extra)],
        [
            blocks_spec((lines, low, width), first_keep),
            blocks_spec((lines, low, width), first_send),
            blocks_spec((lines, late, width), turned),
            blocks_spec((lines, late, width), turned),
        ],
        [sds((cube.pairs // 2, n, width), bf16) for n in (low, low, late, late)],
        4 * tokens * cube.pairs * high * width,
        [left0, left1, right0, right1, got, *extra],
        hold=hold, room=LATE_LIMIT,
    )


def place_blocks(cube, place_ref, total_ref, own_ref, other_ref):
    rows = own_ref.shape[1]
    for chip in range(own_ref.shape[0]):
        if cube.inner == 0:
            own_ref[0] = total_ref[...].astype(bf16)
            continue
        even = total_ref[pl.ds(2 * chip * rows, rows), :].astype(bf16)
        odd = total_ref[pl.ds((2 * chip + 1) * rows, rows), :].astype(bf16)
        first = place_ref[2] == 0
        at = cube.place(2 * chip, 0) ^ place_ref[0]
        own_ref[at] = jnp.where(first, even, odd)
        other_ref[at] = jnp.where(first, odd, even)


def out_grad_kernel(cube, place_ref, left0, left1, right0, right1, own_ref, other_ref, total_ref):
    total_ref[...] = both_layers(left0, left1, right0, right1)
    place_blocks(cube, place_ref, total_ref, own_ref, other_ref)


def block_shapes(cube, rows, width):
    shape = (cube.pairs, rows, width)
    return [sds(shape, bf16)] * 2, [pl.BlockSpec(shape, lambda i: (0, 0, 0))] * 2


def out_grads(cube, place, left0, left1, right0, right1, hold=()):
    tokens, high = left0.shape
    width = right1.shape[1]
    shapes, specs = block_shapes(cube, high // cube.count, width)
    args = [left0, left1, right0, right1]
    return call(
        functools.partial(out_grad_kernel, cube),
        (1,),
        [pl.BlockSpec(memory_space=pltpu.SMEM)] + [whole_spec(a) for a in args],
        specs,
        shapes,
        4 * tokens * high * width,
        [place, *args],
        scratch=[pltpu.VMEM((high, width), f32)],
        hold=hold, room=LATE_LIMIT,
    )


def qkv_grad_kernel(cube, groups, passes, place_ref, pass_ref, *refs):
    lefts0, refs = refs[:groups], refs[groups:]
    left1, right0, right1, wq_ref, sums0_ref, sums1_ref, own_ref, other_ref = refs[:8]
    small_ref, total_ref, count_ref = refs[8:]
    part = pl.program_id(0)
    high = left1.shape[2]
    width = right0.shape[1]
    row = lax.broadcasted_iota(jnp.int32, (8, 1), 0)

    @pl.when(part == 0)
    def _():
        small_ref[...] = jnp.zeros_like(small_ref)
        small_ref[1:2, :] = sums0_ref[0:1, :] + sums1_ref[0:1, :]
        small_ref[3:4, :] = sums0_ref[1:2, :] + sums1_ref[1:2, :]
        for index in range(passes):
            small_ref[4 + index : 5 + index, :] = jnp.where(
                pass_ref[0] == index, sums0_ref[2:3, :], 0.0
            )

    at = 0
    gain_sum = jnp.zeros((1, width), f32)
    shift_sum = jnp.zeros((1, width), f32)
    for left0 in lefts0:
        to = pl.ds(at, left0.shape[2])
        rows = pl.ds(pl.multiple_of(part * high + at, 8), left0.shape[2])
        total = dot_tn(left0[0], right0[...]) + dot_tn(left1[0, :, to], right1[...])
        total_ref[rows, :] = total
        sums = jnp.sum(left0[0].astype(f32) + left1[0, :, to].astype(f32), axis=0, keepdims=True)
        count_ref[pl.ds(part, 1), to] = sums
        terms = split_three(jnp.broadcast_to(sums, (8, left0.shape[2])))
        three = jnp.where(row == 0, terms[0], jnp.where(row == 1, terms[1], terms[2]))
        three = jnp.where(row < 3, three, jnp.zeros_like(three))
        weights = wq_ref[to, :]
        gain_sum += jnp.sum(total * weights.astype(f32), axis=0, keepdims=True)
        shift_sum += jnp.sum(dot_nn(three, weights), axis=0, keepdims=True)
        at += left0.shape[2]
    small_ref[0:1, :] += gain_sum
    small_ref[2:3, :] += shift_sum

    @pl.when(part == pl.num_programs(0) - 1)
    def _():
        extra = 8
        rows = own_ref.shape[1] - extra
        share = width // cube.count
        half = width // 2
        small = small_ref[...]
        counts = jnp.concatenate([count_ref[p : p + 1, :] for p in range(3)], axis=1)
        counts = jnp.broadcast_to(counts, (8, counts.shape[1]))
        for chip in range(cube.pairs):
            found = []
            for device in range(2 * chip, 2 * chip + 1 + (cube.inner > 0)):
                block = total_ref[pl.ds(device * rows, rows), :]
                line, own = small, counts
                if device:
                    line = pltpu.roll(small, width - device * share, 1)
                    own = pltpu.roll(counts, counts.shape[1] - device * rows, 1)
                line = [line[:8, :LANES], own[:, : half - LANES], line[8:, :half]]
                line = jnp.concatenate(line, axis=1)
                found.append(jnp.concatenate([block, line], axis=0).astype(bf16))
            if cube.inner == 0:
                own_ref[0] = found[0]
                continue
            first = place_ref[2] == 0
            own = jnp.where(first, found[0], found[1])
            other = jnp.where(first, found[1], found[0])
            for order in range(2):
                lanes = slice(order * half, (order + 1) * half)
                at = cube.place(2 * chip, order) ^ place_ref[order]
                own_ref[at, :, lanes] = own[:, lanes]
                other_ref[at, :, lanes] = other[:, lanes]


def qkv_grads(cube, passes, place, pass_index, lefts0, left1, right0, right1, kept, hold=()):
    parts, tokens, high = left1.shape
    width = right0.shape[1]
    specs = [
        pl.BlockSpec((1, tokens, a.shape[2]), lambda i: (i, 0, 0)) for a in (*lefts0, left1)
    ]
    shapes, out_specs = block_shapes(cube, parts * high // cube.count + 8, width)
    return call(
        functools.partial(qkv_grad_kernel, cube, len(lefts0), passes),
        (parts,),
        [pl.BlockSpec(memory_space=pltpu.SMEM)] * 2
        + specs
        + [whole_spec(a) for a in (right0, right1)]
        + [rows_spec(high, width)]
        + [whole_spec(a) for a in kept[1:]],
        out_specs + [pl.BlockSpec((16, width), lambda i: (0, 0))],
        shapes + [sds((16, width), f32)],
        4 * tokens * parts * high * width,
        [place, pass_index, *lefts0, left1, right0, right1, *kept],
        scratch=[pltpu.VMEM((parts * high, width), f32), pltpu.VMEM((8, high), f32)],
        hold=hold,
        room=LATE_LIMIT,
    )


def lane_index(shape):
    return lax.broadcasted_iota(jnp.int32, shape, len(shape) - 1)


def split_three(values):
    high = values.astype(bf16)
    rest = values - high.astype(f32)
    middle = rest.astype(bf16)
    low = (rest - middle.astype(f32)).astype(bf16)
    return high, middle, low


def own_lanes(lane, head):
    return (lane < HEAD) if head == 0 else (lane >= HEAD)


def attend_kernel(
    block, q_ref, k_ref, v_ref, live_col_ref, live_row_ref, out_ref, logs_ref, mask_ref
):
    seq = q_ref.shape[0]
    count = seq // block

    @pl.when(pl.program_id(0) == 0)
    def _():
        query = lax.broadcasted_iota(jnp.int32, (block, block), 0)
        key = lax.broadcasted_iota(jnp.int32, (block, block), 1)
        for i in range(count):
            alive = live_row_ref[:, i * block : (i + 1) * block] > 0.5
            visible = (key <= query) & (alive | (key == query))
            mask_ref[i] = jnp.where(visible, 0.0, masked_score)

    lane = lane_index((seq, LANES))
    q = q_ref[...] * 0.125
    k = k_ref[...]
    v = v_ref[...]
    bias = ((live_col_ref[...] - 1.0) * 1e9).astype(bf16)
    zero = jnp.zeros((seq, LANES), bf16)
    one = jnp.ones((seq, LANES), bf16)
    parts = []
    for head in range(2):
        mine = own_lanes(lane, head)
        spare = (1 - head) * HEAD
        parts.append(
            (
                jnp.where(mine, q, zero),
                jnp.where(mine, q, jnp.where(lane == spare, one, zero)),
                jnp.where(mine, k, jnp.where(lane == spare, bias, zero)),
                jnp.where(mine, v, one),
            )
        )
    low = lane_index((block, LANES)) < HEAD

    def score(i, head):
        at, before = slice(i * block, (i + 1) * block), slice(0, i * block)
        q_plain, q_bias, k_bias, _ = parts[head]
        diag = dot_nt(q_plain[at], k[at]) + mask_ref[i]
        return diag, dot_nt(q_bias[at], k_bias[before]) if i > 0 else None

    def soften(diag, off):
        top = jnp.max(diag, axis=-1, keepdims=True)
        if off is None:
            return top, jnp.exp(diag - top).astype(bf16), None
        top = jnp.maximum(top, jnp.max(off, axis=-1, keepdims=True))
        return top, jnp.exp(diag - top).astype(bf16), jnp.exp(off - top).astype(bf16)

    def finish(i, head, top, diag, off):
        at, before = slice(i * block, (i + 1) * block), slice(0, i * block)
        v_ones = parts[head][3]
        total = dot_nn(diag, v_ones[at])
        if i > 0:
            total += dot_nn(off, v_ones[before])
        spare = (1 - head) * HEAD
        weight = total[:, spare : spare + 1]
        found.append((total * (1.0 / weight), top + jnp.log(weight)))
        if head == 1:
            (out0, log0), (out1, log1) = found[-2:]
            out_ref[at, :] = jnp.where(low, out0, out1).astype(bf16)
            logs_ref[at, :] = jnp.where(low, log0, log1)

    found = []
    steps = [(i, head) for i in range(count) for head in range(2)]
    ahead, behind = score(*steps[0]), None
    for place, step in enumerate(steps):
        scored = ahead
        if place + 1 < len(steps):
            ahead = score(*steps[place + 1])
        softened = soften(*scored)
        if behind is not None:
            finish(*steps[place - 1], *behind)
        behind = softened
    finish(*steps[-1], *behind)


def attend(mixed, live_col, live_row, first=0, count=None, hold=(), block=256):
    seq, triple = mixed.shape
    pairs = triple // 3 // LANES
    count = pairs if count is None else count
    width = count * LANES
    block = min(block, seq)

    def cols(offset):
        return pl.BlockSpec((seq, LANES), lambda h: (0, offset + h))

    return call(
        functools.partial(attend_kernel, block),
        (count,),
        [cols(first), cols(first + pairs), cols(first + 2 * pairs), whole_spec(live_col), whole_spec(live_row)],
        [cols(0), cols(0)],
        [sds((seq, width), bf16), sds((seq, width), f32)],
        4 * seq * seq * width,
        [mixed, mixed, mixed, live_col, live_row],
        scratch=[pltpu.VMEM((seq // block, block, block), f32)],
        hold=hold, room=VMEM_LIMIT,
    )


def attend_back_kernel(
    block, q_ref, k_ref, v_ref, grad_ref, att_ref, logs_ref, live_col_ref, out_ref,
    mask_ref, dk_ref, dv_ref,
):
    seq = q_ref.shape[0]
    count = seq // block

    @pl.when(pl.program_id(0) == 0)
    def _():
        key = lax.broadcasted_iota(jnp.int32, (block, block), 0)
        query = lax.broadcasted_iota(jnp.int32, (block, block), 1)
        for i in range(count):
            alive = live_col_ref[i * block : (i + 1) * block, :] > 0.5
            visible = (key <= query) & (alive | (key == query))
            mask_ref[i] = jnp.where(visible, 0.0, masked_score)

    lane = lane_index((seq, LANES))
    q = q_ref[...] * 0.125
    k = k_ref[...]
    v = v_ref[...]
    grad = grad_ref[...]
    logs = logs_ref[...]
    dots = grad.astype(f32) * att_ref[...].astype(f32)
    bias = ((live_col_ref[...] - 1.0) * 1e9).astype(bf16)
    zero = jnp.zeros((seq, LANES), bf16)
    one = jnp.ones((seq, LANES), bf16)
    parts = []
    for head in range(2):
        mine = own_lanes(lane, head)
        spare = (1 - head) * HEAD
        log_terms = split_three(-logs[:, head * HEAD : head * HEAD + 1])
        dot_terms = split_three(-jnp.sum(jnp.where(mine, dots, 0.0), axis=-1, keepdims=True))
        q_more, k_more, k_diag, g_more, v_more = (
            jnp.where(lane == spare, one, zero),
            jnp.where(lane == spare, bias, zero),
            zero,
            zero,
            zero,
        )
        for place in range(3):
            here = lane == spare + 1 + place
            q_more = jnp.where(here, log_terms[place], q_more)
            k_more = jnp.where(here, one, k_more)
            k_diag = jnp.where(here, one, k_diag)
            g_more = jnp.where(here, dot_terms[place], g_more)
            v_more = jnp.where(here, one, v_more)
        parts.append(
            dict(
                q=jnp.where(mine, q, q_more),
                k=jnp.where(mine, k, k_more),
                kd=jnp.where(mine, k, k_diag),
                g=jnp.where(mine, grad, g_more),
                v=jnp.where(mine, v, v_more),
                q0=jnp.where(mine, q, zero),
                k0=jnp.where(mine, k, zero),
                g0=jnp.where(mine, grad, zero),
            )
        )
    def rows(i):
        return slice(i * block, (i + 1) * block)

    def score(i, j, head):
        part = parts[head]
        first = dot_nt(part["kd" if j == i else "k"][rows(j)], part["q"][rows(i)])
        return first, dot_nt(part["v"][rows(j)], part["g"][rows(i)])

    def soften(i, j, head, scores, change):
        if j == i:
            scores = scores + mask_ref[i]
        soft = jnp.exp(scores)
        return soft.astype(bf16), (soft * change).astype(bf16)

    def add(name, value):
        totals[name] = totals[name] + value if name in totals else value

    def finish(i, j, head, soft, change):
        part = parts[head]
        add("v", dot_nn(soft, part["g0"][rows(i)]))
        add("k", dot_nn(change, part["q0"][rows(i)]))
        add("q", dot_tn(change, part["k0"][rows(j)]))
        if head == 1:
            for name, ref in (("v", dv_ref), ("k", dk_ref)):
                if j == i:
                    ref[rows(j), :] = totals.pop(name)
                else:
                    ref[rows(j), :] += totals.pop(name)
            if j == i:
                out_ref[0, rows(i), :] = (totals.pop("q") * 0.125).astype(bf16)

    totals = {}
    steps = [(i, j, head) for i in range(count) for j in range(i + 1) for head in range(2)]
    ahead, behind = score(*steps[0]), None
    for place, step in enumerate(steps):
        scored = ahead
        if place + 1 < len(steps):
            ahead = score(*steps[place + 1])
        softened = soften(*step, *scored)
        if behind is not None:
            finish(*steps[place - 1], *behind)
        behind = softened
    finish(*steps[-1], *behind)
    out_ref[1] = dk_ref[...].astype(bf16)
    out_ref[2] = dv_ref[...].astype(bf16)


def attend_back(mixed, att_grad, att, logs, live_col, first=0, count=None, hold=(), block=256, room=VMEM_LIMIT):
    seq, triple = mixed.shape
    pairs = triple // 3 // LANES
    count = pairs if count is None else count
    width = count * LANES
    block = min(block, seq)

    def cols(offset):
        return pl.BlockSpec((seq, LANES), lambda h: (0, offset + h))

    return call(
        functools.partial(attend_back_kernel, block),
        (count,),
        [cols(first), cols(first + pairs), cols(first + 2 * pairs)]
        + [cols(first), cols(first), cols(first), whole_spec(live_col)],
        [pl.BlockSpec((3, seq, LANES), lambda h: (0, 0, h))],
        [sds((3, seq, width), bf16)],
        10 * seq * seq * width,
        [mixed, mixed, mixed, att_grad, att, logs, live_col],
        scratch=[
            pltpu.VMEM((seq // block, block, block), f32),
            pltpu.VMEM((seq, LANES), f32),
            pltpu.VMEM((seq, LANES), f32),
        ],
        hold=hold, room=room,
    )[0]


def all_masks(bits):
    masks = [0]
    for bit in bits:
        masks += [m | (1 << bit) for m in masks]
    return masks


class Cube:
    def __init__(self):
        inner = lax.axis_size(AXES[1])
        self.count = lax.axis_size(AXES[0]) * inner
        self.bits = self.count.bit_length() - 1
        self.inner = inner.bit_length() - 1
        self.pairs = self.count >> (self.inner > 0)
        self.me = lax.axis_index(AXES)
        self.outer = list(range(self.inner, self.bits))
        self.rest = list(range(1, self.inner))
        self.turns = list(zip(self.outer, self.outer[::-1]))
        self.count_turns = 1 << len(self.outer)
        self.count_line = 1 << len(self.rest)

    def send(self, value, mask):
        return lax.ppermute(value, AXES, [(d, d ^ mask) for d in range(self.count)])

    def send_all(self, value, bits):
        return [self.send(value, mask) for mask in all_masks(bits)[1:]]

    def place(self, device, order):
        bits = [pair[order] for pair in self.turns] + self.rest[::-1]
        found = 0
        for bit in bits:
            found = found * 2 + ((device >> bit) & 1)
        return found

    def places(self):
        return jnp.stack([self.place(self.me, 0), self.place(self.me, 1), self.me & 1, self.me])

    def order(self):
        return sorted(range(self.count), key=lambda d: (d & (self.inner > 0), self.place(d, 0)))

    def turned(self, value):
        count = len(self.turns)
        shape = value.shape
        value = value.reshape((2,) * count + (-1,) + shape[1:])
        axes = tuple(range(count))[::-1] + tuple(range(count, value.ndim))
        return value.transpose(axes).reshape(shape)


class Gather:
    def __init__(self, cube, block, split):
        self.cube, self.split = cube, split
        self.value = block[None]

    def line(self, make=None):
        got = self.cube.send_all(self.value, self.cube.rest)
        if make is not None:
            got = after(got, make)
        self.value = jnp.concatenate([self.value, *got], axis=0)
        self.halves = self.split(self.value)
        self.turns = self.cube.turns[::-1]
        return self.value

    def turn(self, *others):
        if self.turns:
            bits = self.turns.pop(0)
            got = [self.cube.send(v, 1 << bit) for v, bit in zip(self.halves, bits)]
            if others:
                got = after(got, others)
            self.halves = [jnp.concatenate(pair, axis=0) for pair in zip(self.halves, got)]
        return self.halves


def after(value, others):
    return lax.optimization_barrier((value, others))[0]


def across(cube, value):
    return [cube.send(value, 1)] if cube.inner else []


def turn_sum_kernel(count, *refs):
    for half in range(count):
        keep, got = refs[2 * half], refs[2 * half + 1]
        first, second = refs[2 * count + 2 * half], refs[2 * count + 2 * half + 1]
        total = (keep[...].astype(f32) + got[...].astype(f32)).astype(bf16)
        middle = first.shape[0]
        first[...] = total[:middle]
        second[...] = total[middle:]


def join_kernel(lanes, *refs):
    low, low_got, late, late_got = refs[:4]
    for place, out in enumerate(refs[4:]):
        first = (low[place].astype(f32) + low_got[place].astype(f32)).astype(bf16)
        second = (late[place].astype(f32) + late_got[place].astype(f32)).astype(bf16)
        if lanes:
            out[:, : first.shape[1]] = first
            out[:, first.shape[1] :] = second
        else:
            out[: first.shape[0], :] = first
            out[first.shape[0] :, :] = second


def core_sum_kernel(own, got, *outs):
    middle, _, half = outs[0].shape
    for order in range(2):
        for part in range(2):
            at = (slice(part * middle, (part + 1) * middle), slice(None), slice(order * half, (order + 1) * half))
            outs[2 * order + part][...] = (own[at].astype(f32) + got[at].astype(f32)).astype(bf16)


class Scatter:
    def __init__(self, cube, keep, send, lanes):
        self.cube, self.keep, self.sent, self.lanes = cube, list(keep), list(send), lanes
        self.todo = list(cube.turns)
        self.got, self.total = [], None
        if self.todo:
            self.go()
        else:
            self.total = jnp.concatenate(self.keep, axis=2 if lanes else 1)[0].astype(f32)

    def go(self):
        bits = self.todo.pop(0)
        self.got = [self.cube.send(v, 1 << bit) for v, bit in zip(self.sent, bits)]
        self.last = not self.todo

    def step(self, *others):
        if self.total is not None:
            return []
        got = after(self.got, others) if others else self.got
        if self.sent is None:
            total = self.keep.astype(f32)
            for other in got:
                total = total + other.astype(f32)
            self.total = total
            return [total]
        pairs = [v for pair in zip(self.keep, got) for v in pair]
        small = all(v.shape[1] % 16 == 0 or v.shape[1] == 72 for v in self.keep)
        if not self.last:
            middle = self.keep[0].shape[0] // 2
            if small:
                shapes = [sds((middle,) + v.shape[1:], bf16) for v in self.keep for _ in range(2)]
                made = call(
                    functools.partial(turn_sum_kernel, 2), (1,), [whole_spec(v) for v in pairs],
                    [whole_spec(v) for v in shapes], shapes, 0, pairs, room=24,
                )
            else:
                made = []
                for keep, other in zip(self.keep, got):
                    total = (keep.astype(f32) + other.astype(f32)).astype(bf16)
                    made += [total[:middle], total[middle:]]
            self.keep, self.sent = list(made[0::2]), list(made[1::2])
            self.go()
            return self.sent
        masks = all_masks(self.cube.rest)
        if small:
            first, second = [v.shape[1:] for v in self.keep]
            shape = (first[0], first[1] + second[1]) if self.lanes else (first[0] + second[0], first[1])
            shapes = [sds(shape, bf16)] * len(masks)
            made = call(
                functools.partial(join_kernel, self.lanes), (1,), [whole_spec(v) for v in pairs],
                [whole_spec(v) for v in shapes], shapes, 0, pairs, room=24,
            )
        else:
            total = [
                (a.astype(f32) + b.astype(f32)).astype(bf16) for a, b in zip(self.keep, got)
            ]
            total = jnp.concatenate(total, axis=2 if self.lanes else 1)
            made = [total[i] for i in range(len(masks))]
        self.keep, sent = made[0], list(made[1:])
        self.got = [self.cube.send(v, mask) for v, mask in zip(sent, masks[1:])]
        self.sent = None
        return sent

    def result(self):
        while self.total is None:
            self.step()
        return self.total


def after(value, others):
    return lax.optimization_barrier((value, others))[0]


def across(cube, value):
    return [cube.send(value, 1)] if cube.inner else []


def set_down_kernel(cube, sizes, share, place_ref, pass_ref, *refs):
    sources, (wq_ref, wo_ref, norms_ref, emb_ref) = refs[:-4], refs[-4:]
    per = len(sources) // 2
    half = wq_ref.shape[2] // 2
    mid = sizes[0] + sizes[1]
    extra = sources[0].shape[1] - mid
    row = lax.broadcasted_iota(jnp.int32, (extra, 1), 0)
    picked = (row < 8) | (row == 8 + pass_ref[0])
    empty = jnp.zeros((extra, half), f32)
    small = jnp.zeros((extra, 2 * half), f32)
    for device in range(cube.count):
        for order in range(2):
            at = cube.place(device, order) ^ place_ref[order]
            block = sources[order * per][at]
            if per > 1:
                own = ((device & 1) ^ place_ref[2]) == 0
                block = jnp.where(own, block, sources[order * per + 1][at])
            block = block.astype(f32)
            lanes = slice(order * half, (order + 1) * half)
            wq_ref[device, :, lanes] = block[: sizes[0]].astype(bf16)
            wo_ref[device, :, lanes] = block[sizes[0] : mid].astype(bf16)
            if order * half < share:
                line = [jnp.where(picked, block[mid:], 0.0), empty]
                line = jnp.concatenate(line[::-1] if order else line, axis=1)
                small = small + (pltpu.roll(line, device * share, 1) if device else line)
    norms_ref[...] = small[:8]
    emb_ref[...] = jnp.sum(small[8:], axis=0, keepdims=True)


def set_down(cube, place, pass_index, sources, sizes, share):
    width = 2 * sources[0].shape[2]
    shapes = [(cube.count, n, width) for n in sizes]
    wq, wo, norms, emb = call(
        functools.partial(set_down_kernel, cube, sizes, share), (1,),
        [pl.BlockSpec(memory_space=pltpu.SMEM)] * 2 + [whole_spec(a) for a in sources],
        [pl.BlockSpec(n, lambda i: (0, 0, 0)) for n in shapes]
        + [pl.BlockSpec((n, width), lambda i: (0, 0)) for n in (8, 1)],
        [sds(n, bf16) for n in shapes] + [sds((n, width), f32) for n in (8, 1)], 0,
        [place, pass_index, *sources],
    )
    return wq.reshape(-1, width), wo.reshape(-1, width), norms, emb


def body(
    tokens, row_lengths, live_mask, pass_index,
    w_qkv, w_out, w_up, w_down, norm_gains, norm_shifts, pass_table, cotangent,
):
    _, seq, width = tokens.shape
    cube = Cube()
    place = cube.places()
    ff = w_up.shape[1] * cube.count
    block = min(256, seq)
    grid = (seq // block,)
    passes = pass_table.shape[0]

    def split_lanes(v):
        half = v.shape[2] // 2
        return [v[:, :, :half], v[:, :, half:]]

    high = w_up.shape[1]
    share = w_out.shape[1]

    def wide_rows(v):
        return jnp.pad(v, ((0, -v.shape[0] % 8), (0, width - v.shape[1])))

    packed = jnp.concatenate([w_up.T, w_down], axis=0)
    packed = lax.all_gather(packed, AXES, axis=0, tiled=False)

    gains_shifts = wide_rows(jnp.concatenate([norm_gains, norm_shifts], axis=0))
    early = [w_qkv.T, w_out.T, gains_shifts, wide_rows(pass_table)]
    part_q = Gather(cube, jnp.concatenate(early, axis=0), split_lanes)
    part_q.line()
    for _ in cube.turns:
        part_q.turn()
    low, late = part_q.halves
    sources = [low, *across(cube, low), late, *across(cube, late)]
    sizes = (w_qkv.shape[1], w_out.shape[1])
    wq, wo, norms, emb = set_down(cube, place, pass_index, sources, sizes, share)

    positions = jnp.arange(seq, dtype=jnp.int32)
    inside = positions < row_lengths[0]
    live = jnp.where(inside[None, :] & (live_mask[:, 0] > 0), 1.0, 0.0).astype(f32)
    live_cols = [live[0][:, None], live[1][:, None]]
    live_rows = [live[0][None, :], live[1][None, :]]

    x = tokens[0]
    given = cotangent[0]
    rows_w = rows_spec(block, width)
    rows_f = rows_spec(block, ff)
    rows_q = rows_spec(block, 3 * width)
    rows_1 = rows_spec(block, 1)
    rows_3 = pl.BlockSpec((3, block, width), lambda i: (0, i, 0))
    sums_spec = pl.BlockSpec((8, width), lambda i: (0, 0))
    wide = sds((seq, width), f32)
    thin = sds((seq, width), bf16)
    tall = sds((seq, ff), bf16)
    triple = sds((seq, 3 * width), bf16)
    sums_shape = sds((8, width), f32)
    unit = 2 * seq * width

    mixed0, xhat0 = call(
        first_kernel, grid,
        [rows_w, whole_spec(norms), whole_spec(wq)],
        [rows_q, rows_w], [triple, thin], unit * 3 * width, [x, norms, wq],
    )
    pairs = width // LANES
    third = pairs // 3 if pairs % 3 == 0 else pairs
    att0, logs0 = attend(mixed0, live_cols[0], live_rows[0])
    packed = after(packed, att0)
    order, share = cube.order(), high
    if cube.count == 1 or 768 % high or high % 16:
        blocks = [packed[:, at : at + high] for at in (0, high)]
        turned = [
            jnp.take(v, jnp.asarray(order, jnp.int32) ^ cube.me, axis=0).reshape(ff, width)
            for v in blocks
        ]
        packed, share = jnp.concatenate(turned, axis=0)[None], ff
    smem = pl.BlockSpec(memory_space=pltpu.SMEM)
    hidden0, second0, act0, slope0, later, mixed1, xhat1 = call(
        functools.partial(middle_kernel, order, share), grid,
        [smem, whole_spec(packed), rows_w, rows_w, rows_1]
        + [whole_spec(a) for a in (norms, emb, wo, wq)],
        [rows_w, rows_w, rows_f, rows_f, rows_w, rows_q, rows_w],
        [wide, thin, tall, tall, wide, triple, thin],
        unit * (4 * width + 2 * ff),
        [place, packed, att0, x, live_cols[0], norms, emb, wo, wq],
    )
    att1, logs1 = attend(mixed1, live_cols[1], live_rows[1])
    result, second1, act1, drop1, lift1, branch1, hgrad1, agrad1, sums1 = call(
        functools.partial(turn_kernel, order, share), grid,
        [smem, whole_spec(packed), rows_w, rows_w, rows_1, whole_spec(norms), rows_w]
        + [whole_spec(wo)],
        [rows_w, rows_w, rows_f, rows_w, rows_f, rows_w, rows_w, rows_w, sums_spec],
        [thin, thin, tall, thin, tall, thin, wide, thin, sums_shape],
        unit * (2 * width + 4 * ff),
        [place, packed, att1, later, live_cols[1], norms, given, wo],
    )
    mgrad1 = attend_back(mixed1, agrad1, att1, logs1, live_cols[1])
    drop0, lift0, branch0, hgrad0, agrad0, sums0 = call(
        functools.partial(back_kernel, order, share), grid,
        [smem, whole_spec(packed), rows_3, rows_w, rows_w, whole_spec(norms), rows_1, rows_w, rows_f]
        + [whole_spec(a) for a in (wq, wo)],
        [rows_w, rows_f, rows_w, rows_w, rows_w, sums_spec],
        [thin, tall, thin, wide, thin, sums_shape],
        unit * (4 * width + 2 * ff),
        [place, packed, mgrad1, later, hgrad1, norms, live_cols[0], hidden0, slope0, wq, wo],
    )
    chips = cube.pairs * high
    fast = len(cube.turns) == 2 and (cube.count_line * high) % LANES == 0 and high % 32 == 0
    out_own, out_other = out_grads(cube, place, branch0, branch1, att0, att1)
    up_args = (lift0, lift1, second0, second1)
    down_args = (act0, act1, drop0, drop1)

    def split_rows(v):
        start = high // 2
        return [v[:, :start], cube.turned(v[:, start:])]

    def turn_halves(halves):
        middle = cube.pairs // 2
        return [v[:middle] for v in halves], [v[middle:] for v in halves]

    if fast:
        up_other = other_grads(cube, high, *up_args, extra=[out_other])
        (up_got,) = across(cube, up_other)
        down_other = other_grads(cube, high, *down_args, hold=[up_other])
        (down_got,) = across(cube, down_other)
        made = own_grads(cube, high, *up_args, up_got, extra=[out_own], hold=[down_other])
        up_out = Scatter(cube, made[0::2], made[1::2], False)
        made = own_grads(cube, high, *down_args, down_got, hold=made)
        down = Scatter(cube, made[0::2], made[1::2], False)
    else:
        found = []
        for args, more, more_other in ((up_args, out_own, out_other), (down_args, None, None)):
            own = pair_grads(*args, 0, chips)
            if cube.inner:
                got = across(cube, pair_grads(*args, chips, chips))[0]
                own = (own.astype(f32) + got.astype(f32)).astype(bf16)
                if more is not None:
                    got = across(cube, more_other)[0]
                    more = (more.astype(f32) + got.astype(f32)).astype(bf16)
            halves = split_rows(own.reshape(cube.pairs, high, width))
            if more is not None:
                halves[0] = jnp.concatenate([halves[0], more], axis=1)
            keep, send = turn_halves(halves) if cube.turns else (halves, [])
            found.append(Scatter(cube, keep, send, False))
        up_out, down = found
        made = send
    hold = made
    groups = []
    for first in range(0, pairs, third):
        group = attend_back(
            mixed0, agrad0, att0, logs0, live_cols[0], first, third, hold, room=LATE_LIMIT
        )
        groups.append(group)
        hold = [group]
        if first == 0:
            hold = hold + up_out.step(group)
        elif first == third:
            hold = hold + down.step(group) + up_out.step(group)
        else:
            hold = hold + down.step(group) + up_out.step(group)
    own, other, small = qkv_grads(
        cube, passes, place, pass_index, groups, mgrad1, xhat0, xhat1,
        [wq, sums0, sums1], hold,
    )
    got = across(cube, other)
    if got and cube.turns and own.shape[1] % 16 == 0:
        shapes = [sds((cube.pairs // 2, own.shape[1], width // 2), bf16)] * 4
        made = call(
            core_sum_kernel, (1,), [whole_spec(own)] * 2, [whole_spec(v) for v in shapes],
            shapes, 0, [own, got[0]], room=24,
        )
        keep, send = made[0::2], made[1::2]
    else:
        if got:
            own = (own.astype(f32) + got[0].astype(f32)).astype(bf16)
        halves = split_lanes(own)
        keep, send = turn_halves(halves) if cube.turns else (halves, [])
    qkv = Scatter(cube, keep, send, True)
    hold = send
    specs_g = [
        pl.BlockSpec((3, block, a.shape[2]), lambda i: (0, i, 0)) for a in groups
    ]
    input_grad = call(
        functools.partial(last_kernel, len(groups)), grid,
        specs_g + [rows_w, rows_w, whole_spec(norms), whole_spec(wq)],
        [rows_w], [wide], unit * 3 * width,
        [*groups, x, hgrad0, norms, wq],
        hold=hold,
        room=LATE_LIMIT,
    )[0]
    qkv.step(input_grad)
    down = down.result()
    up_out = up_out.result()
    qkv = qkv.result()
    share = w_out.shape[1]
    count = w_qkv.shape[1]
    if cube.count > 1:
        half = width // 2
        ends = qkv[count : count + 8]
        small = jnp.concatenate([ends[:, :share], ends[:, half : half + share]], axis=0)
    counts = qkv[count, LANES : LANES + count]
    if cube.count == 1:
        counts = jnp.sum(
            sum(jnp.concatenate(v, axis=2) for v in (groups, [mgrad1])).astype(f32), axis=1
        ).reshape(-1)
    qkv = (qkv[:count] * norms[0:1] + counts[:, None] * norms[2:3]).T
    low_end = high // 2
    out_end = low_end + share
    up = jnp.concatenate([up_out[:low_end], up_out[out_end:]], axis=0).T
    out = up_out[low_end:out_end].T
    return (
        result[None], input_grad[None], qkv, out, up, down,
        small[:2], small[2], small[3], small[4 : 4 + passes],
    )


def solution(mesh):
    placed = (
        P(AXES, None, None),
        P(AXES),
        P(None, AXES, None),
        P(AXES),
        P(None, AXES),
        P(None, AXES),
        P(None, AXES),
        P(AXES, None),
        P(None, AXES),
        P(None, AXES),
        P(None, AXES),
        P(AXES, None, None),
    )
    return jax.shard_map(
        body,
        mesh=mesh,
        in_specs=placed,
        out_specs=(
            P(AXES, None, None),
            P(AXES, None, None),
            P(None, AXES),
            P(None, AXES),
            P(None, AXES),
            P(AXES, None),
            P(None, AXES),
            P(AXES),
            P(AXES),
            P(None, AXES),
        ),
        check_vma=False,
    )
```

```python
import functools

import jax
import jax.numpy as jnp
from jax import lax
from jax.experimental import pallas as pl
from jax.experimental.pallas import tpu as pltpu
from jax.sharding import PartitionSpec as P

HEAD = 64
LANES = 128
AXES = ("dp", "fsdp")
bf16 = jnp.bfloat16
f32 = jnp.float32

norm_epsilon = 1e-05
masked_score = -1000000000.0
curve_one = 0.7978845608028654
curve_three = 0.7978845608028654 * 0.044715

MIB = 1024 * 1024
VMEM_LIMIT = 52
LATE_LIMIT = 47


def dot_nn(left, right):
    return lax.dot_general(left, right, (((1,), (0,)), ((), ())), preferred_element_type=f32)


def dot_nt(left, right):
    return lax.dot_general(left, right, (((1,), (1,)), ((), ())), preferred_element_type=f32)


def dot_tn(left, right):
    return lax.dot_general(left, right, (((0,), (0,)), ((), ())), preferred_element_type=f32)


def normalize(values):
    center = jnp.mean(values, axis=-1, keepdims=True)
    centered = values - center
    spread = jnp.mean(centered * centered, axis=-1, keepdims=True)
    scale = lax.rsqrt(spread + norm_epsilon)
    return centered * scale, scale


def norm_back(grad, gain, xhat, scale):
    gained = grad * gain
    first = jnp.mean(gained, axis=-1, keepdims=True)
    second = jnp.mean(gained * xhat, axis=-1, keepdims=True)
    return scale * (gained - first - xhat * second)


def gelu_pair(lifted):
    square = lifted * lifted
    cubic = curve_three * square
    half = 0.5 + 0.5 * jnp.tanh(lifted * (curve_one + cubic))
    value = lifted * half
    slope = half + value * ((1.0 - half) * (2.0 * curve_one + 6.0 * cubic))
    return value, slope


def call(
    kernel, grid, in_specs, out_specs, out_shape, flops, args, scratch=(), hold=(), room=VMEM_LIMIT
):
    moved = sum(a.size * a.dtype.itemsize for a in args)
    moved += sum(o.size * o.dtype.itemsize for o in out_shape)
    given, held = len(args), len(hold)

    def run(*refs):
        kernel(*refs[:given], *refs[given + held :])

    return pl.pallas_call(
        run,
        grid=grid,
        in_specs=list(in_specs) + [pl.BlockSpec(memory_space=pl.ANY)] * held,
        out_specs=out_specs,
        out_shape=out_shape,
        scratch_shapes=list(scratch),
        compiler_params=pltpu.CompilerParams(
            dimension_semantics=("arbitrary",) * len(grid), vmem_limit_bytes=room * MIB
        ),
        cost_estimate=pl.CostEstimate(
            flops=flops, bytes_accessed=moved, transcendentals=0
        ),
    )(*args, *hold)


def rows_spec(block_rows, width):
    return pl.BlockSpec((block_rows, width), lambda i: (i, 0))


def whole_spec(array):
    zeros = (0,) * len(array.shape)
    return pl.BlockSpec(array.shape, lambda i: zeros, pipeline_mode=pl.Buffered(1))


def sds(shape, dtype):
    return jax.ShapeDtypeStruct(shape, dtype)


def head_part(x, gain, shift, w_qkv, mixed_ref, xhat_ref):
    xhat, _ = normalize(x)
    normed = (xhat * gain + shift).astype(bf16)
    xhat_ref[...] = xhat.astype(bf16)
    mixed_ref[...] = dot_nt(normed, w_qkv[...]).astype(bf16)


def first_kernel(x_ref, norms_ref, wq_ref, mixed_ref, xhat_ref):
    head_part(
        x_ref[...].astype(f32), norms_ref[0:1, :], norms_ref[2:3, :], wq_ref, mixed_ref, xhat_ref
    )


def ff_chunks(order, place_ref, packed_ref, share):
    found = []
    if share >= 768:
        for at in range(0, share, 768):
            up, down = pl.ds(at, 768), pl.ds(share + at, 768)
            found.append((lambda r=up: packed_ref[0, r, :], lambda r=down: packed_ref[0, r, :], pl.ds(at, 768)))
        return found
    per = 768 // share
    for first in range(0, len(order), per):

        def rows(at, first=first):
            return jnp.concatenate(
                [
                    packed_ref[place_ref[3] ^ mask, pl.ds(at, share), :]
                    for mask in order[first : first + per]
                ],
                axis=0,
            )

        found.append(
            (functools.partial(rows, 0), functools.partial(rows, share), pl.ds(first * share, 768))
        )
    return found


def project_kernel(att_ref, x_ref, live_ref, norms_ref, wo_ref, hidden_ref, second_ref):
    hidden = x_ref[...].astype(f32) + live_ref[...] * dot_nt(att_ref[...], wo_ref[...])
    hidden_ref[...] = hidden
    xhat, _ = normalize(hidden)
    second_ref[...] = (xhat * norms_ref[1:2, :] + norms_ref[3:4, :]).astype(bf16)


def middle_kernel(order, share, place_ref, packed_ref, *refs):
    chunks = ff_chunks(order, place_ref, packed_ref, share)
    (
        hidden_ref, second_ref, live_ref, norms_ref, emb_ref, wq_ref,
        act_ref, slope_ref, later_ref, mixed_ref, xhat_ref,
    ) = refs
    live = live_ref[...]
    hidden = hidden_ref[...]
    second = second_ref[...]
    total = jnp.zeros_like(hidden)
    for up, down, to in chunks:
        value, slope = gelu_pair(dot_nt(second, up()))
        value = value.astype(bf16)
        act_ref[:, to] = value
        slope_ref[:, to] = slope.astype(bf16)
        total = total + dot_nn(value, down())
    later = hidden + live * total + emb_ref[...]
    later_ref[...] = later
    head_part(later, norms_ref[0:1, :], norms_ref[2:3, :], wq_ref, mixed_ref, xhat_ref)


def mlp_back_tail(
    grad, live, hidden, second_grad, norms_ref, wo_ref, branch_ref, hgrad_ref, agrad_ref
):
    xhat, scale = normalize(hidden)
    hgrad = grad + norm_back(second_grad, norms_ref[1:2, :], xhat, scale)
    hgrad_ref[...] = hgrad
    branch = (live * hgrad).astype(bf16)
    branch_ref[...] = branch
    agrad_ref[...] = dot_nn(branch, wo_ref[...]).astype(bf16)
    gain_sum = jnp.sum(second_grad * xhat, axis=0, keepdims=True)
    shift_sum = jnp.sum(second_grad, axis=0, keepdims=True)
    return gain_sum, shift_sum


def add_sums(sums_ref, sums):
    @pl.when(pl.program_id(0) == 0)
    def _():
        sums_ref[...] = jnp.zeros_like(sums_ref)

    for place, value in enumerate(sums):
        sums_ref[place : place + 1, :] += value


def turn_kernel(order, share, place_ref, packed_ref, *refs):
    chunks = ff_chunks(order, place_ref, packed_ref, share)
    (
        att_ref, x_ref, live_ref, norms_ref, grad_ref, wo_ref,
        out_ref, second_ref, act_ref, drop_ref, lift_ref, branch_ref, hgrad_ref, agrad_ref, sums_ref,
    ) = refs
    live = live_ref[...]
    hidden = x_ref[...] + live * dot_nt(att_ref[...], wo_ref[...])
    xhat, _ = normalize(hidden)
    second = (xhat * norms_ref[1:2, :] + norms_ref[3:4, :]).astype(bf16)
    second_ref[...] = second
    grad = grad_ref[...]
    drop = (live * grad).astype(bf16)
    drop_ref[...] = drop
    total = jnp.zeros_like(hidden)
    second_grad = jnp.zeros_like(hidden)
    for up, down, to in chunks:
        up, down = up(), down()
        value, slope = gelu_pair(dot_nt(second, up))
        value = value.astype(bf16)
        act_ref[:, to] = value
        total = total + dot_nn(value, down)
        lift = (dot_nt(drop, down) * slope).astype(bf16)
        lift_ref[:, to] = lift
        second_grad = second_grad + dot_nn(lift, up)
    out_ref[...] = (hidden + live * total).astype(bf16)
    sums = mlp_back_tail(
        grad, live, hidden, second_grad, norms_ref, wo_ref, branch_ref, hgrad_ref, agrad_ref
    )
    add_sums(sums_ref, sums)


def head_back(mixed_grad_refs, wq_ref, x, hgrad, norms_ref):
    width = x.shape[1]
    normed_grad = jnp.zeros_like(x)
    for part in range(3):
        at = part * width
        for ref in mixed_grad_refs:
            normed_grad += dot_nn(ref[part], wq_ref[at : at + ref.shape[2], :])
            at += ref.shape[2]
    xhat, scale = normalize(x)
    return hgrad + norm_back(normed_grad, norms_ref[0:1, :], xhat, scale)


def back_kernel(order, share, place_ref, packed_ref, *refs):
    chunks = ff_chunks(order, place_ref, packed_ref, share)
    (
        mgrad_ref, later_ref, hgrad1_ref, norms_ref, live_ref, hidden_ref, slope_ref, wq_ref, wo_ref,
        drop_ref, lift_ref, branch_ref, hgrad_ref, agrad_ref, sums_ref,
    ) = refs
    grad = head_back([mgrad_ref], wq_ref, later_ref[...], hgrad1_ref[...], norms_ref)
    table_sum = jnp.sum(grad, axis=0, keepdims=True)
    live = live_ref[...]
    drop = (live * grad).astype(bf16)
    drop_ref[...] = drop
    second_grad = jnp.zeros_like(grad)
    for up, down, to in chunks:
        lift = (dot_nt(drop, down()) * slope_ref[:, to].astype(f32)).astype(bf16)
        lift_ref[:, to] = lift
        second_grad = second_grad + dot_nn(lift, up())
    sums = mlp_back_tail(
        grad, live, hidden_ref[...], second_grad, norms_ref, wo_ref, branch_ref, hgrad_ref, agrad_ref
    )
    add_sums(sums_ref, sums + (table_sum,))


def last_kernel(groups, *refs):
    mgrad_refs, (x_ref, hgrad_ref, norms_ref, wq_ref, out_ref) = refs[:groups], refs[groups:]
    out_ref[...] = head_back(
        mgrad_refs, wq_ref, x_ref[...].astype(f32), hgrad_ref[...], norms_ref
    )


def both_layers(left0, left1, right0, right1):
    return dot_tn(left0[...], right0[...]) + dot_tn(left1[...], right1[...])


def pair_grad_kernel(left0, left1, right0, right1, out_ref):
    out_ref[...] = both_layers(left0, left1, right0, right1).astype(bf16)


def pair_grads(left0, left1, right0, right1, start, size, hold=()):
    tokens = left0.shape[0]
    width = right0.shape[1]
    step = 384 if size % 384 == 0 else size
    first = start // step
    cols = pl.BlockSpec((tokens, step), lambda i: (0, first + i))
    return call(
        pair_grad_kernel,
        (size // step,),
        [cols] * 2 + [whole_spec(right0)] * 2,
        [rows_spec(step, width)],
        [sds((size, width), bf16)],
        4 * tokens * size * width,
        [left0, left1, right0, right1],
        hold=hold, room=LATE_LIMIT,
    )[0]


def blocks_spec(shape, index):
    return pl.BlockSpec(shape, lambda i: (index(i), 0, 0))


def other_grad_kernel(high, left0, left1, right0, right1, *refs):
    extra, out_ref = refs[:-1], refs[-1]
    total = both_layers(left0, left1, right0, right1).astype(bf16)
    for place in range(out_ref.shape[0]):
        out_ref[place, :high, :] = total[place * high : (place + 1) * high]
        for ref in extra:
            out_ref[place, high:, :] = ref[place]


def other_grads(cube, high, left0, left1, right0, right1, extra=(), hold=()):
    tokens = left0.shape[0]
    width = right0.shape[1]
    lines, turns = cube.count_line, cube.count_turns
    first = turns
    cols = pl.BlockSpec((tokens, lines * high), lambda i: (0, first + i))
    rows = high + sum(a.shape[1] for a in extra)
    return call(
        functools.partial(other_grad_kernel, high),
        (turns,),
        [cols] * 2
        + [whole_spec(right0)] * 2
        + [blocks_spec((lines,) + a.shape[1:], lambda i: i) for a in extra],
        [blocks_spec((lines, rows, width), lambda i: i)],
        [sds((cube.pairs, rows, width), bf16)],
        4 * tokens * cube.pairs * high * width,
        [left0, left1, right0, right1, *extra],
        hold=hold, room=LATE_LIMIT,
    )[0]


def own_grad_kernel(high, left0, left1, right0, right1, got, *refs):
    extra, (low_keep, low_send, late_keep, late_send) = refs[:-4], refs[-4:]
    middle = high // 2
    half = pl.num_programs(0) // 2
    step = pl.program_id(0)
    total = both_layers(left0, left1, right0, right1)

    def low_part(ref):
        for place in range(ref.shape[0]):
            at = place * high
            ref[place, :middle, :] = (
                total[at : at + middle] + got[place, :middle, :].astype(f32)
            ).astype(bf16)
            for more in extra:
                ref[place, middle:, :] = (
                    more[place].astype(f32) + got[place, high:, :].astype(f32)
                ).astype(bf16)

    def late_part(ref):
        for place in range(ref.shape[0]):
            at = place * high
            ref[place] = (
                total[at + middle : at + high] + got[place, middle:high, :].astype(f32)
            ).astype(bf16)

    @pl.when(step < half)
    def _():
        low_part(low_keep)

    @pl.when(step >= half)
    def _():
        low_part(low_send)

    @pl.when(step % 2 == 0)
    def _():
        late_part(late_keep)

    @pl.when(step % 2 == 1)
    def _():
        late_part(late_send)


def own_grads(cube, high, left0, left1, right0, right1, got, extra=(), hold=()):
    tokens = left0.shape[0]
    width = right0.shape[1]
    lines, turns = cube.count_line, cube.count_turns
    half = turns // 2
    cols = pl.BlockSpec((tokens, lines * high), lambda i: (0, i))
    low = high // 2 + sum(a.shape[1] for a in extra)
    late = high - high // 2

    def turned(i):
        found = 0
        for bit in range(1, turns.bit_length() - 1):
            found = found + (((i >> bit) & 1) << (turns.bit_length() - 2 - bit))
        return found

    def first_keep(i):
        return jnp.minimum(i, half - 1)

    def first_send(i):
        return jnp.maximum(i - half, 0)

    return call(
        functools.partial(own_grad_kernel, high),
        (turns,),
        [cols] * 2
        + [whole_spec(right0)] * 2
        + [blocks_spec((lines,) + a.shape[1:], lambda i: i) for a in (got, *extra)],
        [
            blocks_spec((lines, low, width), first_keep),
            blocks_spec((lines, low, width), first_send),
            blocks_spec((lines, late, width), turned),
            blocks_spec((lines, late, width), turned),
        ],
        [sds((cube.pairs // 2, n, width), bf16) for n in (low, low, late, late)],
        4 * tokens * cube.pairs * high * width,
        [left0, left1, right0, right1, got, *extra],
        hold=hold, room=LATE_LIMIT,
    )


def place_blocks(cube, place_ref, total_ref, own_ref, other_ref):
    rows = own_ref.shape[1]
    for chip in range(own_ref.shape[0]):
        if cube.inner == 0:
            own_ref[0] = total_ref[...].astype(bf16)
            continue
        even = total_ref[pl.ds(2 * chip * rows, rows), :].astype(bf16)
        odd = total_ref[pl.ds((2 * chip + 1) * rows, rows), :].astype(bf16)
        first = place_ref[2] == 0
        at = cube.place(2 * chip, 0) ^ place_ref[0]
        own_ref[at] = jnp.where(first, even, odd)
        other_ref[at] = jnp.where(first, odd, even)


def out_grad_kernel(cube, place_ref, left0, left1, right0, right1, own_ref, other_ref, total_ref):
    total_ref[...] = both_layers(left0, left1, right0, right1)
    place_blocks(cube, place_ref, total_ref, own_ref, other_ref)


def block_shapes(cube, rows, width):
    shape = (cube.pairs, rows, width)
    return [sds(shape, bf16)] * 2, [pl.BlockSpec(shape, lambda i: (0, 0, 0))] * 2


def out_grads(cube, place, left0, left1, right0, right1, hold=()):
    tokens, high = left0.shape
    width = right1.shape[1]
    shapes, specs = block_shapes(cube, high // cube.count, width)
    args = [left0, left1, right0, right1]
    return call(
        functools.partial(out_grad_kernel, cube),
        (1,),
        [pl.BlockSpec(memory_space=pltpu.SMEM)] + [whole_spec(a) for a in args],
        specs,
        shapes,
        4 * tokens * high * width,
        [place, *args],
        scratch=[pltpu.VMEM((high, width), f32)],
        hold=hold, room=LATE_LIMIT,
    )


def qkv_grad_kernel(cube, groups, passes, place_ref, pass_ref, *refs):
    lefts0, refs = refs[:groups], refs[groups:]
    left1, right0, right1, wq_ref, sums0_ref, sums1_ref, own_ref, other_ref = refs[:8]
    small_ref, total_ref, count_ref = refs[8:]
    part = pl.program_id(0)
    high = left1.shape[2]
    width = right0.shape[1]
    row = lax.broadcasted_iota(jnp.int32, (8, 1), 0)

    @pl.when(part == 0)
    def _():
        small_ref[...] = jnp.zeros_like(small_ref)
        small_ref[1:2, :] = sums0_ref[0:1, :] + sums1_ref[0:1, :]
        small_ref[3:4, :] = sums0_ref[1:2, :] + sums1_ref[1:2, :]
        for index in range(passes):
            small_ref[4 + index : 5 + index, :] = jnp.where(
                pass_ref[0] == index, sums0_ref[2:3, :], 0.0
            )

    at = 0
    gain_sum = jnp.zeros((1, width), f32)
    shift_sum = jnp.zeros((1, width), f32)
    for left0 in lefts0:
        to = pl.ds(at, left0.shape[2])
        rows = pl.ds(pl.multiple_of(part * high + at, 8), left0.shape[2])
        total = dot_tn(left0[0], right0[...]) + dot_tn(left1[0, :, to], right1[...])
        total_ref[rows, :] = total
        sums = jnp.sum(left0[0].astype(f32) + left1[0, :, to].astype(f32), axis=0, keepdims=True)
        count_ref[pl.ds(part, 1), to] = sums
        terms = split_three(jnp.broadcast_to(sums, (8, left0.shape[2])))
        three = jnp.where(row == 0, terms[0], jnp.where(row == 1, terms[1], terms[2]))
        three = jnp.where(row < 3, three, jnp.zeros_like(three))
        weights = wq_ref[to, :]
        gain_sum += jnp.sum(total * weights.astype(f32), axis=0, keepdims=True)
        shift_sum += jnp.sum(dot_nn(three, weights), axis=0, keepdims=True)
        at += left0.shape[2]
    small_ref[0:1, :] += gain_sum
    small_ref[2:3, :] += shift_sum

    @pl.when(part == pl.num_programs(0) - 1)
    def _():
        extra = 8
        rows = own_ref.shape[1] - extra
        share = width // cube.count
        half = width // 2
        small = small_ref[...]
        counts = jnp.concatenate([count_ref[p : p + 1, :] for p in range(3)], axis=1)
        counts = jnp.broadcast_to(counts, (8, counts.shape[1]))
        for chip in range(cube.pairs):
            found = []
            for device in range(2 * chip, 2 * chip + 1 + (cube.inner > 0)):
                block = total_ref[pl.ds(device * rows, rows), :]
                line, own = small, counts
                if device:
                    line = pltpu.roll(small, width - device * share, 1)
                    own = pltpu.roll(counts, counts.shape[1] - device * rows, 1)
                line = [line[:8, :LANES], own[:, : half - LANES], line[8:, :half]]
                line = jnp.concatenate(line, axis=1)
                found.append(jnp.concatenate([block, line], axis=0).astype(bf16))
            if cube.inner == 0:
                own_ref[0] = found[0]
                continue
            first = place_ref[2] == 0
            own = jnp.where(first, found[0], found[1])
            other = jnp.where(first, found[1], found[0])
            for order in range(2):
                lanes = slice(order * half, (order + 1) * half)
                at = cube.place(2 * chip, order) ^ place_ref[order]
                own_ref[at, :, lanes] = own[:, lanes]
                other_ref[at, :, lanes] = other[:, lanes]


def qkv_grads(cube, passes, place, pass_index, lefts0, left1, right0, right1, kept, hold=()):
    parts, tokens, high = left1.shape
    width = right0.shape[1]
    specs = [
        pl.BlockSpec((1, tokens, a.shape[2]), lambda i: (i, 0, 0)) for a in (*lefts0, left1)
    ]
    shapes, out_specs = block_shapes(cube, parts * high // cube.count + 8, width)
    return call(
        functools.partial(qkv_grad_kernel, cube, len(lefts0), passes),
        (parts,),
        [pl.BlockSpec(memory_space=pltpu.SMEM)] * 2
        + specs
        + [whole_spec(a) for a in (right0, right1)]
        + [rows_spec(high, width)]
        + [whole_spec(a) for a in kept[1:]],
        out_specs + [pl.BlockSpec((16, width), lambda i: (0, 0))],
        shapes + [sds((16, width), f32)],
        4 * tokens * parts * high * width,
        [place, pass_index, *lefts0, left1, right0, right1, *kept],
        scratch=[pltpu.VMEM((parts * high, width), f32), pltpu.VMEM((8, high), f32)],
        hold=hold,
        room=LATE_LIMIT,
    )


def lane_index(shape):
    return lax.broadcasted_iota(jnp.int32, shape, len(shape) - 1)


def split_three(values):
    high = values.astype(bf16)
    rest = values - high.astype(f32)
    middle = rest.astype(bf16)
    low = (rest - middle.astype(f32)).astype(bf16)
    return high, middle, low


def own_lanes(lane, head):
    return (lane < HEAD) if head == 0 else (lane >= HEAD)


def attend_kernel(
    block, q_ref, k_ref, v_ref, live_col_ref, live_row_ref, out_ref, logs_ref, mask_ref
):
    seq = q_ref.shape[0]
    count = seq // block

    @pl.when(pl.program_id(0) == 0)
    def _():
        query = lax.broadcasted_iota(jnp.int32, (block, block), 0)
        key = lax.broadcasted_iota(jnp.int32, (block, block), 1)
        for i in range(count):
            alive = live_row_ref[:, i * block : (i + 1) * block] > 0.5
            visible = (key <= query) & (alive | (key == query))
            mask_ref[i] = jnp.where(visible, 0.0, masked_score)

    lane = lane_index((seq, LANES))
    q = q_ref[...] * 0.125
    k = k_ref[...]
    v = v_ref[...]
    bias = ((live_col_ref[...] - 1.0) * 1e9).astype(bf16)
    zero = jnp.zeros((seq, LANES), bf16)
    one = jnp.ones((seq, LANES), bf16)
    parts = []
    for head in range(2):
        mine = own_lanes(lane, head)
        spare = (1 - head) * HEAD
        parts.append(
            (
                jnp.where(mine, q, zero),
                jnp.where(mine, q, jnp.where(lane == spare, one, zero)),
                jnp.where(mine, k, jnp.where(lane == spare, bias, zero)),
                jnp.where(mine, v, one),
            )
        )
    low = lane_index((block, LANES)) < HEAD

    def score(i, head):
        at, before = slice(i * block, (i + 1) * block), slice(0, i * block)
        q_plain, q_bias, k_bias, _ = parts[head]
        diag = dot_nt(q_plain[at], k[at]) + mask_ref[i]
        return diag, dot_nt(q_bias[at], k_bias[before]) if i > 0 else None

    def soften(diag, off):
        top = jnp.max(diag, axis=-1, keepdims=True)
        if off is None:
            return top, jnp.exp(diag - top).astype(bf16), None
        top = jnp.maximum(top, jnp.max(off, axis=-1, keepdims=True))
        return top, jnp.exp(diag - top).astype(bf16), jnp.exp(off - top).astype(bf16)

    def finish(i, head, top, diag, off):
        at, before = slice(i * block, (i + 1) * block), slice(0, i * block)
        v_ones = parts[head][3]
        total = dot_nn(diag, v_ones[at])
        if i > 0:
            total += dot_nn(off, v_ones[before])
        spare = (1 - head) * HEAD
        weight = total[:, spare : spare + 1]
        found.append((total * (1.0 / weight), top + jnp.log(weight)))
        if head == 1:
            (out0, log0), (out1, log1) = found[-2:]
            out_ref[at, :] = jnp.where(low, out0, out1).astype(bf16)
            logs_ref[at, :] = jnp.where(low, log0, log1)

    found = []
    steps = [(i, head) for i in range(count) for head in range(2)]
    ahead, behind = score(*steps[0]), None
    for place, step in enumerate(steps):
        scored = ahead
        if place + 1 < len(steps):
            ahead = score(*steps[place + 1])
        softened = soften(*scored)
        if behind is not None:
            finish(*steps[place - 1], *behind)
        behind = softened
    finish(*steps[-1], *behind)


def attend(mixed, live_col, live_row, first=0, count=None, hold=(), block=256):
    seq, triple = mixed.shape
    pairs = triple // 3 // LANES
    count = pairs if count is None else count
    width = count * LANES
    block = min(block, seq)

    def cols(offset):
        return pl.BlockSpec((seq, LANES), lambda h: (0, offset + h))

    return call(
        functools.partial(attend_kernel, block),
        (count,),
        [cols(first), cols(first + pairs), cols(first + 2 * pairs), whole_spec(live_col), whole_spec(live_row)],
        [cols(0), cols(0)],
        [sds((seq, width), bf16), sds((seq, width), f32)],
        4 * seq * seq * width,
        [mixed, mixed, mixed, live_col, live_row],
        scratch=[pltpu.VMEM((seq // block, block, block), f32)],
        hold=hold, room=VMEM_LIMIT,
    )


def attend_back_kernel(
    block, q_ref, k_ref, v_ref, grad_ref, att_ref, logs_ref, live_col_ref, out_ref,
    mask_ref, dk_ref, dv_ref,
):
    seq = q_ref.shape[0]
    count = seq // block

    @pl.when(pl.program_id(0) == 0)
    def _():
        key = lax.broadcasted_iota(jnp.int32, (block, block), 0)
        query = lax.broadcasted_iota(jnp.int32, (block, block), 1)
        for i in range(count):
            alive = live_col_ref[i * block : (i + 1) * block, :] > 0.5
            visible = (key <= query) & (alive | (key == query))
            mask_ref[i] = jnp.where(visible, 0.0, masked_score)

    lane = lane_index((seq, LANES))
    q = q_ref[...] * 0.125
    k = k_ref[...]
    v = v_ref[...]
    grad = grad_ref[...]
    logs = logs_ref[...]
    dots = grad.astype(f32) * att_ref[...].astype(f32)
    bias = ((live_col_ref[...] - 1.0) * 1e9).astype(bf16)
    zero = jnp.zeros((seq, LANES), bf16)
    one = jnp.ones((seq, LANES), bf16)
    parts = []
    for head in range(2):
        mine = own_lanes(lane, head)
        spare = (1 - head) * HEAD
        log_terms = split_three(-logs[:, head * HEAD : head * HEAD + 1])
        dot_terms = split_three(-jnp.sum(jnp.where(mine, dots, 0.0), axis=-1, keepdims=True))
        q_more, k_more, k_diag, g_more, v_more = (
            jnp.where(lane == spare, one, zero),
            jnp.where(lane == spare, bias, zero),
            zero,
            zero,
            zero,
        )
        for place in range(3):
            here = lane == spare + 1 + place
            q_more = jnp.where(here, log_terms[place], q_more)
            k_more = jnp.where(here, one, k_more)
            k_diag = jnp.where(here, one, k_diag)
            g_more = jnp.where(here, dot_terms[place], g_more)
            v_more = jnp.where(here, one, v_more)
        parts.append(
            dict(
                q=jnp.where(mine, q, q_more),
                k=jnp.where(mine, k, k_more),
                kd=jnp.where(mine, k, k_diag),
                g=jnp.where(mine, grad, g_more),
                v=jnp.where(mine, v, v_more),
                q0=jnp.where(mine, q, zero),
                k0=jnp.where(mine, k, zero),
                g0=jnp.where(mine, grad, zero),
            )
        )
    def rows(i):
        return slice(i * block, (i + 1) * block)

    def score(i, j, head):
        part = parts[head]
        first = dot_nt(part["kd" if j == i else "k"][rows(j)], part["q"][rows(i)])
        return first, dot_nt(part["v"][rows(j)], part["g"][rows(i)])

    def soften(i, j, head, scores, change):
        if j == i:
            scores = scores + mask_ref[i]
        soft = jnp.exp(scores)
        return soft.astype(bf16), (soft * change).astype(bf16)

    def add(name, value):
        totals[name] = totals[name] + value if name in totals else value

    def finish(i, j, head, soft, change):
        part = parts[head]
        add("v", dot_nn(soft, part["g0"][rows(i)]))
        add("k", dot_nn(change, part["q0"][rows(i)]))
        add("q", dot_tn(change, part["k0"][rows(j)]))
        if head == 1:
            for name, ref in (("v", dv_ref), ("k", dk_ref)):
                if j == i:
                    ref[rows(j), :] = totals.pop(name)
                else:
                    ref[rows(j), :] += totals.pop(name)
            if j == i:
                out_ref[0, rows(i), :] = (totals.pop("q") * 0.125).astype(bf16)

    totals = {}
    steps = [(i, j, head) for i in range(count) for j in range(i + 1) for head in range(2)]
    ahead, behind = score(*steps[0]), None
    for place, step in enumerate(steps):
        scored = ahead
        if place + 1 < len(steps):
            ahead = score(*steps[place + 1])
        softened = soften(*step, *scored)
        if behind is not None:
            finish(*steps[place - 1], *behind)
        behind = softened
    finish(*steps[-1], *behind)
    out_ref[1] = dk_ref[...].astype(bf16)
    out_ref[2] = dv_ref[...].astype(bf16)


def attend_back(mixed, att_grad, att, logs, live_col, first=0, count=None, hold=(), block=256, room=VMEM_LIMIT):
    seq, triple = mixed.shape
    pairs = triple // 3 // LANES
    count = pairs if count is None else count
    width = count * LANES
    block = min(block, seq)

    def cols(offset):
        return pl.BlockSpec((seq, LANES), lambda h: (0, offset + h))

    return call(
        functools.partial(attend_back_kernel, block),
        (count,),
        [cols(first), cols(first + pairs), cols(first + 2 * pairs)]
        + [cols(first), cols(first), cols(first), whole_spec(live_col)],
        [pl.BlockSpec((3, seq, LANES), lambda h: (0, 0, h))],
        [sds((3, seq, width), bf16)],
        10 * seq * seq * width,
        [mixed, mixed, mixed, att_grad, att, logs, live_col],
        scratch=[
            pltpu.VMEM((seq // block, block, block), f32),
            pltpu.VMEM((seq, LANES), f32),
            pltpu.VMEM((seq, LANES), f32),
        ],
        hold=hold, room=room,
    )[0]


def all_masks(bits):
    masks = [0]
    for bit in bits:
        masks += [m | (1 << bit) for m in masks]
    return masks


class Cube:
    def __init__(self):
        inner = lax.axis_size(AXES[1])
        self.count = lax.axis_size(AXES[0]) * inner
        self.bits = self.count.bit_length() - 1
        self.inner = inner.bit_length() - 1
        self.pairs = self.count >> (self.inner > 0)
        self.me = lax.axis_index(AXES)
        self.outer = list(range(self.inner, self.bits))
        self.rest = list(range(1, self.inner))
        self.turns = list(zip(self.outer, self.outer[::-1]))
        self.count_turns = 1 << len(self.outer)
        self.count_line = 1 << len(self.rest)

    def send(self, value, mask):
        return lax.ppermute(value, AXES, [(d, d ^ mask) for d in range(self.count)])

    def send_all(self, value, bits):
        return [self.send(value, mask) for mask in all_masks(bits)[1:]]

    def place(self, device, order):
        bits = [pair[order] for pair in self.turns] + self.rest[::-1]
        found = 0
        for bit in bits:
            found = found * 2 + ((device >> bit) & 1)
        return found

    def places(self):
        return jnp.stack([self.place(self.me, 0), self.place(self.me, 1), self.me & 1, self.me])

    def order(self):
        return sorted(range(self.count), key=lambda d: (d & (self.inner > 0), self.place(d, 0)))

    def turned(self, value):
        count = len(self.turns)
        shape = value.shape
        value = value.reshape((2,) * count + (-1,) + shape[1:])
        axes = tuple(range(count))[::-1] + tuple(range(count, value.ndim))
        return value.transpose(axes).reshape(shape)


class Gather:
    def __init__(self, cube, block, split):
        self.cube, self.split = cube, split
        self.value = block[None]

    def line(self, make=None):
        got = self.cube.send_all(self.value, self.cube.rest)
        if make is not None:
            got = after(got, make)
        self.value = jnp.concatenate([self.value, *got], axis=0)
        self.halves = self.split(self.value)
        self.turns = self.cube.turns[::-1]
        return self.value

    def turn(self, *others):
        if self.turns:
            bits = self.turns.pop(0)
            got = [self.cube.send(v, 1 << bit) for v, bit in zip(self.halves, bits)]
            if others:
                got = after(got, others)
            self.halves = [jnp.concatenate(pair, axis=0) for pair in zip(self.halves, got)]
        return self.halves


def after(value, others):
    return lax.optimization_barrier((value, others))[0]


def across(cube, value):
    return [cube.send(value, 1)] if cube.inner else []


def turn_sum_kernel(count, *refs):
    for half in range(count):
        keep, got = refs[2 * half], refs[2 * half + 1]
        first, second = refs[2 * count + 2 * half], refs[2 * count + 2 * half + 1]
        total = (keep[...].astype(f32) + got[...].astype(f32)).astype(bf16)
        middle = first.shape[0]
        first[...] = total[:middle]
        second[...] = total[middle:]


def join_kernel(lanes, *refs):
    low, low_got, late, late_got = refs[:4]
    for place, out in enumerate(refs[4:]):
        first = (low[place].astype(f32) + low_got[place].astype(f32)).astype(bf16)
        second = (late[place].astype(f32) + late_got[place].astype(f32)).astype(bf16)
        if lanes:
            out[:, : first.shape[1]] = first
            out[:, first.shape[1] :] = second
        else:
            out[: first.shape[0], :] = first
            out[first.shape[0] :, :] = second


def core_sum_kernel(own, got, *outs):
    middle, _, half = outs[0].shape
    for order in range(2):
        for part in range(2):
            at = (slice(part * middle, (part + 1) * middle), slice(None), slice(order * half, (order + 1) * half))
            outs[2 * order + part][...] = (own[at].astype(f32) + got[at].astype(f32)).astype(bf16)


class Scatter:
    def __init__(self, cube, keep, send, lanes):
        self.cube, self.keep, self.sent, self.lanes = cube, list(keep), list(send), lanes
        self.todo = list(cube.turns)
        self.got, self.total = [], None
        if self.todo:
            self.go()
        else:
            self.total = jnp.concatenate(self.keep, axis=2 if lanes else 1)[0].astype(f32)

    def go(self):
        bits = self.todo.pop(0)
        self.got = [self.cube.send(v, 1 << bit) for v, bit in zip(self.sent, bits)]
        self.last = not self.todo

    def step(self, *others):
        if self.total is not None:
            return []
        got = after(self.got, others) if others else self.got
        if self.sent is None:
            total = self.keep.astype(f32)
            for other in got:
                total = total + other.astype(f32)
            self.total = total
            return [total]
        pairs = [v for pair in zip(self.keep, got) for v in pair]
        small = all(v.shape[1] % 16 == 0 or v.shape[1] == 72 for v in self.keep)
        if not self.last:
            middle = self.keep[0].shape[0] // 2
            if small:
                shapes = [sds((middle,) + v.shape[1:], bf16) for v in self.keep for _ in range(2)]
                made = call(
                    functools.partial(turn_sum_kernel, 2), (1,), [whole_spec(v) for v in pairs],
                    [whole_spec(v) for v in shapes], shapes, 0, pairs, room=24,
                )
            else:
                made = []
                for keep, other in zip(self.keep, got):
                    total = (keep.astype(f32) + other.astype(f32)).astype(bf16)
                    made += [total[:middle], total[middle:]]
            self.keep, self.sent = list(made[0::2]), list(made[1::2])
            self.go()
            return self.sent
        masks = all_masks(self.cube.rest)
        if small:
            first, second = [v.shape[1:] for v in self.keep]
            shape = (first[0], first[1] + second[1]) if self.lanes else (first[0] + second[0], first[1])
            shapes = [sds(shape, bf16)] * len(masks)
            made = call(
                functools.partial(join_kernel, self.lanes), (1,), [whole_spec(v) for v in pairs],
                [whole_spec(v) for v in shapes], shapes, 0, pairs, room=24,
            )
        else:
            total = [
                (a.astype(f32) + b.astype(f32)).astype(bf16) for a, b in zip(self.keep, got)
            ]
            total = jnp.concatenate(total, axis=2 if self.lanes else 1)
            made = [total[i] for i in range(len(masks))]
        self.keep, sent = made[0], list(made[1:])
        self.got = [self.cube.send(v, mask) for v, mask in zip(sent, masks[1:])]
        self.sent = None
        return sent

    def result(self):
        while self.total is None:
            self.step()
        return self.total


def after(value, others):
    return lax.optimization_barrier((value, others))[0]


def across(cube, value):
    return [cube.send(value, 1)] if cube.inner else []


def set_down_kernel(cube, sizes, share, place_ref, pass_ref, *refs):
    sources, (wq_ref, wo_ref, norms_ref, emb_ref) = refs[:-4], refs[-4:]
    per = len(sources) // 2
    half = wq_ref.shape[2] // 2
    mid = sizes[0] + sizes[1]
    extra = sources[0].shape[1] - mid
    row = lax.broadcasted_iota(jnp.int32, (extra, 1), 0)
    picked = (row < 8) | (row == 8 + pass_ref[0])
    empty = jnp.zeros((extra, half), f32)
    small = jnp.zeros((extra, 2 * half), f32)
    for device in range(cube.count):
        for order in range(2):
            at = cube.place(device, order) ^ place_ref[order]
            block = sources[order * per][at]
            if per > 1:
                own = ((device & 1) ^ place_ref[2]) == 0
                block = jnp.where(own, block, sources[order * per + 1][at])
            block = block.astype(f32)
            lanes = slice(order * half, (order + 1) * half)
            wq_ref[device, :, lanes] = block[: sizes[0]].astype(bf16)
            wo_ref[device, :, lanes] = block[sizes[0] : mid].astype(bf16)
            if order * half < share:
                line = [jnp.where(picked, block[mid:], 0.0), empty]
                line = jnp.concatenate(line[::-1] if order else line, axis=1)
                small = small + (pltpu.roll(line, device * share, 1) if device else line)
    norms_ref[...] = small[:8]
    emb_ref[...] = jnp.sum(small[8:], axis=0, keepdims=True)


def set_down(cube, place, pass_index, sources, sizes, share):
    width = 2 * sources[0].shape[2]
    shapes = [(cube.count, n, width) for n in sizes]
    wq, wo, norms, emb = call(
        functools.partial(set_down_kernel, cube, sizes, share), (1,),
        [pl.BlockSpec(memory_space=pltpu.SMEM)] * 2 + [whole_spec(a) for a in sources],
        [pl.BlockSpec(n, lambda i: (0, 0, 0)) for n in shapes]
        + [pl.BlockSpec((n, width), lambda i: (0, 0)) for n in (8, 1)],
        [sds(n, bf16) for n in shapes] + [sds((n, width), f32) for n in (8, 1)], 0,
        [place, pass_index, *sources],
    )
    return wq.reshape(-1, width), wo.reshape(-1, width), norms, emb


def body(
    tokens, row_lengths, live_mask, pass_index,
    w_qkv, w_out, w_up, w_down, norm_gains, norm_shifts, pass_table, cotangent,
):
    _, seq, width = tokens.shape
    cube = Cube()
    place = cube.places()
    ff = w_up.shape[1] * cube.count
    block = min(256, seq)
    grid = (seq // block,)
    passes = pass_table.shape[0]

    def split_lanes(v):
        half = v.shape[2] // 2
        return [v[:, :, :half], v[:, :, half:]]

    high = w_up.shape[1]
    share = w_out.shape[1]

    def wide_rows(v):
        return jnp.pad(v, ((0, -v.shape[0] % 8), (0, width - v.shape[1])))

    packed = jnp.concatenate([w_up.T, w_down], axis=0)
    packed = lax.all_gather(packed, AXES, axis=0, tiled=False)

    gains_shifts = wide_rows(jnp.concatenate([norm_gains, norm_shifts], axis=0))
    early = [w_qkv.T, w_out.T, gains_shifts, wide_rows(pass_table)]
    part_q = Gather(cube, jnp.concatenate(early, axis=0), split_lanes)
    part_q.line()
    for _ in cube.turns:
        part_q.turn()
    low, late = part_q.halves
    sources = [low, *across(cube, low), late, *across(cube, late)]
    sizes = (w_qkv.shape[1], w_out.shape[1])
    wq, wo, norms, emb = set_down(cube, place, pass_index, sources, sizes, share)

    positions = jnp.arange(seq, dtype=jnp.int32)
    inside = positions < row_lengths[0]
    live = jnp.where(inside[None, :] & (live_mask[:, 0] > 0), 1.0, 0.0).astype(f32)
    live_cols = [live[0][:, None], live[1][:, None]]
    live_rows = [live[0][None, :], live[1][None, :]]

    x = tokens[0]
    given = cotangent[0]
    rows_w = rows_spec(block, width)
    rows_f = rows_spec(block, ff)
    rows_q = rows_spec(block, 3 * width)
    rows_1 = rows_spec(block, 1)
    rows_3 = pl.BlockSpec((3, block, width), lambda i: (0, i, 0))
    sums_spec = pl.BlockSpec((8, width), lambda i: (0, 0))
    wide = sds((seq, width), f32)
    thin = sds((seq, width), bf16)
    tall = sds((seq, ff), bf16)
    triple = sds((seq, 3 * width), bf16)
    sums_shape = sds((8, width), f32)
    unit = 2 * seq * width

    mixed0, xhat0 = call(
        first_kernel, grid,
        [rows_w, whole_spec(norms), whole_spec(wq)],
        [rows_q, rows_w], [triple, thin], unit * 3 * width, [x, norms, wq],
    )
    pairs = width // LANES
    third = pairs // 3 if pairs % 3 == 0 else pairs
    att0, logs0 = attend(mixed0, live_cols[0], live_rows[0])
    hidden0, second0 = call(
        project_kernel, grid,
        [rows_w, rows_w, rows_1, whole_spec(norms), whole_spec(wo)],
        [rows_w, rows_w], [wide, thin], unit * width, [att0, x, live_cols[0], norms, wo],
    )
    packed = after(packed, second0)
    order, share = cube.order(), high
    if cube.count == 1 or 768 % high or high % 16:
        blocks = [packed[:, at : at + high] for at in (0, high)]
        turned = [
            jnp.take(v, jnp.asarray(order, jnp.int32) ^ cube.me, axis=0).reshape(ff, width)
            for v in blocks
        ]
        packed, share = jnp.concatenate(turned, axis=0)[None], ff
    smem = pl.BlockSpec(memory_space=pltpu.SMEM)
    act0, slope0, later, mixed1, xhat1 = call(
        functools.partial(middle_kernel, order, share), grid,
        [smem, whole_spec(packed), rows_w, rows_w, rows_1]
        + [whole_spec(a) for a in (norms, emb, wq)],
        [rows_f, rows_f, rows_w, rows_q, rows_w],
        [tall, tall, wide, triple, thin],
        unit * (3 * width + 2 * ff),
        [place, packed, hidden0, second0, live_cols[0], norms, emb, wq],
    )
    att1, logs1 = attend(mixed1, live_cols[1], live_rows[1])
    result, second1, act1, drop1, lift1, branch1, hgrad1, agrad1, sums1 = call(
        functools.partial(turn_kernel, order, share), grid,
        [smem, whole_spec(packed), rows_w, rows_w, rows_1, whole_spec(norms), rows_w]
        + [whole_spec(wo)],
        [rows_w, rows_w, rows_f, rows_w, rows_f, rows_w, rows_w, rows_w, sums_spec],
        [thin, thin, tall, thin, tall, thin, wide, thin, sums_shape],
        unit * (2 * width + 4 * ff),
        [place, packed, att1, later, live_cols[1], norms, given, wo],
    )
    mgrad1 = attend_back(mixed1, agrad1, att1, logs1, live_cols[1])
    drop0, lift0, branch0, hgrad0, agrad0, sums0 = call(
        functools.partial(back_kernel, order, share), grid,
        [smem, whole_spec(packed), rows_3, rows_w, rows_w, whole_spec(norms), rows_1, rows_w, rows_f]
        + [whole_spec(a) for a in (wq, wo)],
        [rows_w, rows_f, rows_w, rows_w, rows_w, sums_spec],
        [thin, tall, thin, wide, thin, sums_shape],
        unit * (4 * width + 2 * ff),
        [place, packed, mgrad1, later, hgrad1, norms, live_cols[0], hidden0, slope0, wq, wo],
    )
    chips = cube.pairs * high
    fast = len(cube.turns) == 2 and (cube.count_line * high) % LANES == 0 and high % 32 == 0
    out_own, out_other = out_grads(cube, place, branch0, branch1, att0, att1)
    up_args = (lift0, lift1, second0, second1)
    down_args = (act0, act1, drop0, drop1)

    def split_rows(v):
        start = high // 2
        return [v[:, :start], cube.turned(v[:, start:])]

    def turn_halves(halves):
        middle = cube.pairs // 2
        return [v[:middle] for v in halves], [v[middle:] for v in halves]

    if fast:
        up_other = other_grads(cube, high, *up_args, extra=[out_other])
        (up_got,) = across(cube, up_other)
        down_other = other_grads(cube, high, *down_args, hold=[up_other])
        (down_got,) = across(cube, down_other)
        made = own_grads(cube, high, *up_args, up_got, extra=[out_own], hold=[down_other])
        up_out = Scatter(cube, made[0::2], made[1::2], False)
        made = own_grads(cube, high, *down_args, down_got, hold=made)
        down = Scatter(cube, made[0::2], made[1::2], False)
    else:
        found = []
        for args, more, more_other in ((up_args, out_own, out_other), (down_args, None, None)):
            own = pair_grads(*args, 0, chips)
            if cube.inner:
                got = across(cube, pair_grads(*args, chips, chips))[0]
                own = (own.astype(f32) + got.astype(f32)).astype(bf16)
                if more is not None:
                    got = across(cube, more_other)[0]
                    more = (more.astype(f32) + got.astype(f32)).astype(bf16)
            halves = split_rows(own.reshape(cube.pairs, high, width))
            if more is not None:
                halves[0] = jnp.concatenate([halves[0], more], axis=1)
            keep, send = turn_halves(halves) if cube.turns else (halves, [])
            found.append(Scatter(cube, keep, send, False))
        up_out, down = found
        made = send
    hold = made
    groups = []
    for first in range(0, pairs, third):
        group = attend_back(
            mixed0, agrad0, att0, logs0, live_cols[0], first, third, hold, room=LATE_LIMIT
        )
        groups.append(group)
        hold = [group]
        if first == 0:
            hold = hold + up_out.step(group)
        elif first == third:
            hold = hold + down.step(group) + up_out.step(group)
        else:
            hold = hold + down.step(group) + up_out.step(group)
    own, other, small = qkv_grads(
        cube, passes, place, pass_index, groups, mgrad1, xhat0, xhat1,
        [wq, sums0, sums1], hold,
    )
    got = across(cube, other)
    if got and cube.turns and own.shape[1] % 16 == 0:
        shapes = [sds((cube.pairs // 2, own.shape[1], width // 2), bf16)] * 4
        made = call(
            core_sum_kernel, (1,), [whole_spec(own)] * 2, [whole_spec(v) for v in shapes],
            shapes, 0, [own, got[0]], room=24,
        )
        keep, send = made[0::2], made[1::2]
    else:
        if got:
            own = (own.astype(f32) + got[0].astype(f32)).astype(bf16)
        halves = split_lanes(own)
        keep, send = turn_halves(halves) if cube.turns else (halves, [])
    qkv = Scatter(cube, keep, send, True)
    hold = send
    specs_g = [
        pl.BlockSpec((3, block, a.shape[2]), lambda i: (0, i, 0)) for a in groups
    ]
    input_grad = call(
        functools.partial(last_kernel, len(groups)), grid,
        specs_g + [rows_w, rows_w, whole_spec(norms), whole_spec(wq)],
        [rows_w], [wide], unit * 3 * width,
        [*groups, x, hgrad0, norms, wq],
        hold=hold,
        room=LATE_LIMIT,
    )[0]
    qkv.step(input_grad)
    down = down.result()
    up_out = up_out.result()
    qkv = qkv.result()
    share = w_out.shape[1]
    count = w_qkv.shape[1]
    if cube.count > 1:
        half = width // 2
        ends = qkv[count : count + 8]
        small = jnp.concatenate([ends[:, :share], ends[:, half : half + share]], axis=0)
    counts = qkv[count, LANES : LANES + count]
    if cube.count == 1:
        counts = jnp.sum(
            sum(jnp.concatenate(v, axis=2) for v in (groups, [mgrad1])).astype(f32), axis=1
        ).reshape(-1)
    qkv = (qkv[:count] * norms[0:1] + counts[:, None] * norms[2:3]).T
    low_end = high // 2
    out_end = low_end + share
    up = jnp.concatenate([up_out[:low_end], up_out[out_end:]], axis=0).T
    out = up_out[low_end:out_end].T
    return (
        result[None], input_grad[None], qkv, out, up, down,
        small[:2], small[2], small[3], small[4 : 4 + passes],
    )


def solution(mesh):
    placed = (
        P(AXES, None, None),
        P(AXES),
        P(None, AXES, None),
        P(AXES),
        P(None, AXES),
        P(None, AXES),
        P(None, AXES),
        P(AXES, None),
        P(None, AXES),
        P(None, AXES),
        P(None, AXES),
        P(AXES, None, None),
    )
    return jax.shard_map(
        body,
        mesh=mesh,
        in_specs=placed,
        out_specs=(
            P(AXES, None, None),
            P(AXES, None, None),
            P(None, AXES),
            P(None, AXES),
            P(None, AXES),
            P(AXES, None),
            P(None, AXES),
            P(AXES),
            P(AXES),
            P(None, AXES),
        ),
        check_vma=False,
    )
```
